128 devices in a mesh: member: 8 (over y_lo, z), tok: 8 (over x, core), col: 2 (over y_hi).
Axes of the slice: x: 4, y: 4 (y_hi: 2, y_lo: 2; y = y_hi * 2 + y_lo), z: 4, core: 2. Of those that a mesh axis runs over, the one named last changes fastest.
Arguments:
- inputs: bfloat16 [16, 6144, 8192], P('member', 'tok', 'col'), may hold values from -40 to 40
- grads: bfloat16 [16, 6144, 512], P('member', 'tok', 'col'), may hold values from -40 to 40
- weights: bfloat16 [16, 8192, 512], P('member', 'tok', 'col'), may hold values from -6 to 6
Outputs:
- merged: float32 [8192, 512], P(('tok', 'member'), 'col')
The draws below stay inside these ranges and needn't reach their ends.
All inputs are finite; a program needn't handle non-finite values.
Results may differ from the reference program's by a relative error of at most 0.0065.
Values may be sent and summed in bfloat16 or wider, within the bound.
No kernel may reach another device: no remote copies, remote signals or barrier semaphores. Data moves between devices by JAX's collectives and lax.ppermute only.
A program may use at most 192 MiB of HBM per device.

```python
import math
import jax
import jax.numpy as jnp
from jax import lax

DIN = 8192
ROWS = 512
MEMBERS = 16
TOKENS = 6144


def scaled_field(key, members, count, width):
    first, second, third = jax.random.split(key, 3)
    shape = (members, count, width)
    base = jnp.clip(jax.random.normal(first, shape, jnp.float32), -4.0, 4.0)
    feature = jnp.exp(jax.random.uniform(second, (members, 1, width), jnp.float32, math.log(0.5), math.log(5.0)))
    token = jnp.exp(jax.random.uniform(third, (members, count, 1), jnp.float32, math.log(0.5), math.log(2.0)))
    return base * feature * token


def draw_inputs(key, part):
    key = jax.random.fold_in(key, 11)
    return scaled_field(key, MEMBERS, TOKENS, DIN).astype(jnp.bfloat16)


def draw_grads(key, part):
    key = jax.random.fold_in(key, 23)
    return scaled_field(key, MEMBERS, TOKENS, ROWS).astype(jnp.bfloat16)


def block_scale(stream_key, extent, cuts, smallest, high):
    def one(axis_at, parts):
        draws = jax.random.uniform(jax.random.fold_in(jax.random.fold_in(stream_key, 6), axis_at), (parts,), jnp.float32, smallest / len(cuts), high / len(cuts))
        return jnp.repeat(jnp.exp(draws), extent[axis_at] // parts).reshape((-1,) + (1,) * (len(extent) - axis_at - 1))

    factor_of = one(*cuts[0])
    for cut in cuts[1:]:
        factor_of = factor_of * one(*cut)
    return factor_of


def bell_draw(own_key, extent, deviation, reach, shards=(), kind=jnp.bfloat16):
    result = deviation * jax.random.normal(own_key, extent, jnp.float32)
    if shards:
        result = result * block_scale(own_key, extent, shards, -0.22, 0.18)
    return jnp.clip(result, -reach, reach).astype(kind)


def setup_inputs(seed: int = 0) -> dict:
    keys = jax.random.split(jax.random.key(seed), 4)
    inputs = draw_inputs(jax.random.fold_in(keys[3], 71), 0)
    grads = draw_grads(jax.random.fold_in(keys[3], 71), 0)
    weights = bell_draw(keys[2], (MEMBERS, DIN, ROWS), 1.0, 6.0, ((0, 8), (1, 8), (2, 2)))
    return {"inputs": inputs, "grads": grads, "weights": weights}


def reference(inputs, grads, weights):
    def one_member(index, carry):
        weighted, total = carry
        member_in = lax.dynamic_index_in_dim(inputs, index, 0, keepdims=False)
        member_grad = lax.dynamic_index_in_dim(grads, index, 0, keepdims=False)
        member_weight = lax.dynamic_index_in_dim(weights, index, 0, keepdims=False)
        input_sq = (member_in.astype(jnp.float32) ** 2).astype(jnp.bfloat16)
        grad_sq = (member_grad.astype(jnp.float32) ** 2).astype(jnp.bfloat16)
        fisher = jnp.dot(input_sq.T, grad_sq, preferred_element_type=jnp.float32)
        return (weighted + fisher * member_weight.astype(jnp.float32), total + fisher)

    start = jnp.zeros((DIN, ROWS), jnp.float32)
    weighted, total = lax.fori_loop(0, MEMBERS, one_member, (start, start))
    return weighted / total
```

```python
import jax
import jax.numpy as jnp
from jax import lax
from jax.experimental import pallas as pl
from jax.experimental.pallas import tpu as pltpu
from jax.sharding import PartitionSpec as P

F32 = jnp.float32
BF16 = jnp.bfloat16

GRID = 1.00297
BIG = 2.0**28
SMALL = 2.0**16
EDGE = 2.0**-40
EDGE_CODE = 2.0**-24

X, CORES, Z = 4, 2, 4


def encode(values):
    scaled = values * BIG
    code = jnp.where(values >= EDGE, scaled * scaled, values * SMALL)
    first = code.astype(BF16).astype(F32)
    second = (code * (1.0 / GRID)).astype(BF16).astype(F32)
    near = jnp.abs(first - code) <= jnp.abs(second * GRID - code)
    return jnp.where(near, first, -second).astype(BF16)


def decode(sent):
    code = sent.astype(F32)
    code = jnp.where(code < 0.0, code * (-GRID), code)
    return jnp.where(code >= EDGE_CODE, jnp.sqrt(code) * (1.0 / BIG), code * (1.0 / SMALL))


def fisher_block(step, x_ref, g_ref, gt_ref):
    @pl.when(step == 0)
    def _():
        g = g_ref[0].astype(F32)
        gt_ref[...] = (g * g).T.astype(BF16)

    x = x_ref[0]
    return jnp.dot(gt_ref[...], x * x, preferred_element_type=F32)


def send_kernel(place, x_ref, g_ref, out_ref, gt_ref):
    out_ref[0] = encode(fisher_block(pl.program_id(0), x_ref, g_ref, gt_ref))


def own_kernel(place, x_ref, g_ref, got_ref, own_ref, one_ref, two_ref, three_ref, gt_ref):
    step = pl.program_id(0)
    block = fisher_block(step, x_ref, g_ref, gt_ref) + decode(got_ref[0])

    @pl.when(step == 3)
    def _():
        own_ref[...] = block

    for at, ref in enumerate((two_ref, one_ref, three_ref)):

        @pl.when(step == at)
        def _(ref=ref):
            ref[...] = encode(block)


def fisher_specs(inputs, grads, member, base, order):
    tokens, width = inputs.shape[1:]
    outs = grads.shape[2]
    wide = width // 8
    x_spec = pl.BlockSpec((1, tokens, wide), lambda s, place: (member, 0, place[base + s]))
    g_spec = pl.BlockSpec((1, tokens, outs), lambda s, place: (member, 0, 0))
    return x_spec, g_spec, tokens, outs, wide


def send_part(place, inputs, grads, member):
    x_spec, g_spec, tokens, outs, wide = fisher_specs(inputs, grads, member, 0, None)
    return pl.pallas_call(
        send_kernel,
        out_shape=jax.ShapeDtypeStruct((4, outs, wide), BF16),
        grid_spec=pltpu.PrefetchScalarGridSpec(
            num_scalar_prefetch=1,
            grid=(4,),
            in_specs=[x_spec, g_spec],
            out_specs=pl.BlockSpec((1, outs, wide), lambda s, place: (s, 0, 0)),
            scratch_shapes=[pltpu.VMEM((outs, tokens), BF16)],
        ),
        compiler_params=pltpu.CompilerParams(vmem_limit_bytes=24 << 20),
        cost_estimate=pl.CostEstimate(
            flops=8 * outs * wide * tokens, bytes_accessed=8 * tokens * wide + 8 * outs * wide, transcendentals=0
        ),
        name="fisher_for_other_core",
    )(place, inputs, grads)


def own_part(place, inputs, grads, got, member):
    x_spec, g_spec, tokens, outs, wide = fisher_specs(inputs, grads, member, 4, None)
    whole = pl.BlockSpec((outs, wide), lambda s, place: (0, 0))
    sent = jax.ShapeDtypeStruct((outs, wide), BF16)
    return pl.pallas_call(
        own_kernel,
        out_shape=[jax.ShapeDtypeStruct((outs, wide), F32), sent, sent, sent],
        grid_spec=pltpu.PrefetchScalarGridSpec(
            num_scalar_prefetch=1,
            grid=(4,),
            in_specs=[x_spec, g_spec, pl.BlockSpec((1, outs, wide), lambda s, place: (s, 0, 0))],
            out_specs=[whole] * 4,
            scratch_shapes=[pltpu.VMEM((outs, tokens), BF16)],
        ),
        compiler_params=pltpu.CompilerParams(vmem_limit_bytes=24 << 20),
        cost_estimate=pl.CostEstimate(
            flops=8 * outs * wide * tokens, bytes_accessed=8 * tokens * wide + 16 * outs * wide, transcendentals=0
        ),
        name="fisher_of_own_core",
    )(place, inputs, grads, got)


def gather_kernel(own_ref, one_ref, two_ref, three_ref, out_ref):
    outs, wide = own_ref.shape
    half, part = outs // 2, wide // Z
    for z in range(Z):
        cols = slice(z * part, (z + 1) * part)
        total = own_ref[:, cols] + decode(one_ref[:, cols]) + decode(two_ref[:, cols]) + decode(three_ref[:, cols])
        total = encode(total.T)
        for y in range(2):
            out_ref[y * Z + z] = total[:, y * half : (y + 1) * half]


def gather_parts(own, one, two, three):
    outs, wide = own.shape
    return pl.pallas_call(
        gather_kernel,
        out_shape=jax.ShapeDtypeStruct((2 * Z, wide // Z, outs // 2), BF16),
        compiler_params=pltpu.CompilerParams(vmem_limit_bytes=24 << 20),
        cost_estimate=pl.CostEstimate(flops=20 * outs * wide, bytes_accessed=12 * outs * wide, transcendentals=0),
        name="fisher_over_tokens",
    )(own, one, two, three)


def merge_kernel(which, a_ref, b_ref, w_ref, out_ref):
    weighted = jnp.zeros(out_ref.shape, F32)
    total = jnp.zeros(out_ref.shape, F32)
    for group in range(a_ref.shape[0]):
        for member, ref in enumerate((a_ref, b_ref)):
            fisher = decode(ref[group])
            weighted += fisher * w_ref[group, 0, member].astype(F32)
            total += fisher
    out_ref[...] = weighted / total


def merge(which, first, second, weights):
    groups, rows, cols = first.shape
    whole = pl.BlockSpec((groups, rows, cols), lambda s, which: (0, 0, 0))
    return pl.pallas_call(
        merge_kernel,
        out_shape=jax.ShapeDtypeStruct((rows, cols), F32),
        grid_spec=pltpu.PrefetchScalarGridSpec(
            num_scalar_prefetch=1,
            grid=(1,),
            in_specs=[
                whole,
                whole,
                pl.BlockSpec((groups, 1, 2, rows, cols), lambda s, which: (0, which[0], 0, 0, 0)),
            ],
            out_specs=pl.BlockSpec((rows, cols), lambda s, which: (0, 0)),
        ),
        compiler_params=pltpu.CompilerParams(vmem_limit_bytes=24 << 20),
        cost_estimate=pl.CostEstimate(
            flops=20 * groups * rows * cols, bytes_accessed=8 * groups * rows * cols, transcendentals=0
        ),
        name="merge_members",
    )(which, first, second, weights)


def keeper(local, half):
    home = 2 * half + local // 2
    return home if local % 2 == 0 else 3 - home


def kept(x, half):
    return 2 * (x % 2) if x // 2 == half else 2 * ((3 - x) % 2) + 1


def weight_pairs(flip):
    pairs = []
    for tok in range(X * CORES):
        half, local = divmod(tok, 4)
        for col in range(2):
            to = keeper(local, half) * 2 + (col ^ flip)
            pairs.append((tok * 2 + col, to * 2 + half))
    return pairs


def result_pairs(flip):
    pairs = []
    for member in range(8):
        y_lo, z = divmod(member, 4)
        for tok in range(8):
            x, core = divmod(tok, 2)
            for half in range(2):
                to_member = core * 4 + z
                to_tok = 4 * half + kept(x, half)
                to_col = y_lo ^ flip
                pairs.append(((member * 8 + tok) * 2 + half, (to_member * 8 + to_tok) * 2 + to_col))
    return pairs


def x_pairs(distance):
    return [(t, ((t // 2 + distance) % X) * 2 + t % 2) for t in range(X * CORES)]


def shards(inputs, grads, weights):
    tok = lax.axis_index("tok")
    half = lax.axis_index("col")
    x, core = tok // 2, tok % 2
    y_lo = lax.axis_index("member") // 4

    steps = (x + jnp.array([2, 1, 3, 0], jnp.int32)) % X
    local = jnp.where(steps // 2 == half, 2 * (steps % 2), 2 * ((3 - steps) % 2) + 1)
    place = jnp.concatenate([2 * local + 1 - core, 2 * local + core]).astype(jnp.int32)

    other_grads = lax.ppermute(grads, "col", [(0, 1), (1, 0)])

    rows = weights.shape[1] // 2
    cut = weights.reshape(2, 2, rows, weights.shape[2])
    by_row = [lax.dynamic_index_in_dim(cut, half ^ flip, 1, keepdims=False) for flip in (0, 1)]
    moved = [lax.ppermute(by_row[flip], ("tok", "col"), weight_pairs(flip)) for flip in (0, 1)]
    moved = jnp.stack(moved).reshape(2, 2, Z, rows // Z, 2, weights.shape[2] // 2)
    moved = jnp.transpose(moved, (4, 2, 0, 1, 3, 5)).reshape(8, 2, 2, rows // Z, weights.shape[2] // 2)
    spread = lax.all_to_all(moved, "member", 0, 0, tiled=True)

    merged = []
    for phase, g in enumerate((grads, other_grads)):
        arrived = []
        for member in range(2):
            sent = send_part(place, inputs, g, member)
            got = lax.ppermute(sent, "tok", [(t, t ^ 1) for t in range(8)])
            own, one, two, three = own_part(place, inputs, g, got, member)
            two = lax.ppermute(two, "tok", x_pairs(2))
            one = lax.ppermute(one, "tok", x_pairs(1))
            three = lax.ppermute(three, "tok", x_pairs(3))
            pieces = gather_parts(own, one, two, three)
            arrived.append(lax.all_to_all(pieces, "member", 0, 0, tiled=True))
        which = ((core ^ half) ^ phase).astype(jnp.int32).reshape(1)
        merged.append(merge(which, arrived[0], arrived[1], spread))

    swap = (y_lo ^ half) == 1
    near = jnp.where(swap, merged[1], merged[0])
    far = jnp.where(swap, merged[0], merged[1])
    names = ("member", "tok", "col")
    near = lax.ppermute(near, names, result_pairs(0))
    far = lax.ppermute(far, names, result_pairs(1))
    left = jnp.where(half == 0, near, far)
    right = jnp.where(half == 0, far, near)
    return jnp.concatenate([left, right], axis=1)


def solution(mesh):
    in_specs = (P("member", "tok", "col"), P("member", "tok", "col"), P("member", "tok", "col"))
    out_specs = P(("tok", "member"), "col")
    return jax.shard_map(shards, mesh=mesh, in_specs=in_specs, out_specs=out_specs, check_vma=False)
```

```python
import jax
import jax.numpy as jnp
from jax import lax
from jax.experimental import pallas as pl
from jax.experimental.pallas import tpu as pltpu
from jax.sharding import PartitionSpec as P

F32 = jnp.float32
BF16 = jnp.bfloat16
ANY = pl.BlockSpec(memory_space=pltpu.HBM)
SMEM = pl.BlockSpec(memory_space=pltpu.SMEM)
VMEM_LIMIT = 56 << 20

GRID = 1.00297
BIG = 2.0**28
SMALL = 2.0**16
EDGE = 2.0**-40
EDGE_CODE = 2.0**-24

X, CORES, Z = 4, 2, 4


def code_of(values):
    scaled = values * BIG
    return jnp.where(values >= EDGE, scaled * scaled, values * SMALL)


def value_of(code):
    return jnp.where(code >= EDGE_CODE, jnp.sqrt(code) * (1.0 / BIG), code * (1.0 / SMALL))


def encode(values):
    return code_of(values).astype(BF16)


def decode(sent):
    return value_of(sent.astype(F32))


def encode_fine(values):
    code = code_of(values)
    first = code.astype(BF16).astype(F32)
    second = (code * (1.0 / GRID)).astype(BF16).astype(F32)
    near = jnp.abs(first - code) <= jnp.abs(second * GRID - code)
    return jnp.where(near, first, -second).astype(BF16)


def decode_fine(sent):
    code = sent.astype(F32)
    return value_of(jnp.where(code < 0.0, code * (-GRID), code))


def load_all(place, base, member, x_ref, g_ref, x_buf, g_buf, x_sem, g_sem):
    wide = x_buf.shape[2]
    g_copy = pltpu.make_async_copy(g_ref, g_buf, g_sem)
    g_copy.start()
    copies = []
    for s in range(4):
        at = pl.multiple_of(place[base + s] * wide, wide)
        copies.append(pltpu.make_async_copy(x_ref.at[member, :, pl.ds(at, wide)], x_buf.at[s], x_sem.at[s]))
        copies[s].start()
    return g_copy, copies


def squared_grads(g_copy, g_buf, gt_buf):
    g_copy.wait()
    g = g_buf[...].astype(F32)
    gt_buf[...] = (g * g).T.astype(BF16)


def send_kernel(member, place, x_ref, g_ref, after, out_ref, x_buf, g_buf, gt_buf, out_buf, x_sem, g_sem, out_sem):
    g_copy, copies = load_all(place, 0, member, x_ref, g_ref, x_buf, g_buf, x_sem, g_sem)
    squared_grads(g_copy, g_buf, gt_buf)
    outs = []
    for s in range(4):
        copies[s].wait()
        x = x_buf[s]
        out_buf[s] = jnp.dot(gt_buf[...], x * x, preferred_element_type=F32).astype(BF16)
        outs.append(pltpu.make_async_copy(out_buf.at[s], out_ref.at[s], out_sem.at[s]))
        outs[s].start()
    for copy in outs:
        copy.wait()


def own_kernel(
    member, place, x_ref, g_ref, got_ref, after, two_ref, one_ref, three_ref, own_ref,
    x_buf, g_buf, gt_buf, got_buf, out_buf, own_buf, x_sem, g_sem, got_sem, out_sem,
):
    g_copy, copies = load_all(place, 4, member, x_ref, g_ref, x_buf, g_buf, x_sem, g_sem)
    gots = []
    for s in range(4):
        gots.append(pltpu.make_async_copy(got_ref.at[s], got_buf.at[s], got_sem.at[s]))
        gots[s].start()
    squared_grads(g_copy, g_buf, gt_buf)
    outs = []
    for s, ref in enumerate((two_ref, one_ref, three_ref, own_ref)):
        copies[s].wait()
        gots[s].wait()
        x = x_buf[s]
        block = jnp.dot(gt_buf[...], x * x, preferred_element_type=F32) + got_buf[s].astype(F32)
        if s < 3:
            out_buf[s] = encode(block)
            outs.append(pltpu.make_async_copy(out_buf.at[s], ref, out_sem.at[s]))
        else:
            own_buf[...] = block
            outs.append(pltpu.make_async_copy(own_buf, ref, out_sem.at[s]))
        outs[s].start()
    for copy in outs:
        copy.wait()


def kernel_sizes(inputs, grads):
    tokens, width = inputs.shape[1:]
    return tokens, grads.shape[1], width // 8


def fisher_cost(tokens, outs, wide):
    return pl.CostEstimate(
        flops=8 * outs * wide * tokens, bytes_accessed=8 * tokens * wide + 16 * outs * wide, transcendentals=0
    )


def send_part(place, inputs, grads, member, after):
    tokens, outs, wide = kernel_sizes(inputs, grads)
    return pl.pallas_call(
        lambda *refs: send_kernel(member, *refs),
        out_shape=jax.ShapeDtypeStruct((4, outs, wide), BF16),
        in_specs=[SMEM, ANY, ANY, ANY],
        out_specs=ANY,
        scratch_shapes=[
            pltpu.VMEM((4, tokens, wide), BF16),
            pltpu.VMEM((tokens, outs), BF16),
            pltpu.VMEM((outs, tokens), BF16),
            pltpu.VMEM((4, outs, wide), BF16),
            pltpu.SemaphoreType.DMA((4,)),
            pltpu.SemaphoreType.DMA,
            pltpu.SemaphoreType.DMA((4,)),
        ],
        compiler_params=pltpu.CompilerParams(vmem_limit_bytes=VMEM_LIMIT),
        cost_estimate=fisher_cost(tokens, outs, wide),
        name="fisher_for_other_core",
    )(place, inputs, grads, after)


def own_part(place, inputs, grads, got, member, after):
    tokens, outs, wide = kernel_sizes(inputs, grads)
    sent = jax.ShapeDtypeStruct((outs, wide), BF16)
    return pl.pallas_call(
        lambda *refs: own_kernel(member, *refs),
        out_shape=[sent, sent, sent, jax.ShapeDtypeStruct((outs, wide), F32)],
        in_specs=[SMEM, ANY, ANY, ANY, ANY],
        out_specs=[ANY] * 4,
        scratch_shapes=[
            pltpu.VMEM((4, tokens, wide), BF16),
            pltpu.VMEM((tokens, outs), BF16),
            pltpu.VMEM((outs, tokens), BF16),
            pltpu.VMEM((4, outs, wide), BF16),
            pltpu.VMEM((3, outs, wide), BF16),
            pltpu.VMEM((outs, wide), F32),
            pltpu.SemaphoreType.DMA((4,)),
            pltpu.SemaphoreType.DMA,
            pltpu.SemaphoreType.DMA((4,)),
            pltpu.SemaphoreType.DMA((4,)),
        ],
        compiler_params=pltpu.CompilerParams(vmem_limit_bytes=VMEM_LIMIT),
        cost_estimate=fisher_cost(tokens, outs, wide),
        name="fisher_of_own_core",
    )(place, inputs, grads, got, after)


def pick_kernel(half, w_ref, after, a_ref, b_ref, sem):
    rows = a_ref.shape[1]
    copies = []
    for flip, ref in enumerate((a_ref, b_ref)):
        at = pl.multiple_of((half[0] ^ flip) * rows, rows)
        copies.append(pltpu.make_async_copy(w_ref.at[:, pl.ds(at, rows), :], ref, sem.at[flip]))
        copies[flip].start()
    for copy in copies:
        copy.wait()


def pick_weights(half, weights, after):
    members, rows, outs = weights.shape
    part = jax.ShapeDtypeStruct((members, rows // 2, outs), BF16)
    return pl.pallas_call(
        pick_kernel,
        out_shape=[part, part],
        in_specs=[SMEM, ANY, ANY],
        out_specs=[ANY, ANY],
        scratch_shapes=[pltpu.SemaphoreType.DMA((2,))],
        compiler_params=pltpu.CompilerParams(vmem_limit_bytes=VMEM_LIMIT),
        cost_estimate=pl.CostEstimate(flops=0, bytes_accessed=4 * members * rows * outs, transcendentals=0),
        name="pick_weights",
    )(half, weights, after)


def weigh_kernel(which, *refs):
    parts, (w_a, w_b, after, out_ref), (buf, own_buf, w_buf, out_buf, sem, w_sem, out_sem) = refs[:8], refs[8:12], refs[12:]
    copies = []
    for m in range(2):
        for j in range(3):
            copies.append(pltpu.make_async_copy(parts[4 * m + j], buf.at[m, j], sem.at[m, j]))
        copies.append(pltpu.make_async_copy(parts[4 * m + 3], own_buf.at[m], sem.at[m, 3]))
    for copy in copies:
        copy.start()

    @pl.when(which[0] == 0)
    def _():
        pltpu.make_async_copy(w_a, w_buf, w_sem).start()

    @pl.when(which[0] != 0)
    def _():
        pltpu.make_async_copy(w_b, w_buf, w_sem).start()

    for copy in copies:
        copy.wait()
    pltpu.make_async_copy(w_a, w_buf, w_sem).wait()
    outs, wide = own_buf.shape[1:]
    half, part = outs // 2, wide // Z
    done = []
    for z in range(Z):
        cols = slice(z * part, (z + 1) * part)
        weighted = total = None
        for m in range(2):
            fisher = own_buf[m, :, cols]
            for j in range(3):
                fisher += decode(buf[m, j, :, cols])
            fisher = fisher.T
            product = fisher * w_buf[m, cols, :].astype(F32)
            weighted = product if m == 0 else weighted + product
            total = fisher if m == 0 else total + fisher
        high = weighted.astype(BF16)
        low = (weighted - high.astype(F32)).astype(BF16)
        code = encode_fine(total)
        for y in range(2):
            outcols = slice(y * half, (y + 1) * half)
            for word, values in enumerate((high, low, code)):
                out_buf[y * Z + z, word] = values[:, outcols]
            done.append(pltpu.make_async_copy(out_buf.at[y * Z + z], out_ref.at[y * Z + z], out_sem.at[y * Z + z]))
            done[-1].start()
    for copy in done:
        copy.wait()


def weigh(which, parts, w_a, w_b, after):
    outs, wide = parts[3].shape
    members = w_a.shape[0]
    shape = (2 * Z, 3, wide // Z, outs // 2)
    return pl.pallas_call(
        weigh_kernel,
        out_shape=jax.ShapeDtypeStruct(shape, BF16),
        in_specs=[SMEM] + [ANY] * 11,
        out_specs=ANY,
        scratch_shapes=[
            pltpu.VMEM((members, 3, outs, wide), BF16),
            pltpu.VMEM((members, outs, wide), F32),
            pltpu.VMEM(w_a.shape, BF16),
            pltpu.VMEM(shape, BF16),
            pltpu.SemaphoreType.DMA((members, 4)),
            pltpu.SemaphoreType.DMA,
            pltpu.SemaphoreType.DMA((2 * Z,)),
        ],
        compiler_params=pltpu.CompilerParams(vmem_limit_bytes=VMEM_LIMIT),
        cost_estimate=pl.CostEstimate(flops=40 * outs * wide, bytes_accessed=30 * outs * wide, transcendentals=0),
        name="weigh_members",
    )(which, *parts, w_a, w_b, after)


def merge_kernel(got_ref, out_ref):
    weighted = total = 0.0
    for group in range(got_ref.shape[0]):
        weighted += got_ref[group, 0].astype(F32) + got_ref[group, 1].astype(F32)
        total += decode_fine(got_ref[group, 2])
    out_ref[...] = weighted / total


def merge(got):
    groups, words, rows, cols = got.shape
    return pl.pallas_call(
        merge_kernel,
        out_shape=jax.ShapeDtypeStruct((rows, cols), F32),
        compiler_params=pltpu.CompilerParams(vmem_limit_bytes=VMEM_LIMIT),
        cost_estimate=pl.CostEstimate(
            flops=20 * groups * rows * cols, bytes_accessed=6 * groups * rows * cols, transcendentals=0
        ),
        name="merge_members",
    )(got)


def keeper(local, half):
    home = 2 * half + local // 2
    return home if local % 2 == 0 else 3 - home


def kept(x, half):
    return 2 * (x % 2) if x // 2 == half else 2 * ((3 - x) % 2) + 1


def weight_pairs(flip):
    pairs = []
    for tok in range(X * CORES):
        half, local = divmod(tok, 4)
        for col in range(2):
            to = keeper(local, half) * 2 + (col ^ flip)
            pairs.append((tok * 2 + col, to * 2 + half))
    return pairs


def result_pairs(flip):
    pairs = []
    for member in range(8):
        y_lo, z = divmod(member, 4)
        for tok in range(8):
            x, core = divmod(tok, 2)
            for half in range(2):
                to_member = core * 4 + z
                to_tok = 4 * half + kept(x, half)
                to_col = y_lo ^ flip
                pairs.append(((member * 8 + tok) * 2 + half, (to_member * 8 + to_tok) * 2 + to_col))
    return pairs


def x_pairs(distance):
    return [(t, ((t // 2 + distance) % X) * 2 + t % 2) for t in range(X * CORES)]


def shards(inputs, grads, weights):
    tok = lax.axis_index("tok")
    half = lax.axis_index("col")
    x, core = tok // 2, tok % 2
    y_lo = lax.axis_index("member") // 4

    steps = (x + jnp.array([2, 1, 3, 0], jnp.int32)) % X
    local = jnp.where(steps // 2 == half, 2 * (steps % 2), 2 * ((3 - steps) % 2) + 1)
    place = jnp.concatenate([2 * local + 1 - core, 2 * local + core]).astype(jnp.int32)

    own_grads = [grads[0], grads[1]]
    other_grads = [lax.ppermute(g, "col", [(0, 1), (1, 0)]) for g in own_grads]

    after = place
    words = []
    moved = None
    for phase, gs in enumerate((own_grads, other_grads)):
        got = []
        for member in range(2):
            after = send_part(place, inputs, gs[member], member, after)
            got.append(lax.ppermute(after, "tok", [(t, t ^ 1) for t in range(8)]))
        parts = []
        for member in range(2):
            two, one, three, own = own_part(place, inputs, gs[member], got[member], member, after)
            after = own
            two = lax.ppermute(two, "tok", x_pairs(2))
            one = lax.ppermute(one, "tok", x_pairs(1))
            three = lax.ppermute(three, "tok", x_pairs(3))
            parts += [two, one, three, own]
            if moved is None:
                picked = pick_weights(half.reshape(1), weights, after)
                moved = [lax.ppermute(w, ("tok", "col"), weight_pairs(flip)) for flip, w in enumerate(picked)]
        words.append(parts)

    merged = []
    for phase in range(2):
        which = ((core ^ half) ^ phase).astype(jnp.int32).reshape(1)
        after = weigh(which, words[phase], moved[0], moved[1], after)
        merged.append(merge(lax.all_to_all(after, "member", 0, 0, tiled=True)))

    swap = (y_lo ^ half) == 1
    near = jnp.where(swap, merged[1], merged[0])
    far = jnp.where(swap, merged[0], merged[1])
    names = ("member", "tok", "col")
    near = lax.ppermute(near, names, result_pairs(0))
    far = lax.ppermute(far, names, result_pairs(1))
    left = jnp.where(half == 0, near, far)
    right = jnp.where(half == 0, far, near)
    return jnp.concatenate([left, right], axis=1)


def solution(mesh):
    in_specs = (P("member", "tok", "col"), P("member", "tok", "col"), P("member", "tok", "col"))
    out_specs = P(("tok", "member"), "col")
    return jax.shard_map(shards, mesh=mesh, in_specs=in_specs, out_specs=out_specs, check_vma=False)
```

```python
import jax
import jax.numpy as jnp
from jax import lax
from jax.experimental import pallas as pl
from jax.experimental.pallas import tpu as pltpu
from jax.sharding import PartitionSpec as P

F32 = jnp.float32
BF16 = jnp.bfloat16
HBM = pl.BlockSpec(memory_space=pltpu.HBM)
SMEM = pl.BlockSpec(memory_space=pltpu.SMEM)
VMEM = pl.BlockSpec(memory_space=pltpu.VMEM)
VMEM_LIMIT = 16 << 20

GRID = 1.00297
BIG = 2.0**28
SMALL = 2.0**16
EDGE = 2.0**-40
EDGE_CODE = 2.0**-24

X, CORES, Z = 4, 2, 4


def code_of(values):
    scaled = values * BIG
    return jnp.where(values >= EDGE, scaled * scaled, values * SMALL)


def value_of(code):
    return jnp.where(code >= EDGE_CODE, jnp.sqrt(code) * (1.0 / BIG), code * (1.0 / SMALL))


def encode(values):
    return code_of(values).astype(BF16)


def decode(sent):
    return value_of(sent.astype(F32))


def encode_fine(values):
    code = code_of(values)
    first = code.astype(BF16).astype(F32)
    second = (code * (1.0 / GRID)).astype(BF16).astype(F32)
    near = jnp.abs(first - code) <= jnp.abs(second * GRID - code)
    return jnp.where(near, first, -second).astype(BF16)


def decode_fine(sent):
    code = sent.astype(F32)
    return value_of(jnp.where(code < 0.0, code * (-GRID), code))


def in_vmem(array):
    return pltpu.with_memory_space_constraint(array, pltpu.VMEM)


def in_hbm(array):
    return pltpu.with_memory_space_constraint(array, pltpu.HBM)


def call(kernel, name, outs, scalars, hbm, vmem, scratch=(), flops=0):
    single = not isinstance(outs, list)
    shapes = [pltpu.VMEM(shape, kind) for shape, kind in ([outs] if single else outs)]
    moved = sum(a.size * 2 for a in vmem) + sum(a.size * 2 for a in hbm)
    result = pl.pallas_call(
        kernel,
        out_shape=shapes,
        in_specs=[SMEM] * len(scalars) + [HBM] * len(hbm) + [VMEM] * len(vmem),
        out_specs=[VMEM] * len(shapes),
        scratch_shapes=list(scratch),
        compiler_params=pltpu.CompilerParams(vmem_limit_bytes=VMEM_LIMIT),
        cost_estimate=pl.CostEstimate(flops=flops, bytes_accessed=moved, transcendentals=0),
        name=name,
    )(*scalars, *[in_hbm(a) for a in hbm], *[in_vmem(a) for a in vmem])
    return result[0] if single else result


def squared_transposed(g):
    g = g.astype(F32)
    return (g * g).T.astype(BF16)


def fisher_block(x, gt_ref):
    return jnp.dot(gt_ref[...], x * x, preferred_element_type=F32)


def load_inputs(member, place, x_ref, x_out, sem):
    wide = x_out.shape[2]
    copies = []
    for s in range(8):
        at = pl.multiple_of(place[s] * wide, wide)
        copies.append(pltpu.make_async_copy(x_ref.at[member, :, pl.ds(at, wide)], x_out.at[s], sem.at[s]))
        copies[s].start()
    return copies


def send_blocks(copies, x_out, gt_out, send_out):
    for s in range(8):
        copies[s].wait()
        if s < 4:
            send_out[s] = fisher_block(x_out[s], gt_out).astype(BF16)


def load_kernel(member, place, x_ref, g_ref, *refs):
    send_out, x_out, gt_out, g_buf, sem, g_sem = refs[-6:]
    load = pltpu.make_async_copy(g_ref.at[member], g_buf, g_sem)
    load.start()
    copies = load_inputs(member, place, x_ref, x_out, sem)
    load.wait()
    gt_out[...] = squared_transposed(g_buf[...])
    send_blocks(copies, x_out, gt_out, send_out)


def send_kernel(member, x_ref, g_ref, after, send_out, gt_out):
    gt_out[...] = squared_transposed(g_ref[member])
    for s in range(4):
        send_out[s] = fisher_block(x_ref[s], gt_out).astype(BF16)


def own_kernel(x_ref, gt_ref, got_ref, after, sent_out, kept_out):
    for s in range(4):
        block = fisher_block(x_ref[4 + s], gt_ref) + got_ref[s].astype(F32)
        if s < 2:
            sent_out[s] = encode(block)
        else:
            kept_out[s - 2] = block


def middle_kernel(kept_ref, got_ref, after, sent_out, own_out):
    sent_out[...] = encode_fine(kept_ref[1] + decode(got_ref[1]))
    own_out[...] = kept_ref[0] + decode(got_ref[0])


def split_kernel(core, w_ref, after, own_out, send_out):
    rows = own_out.shape[1]
    own_out[...] = w_ref[:, pl.ds(pl.multiple_of(core[0] * rows, rows), rows), :]
    send_out[...] = w_ref[:, pl.ds(pl.multiple_of((1 - core[0]) * rows, rows), rows), :]


def over_tokens(own, got, cols):
    return (own[:, cols] + decode_fine(got[:, cols])).T


def begin_kernel(which, own, got, w_a, w_b, after, weighted_out, total_out):
    part = own.shape[1] // Z
    for z in range(Z):
        cols = slice(z * part, (z + 1) * part)
        fisher = over_tokens(own, got, cols)
        weight = jnp.where(which[0] == 0, w_a[0, cols, :].astype(F32), w_b[0, cols, :].astype(F32))
        weighted_out[cols, :] = fisher * weight
        total_out[cols, :] = fisher


def finish_kernel(which, own, got, w_a, w_b, weighted_ref, total_ref, out):
    outs, wide = own.shape
    half, part = outs // 2, wide // Z
    for z in range(Z):
        cols = slice(z * part, (z + 1) * part)
        fisher = over_tokens(own, got, cols)
        weight = jnp.where(which[0] == 0, w_a[1, cols, :].astype(F32), w_b[1, cols, :].astype(F32))
        weighted = weighted_ref[cols, :] + fisher * weight
        high = weighted.astype(BF16)
        low = (weighted - high.astype(F32)).astype(BF16)
        code = encode_fine(total_ref[cols, :] + fisher)
        for y in range(2):
            for word, values in enumerate((high, low, code)):
                out[y * Z + z, word] = values[:, y * half : (y + 1) * half]


def merged_of(got_ref):
    weighted = total = 0.0
    for group in range(got_ref.shape[0]):
        weighted += got_ref[group, 0].astype(F32) + got_ref[group, 1].astype(F32)
        total += decode_fine(got_ref[group, 2])
    return weighted / total


def merge_kernel(got_ref, out):
    out[...] = merged_of(got_ref)


def merge_last_kernel(swap, got_ref, first_ref, near_out, far_out):
    first, second = first_ref[...], merged_of(got_ref)
    near_out[...] = jnp.where(swap[0] == 1, second, first)
    far_out[...] = jnp.where(swap[0] == 1, first, second)


def keeper(local, half):
    home = 2 * half + local // 2
    return home if local % 2 == 0 else 3 - home


def kept(x, half):
    return 2 * (x % 2) if x // 2 == half else 2 * ((3 - x) % 2) + 1


def weight_pairs():
    pairs = []
    for tok in range(X * CORES):
        half, local = divmod(tok, 4)
        for col in range(2):
            pairs.append((tok * 2 + col, (keeper(local, half) * 2 + col) * 2 + half))
    return pairs


def result_pairs(flip):
    pairs = []
    for member in range(8):
        y_lo, z = divmod(member, 4)
        for tok in range(8):
            x, core = divmod(tok, 2)
            for half in range(2):
                to_member = core * 4 + z
                to_tok = 4 * half + kept(x, half)
                to_col = y_lo ^ flip
                pairs.append(((member * 8 + tok) * 2 + half, (to_member * 8 + to_tok) * 2 + to_col))
    return pairs


def x_pairs(flip):
    return [(t, ((t // 2) ^ flip) * 2 + t % 2) for t in range(X * CORES)]


def shards(inputs, grads, weights):
    tok = lax.axis_index("tok")
    half = lax.axis_index("col")
    x, core = tok // 2, tok % 2
    y_lo = lax.axis_index("member") // 4

    flips = ((1, 3), (3, 1))
    places = []
    for first, second in flips:
        steps = x ^ jnp.array([first, 2, 0, second], jnp.int32)
        local = jnp.where(steps // 2 == half, 2 * (steps % 2), 2 * ((3 - steps) % 2) + 1)
        places.append(jnp.concatenate([2 * local + 1 - core, 2 * local + core]).astype(jnp.int32))

    tokens, outs = grads.shape[1:]
    wide = inputs.shape[2] // 8
    send_shape, x_shape, gt_shape = ((4, outs, wide), BF16), ((8, tokens, wide), BF16), ((outs, tokens), BF16)
    pair, kept_shape = ((2, outs, wide), BF16), ((2, outs, wide), F32)
    block, own_shape, sums = ((outs, wide), BF16), ((outs, wide), F32), ((wide, outs), F32)
    dma = pltpu.SemaphoreType.DMA
    flops = 8 * outs * wide * tokens

    def swap_cores(send):
        return lax.ppermute(send, "tok", [(t, t ^ 1) for t in range(8)])

    def load(member, after):
        return call(
            lambda *refs: load_kernel(member, *refs), "load_and_fisher_for_other_core",
            [send_shape, x_shape, gt_shape], [places[member]], [inputs, grads], after,
            [pltpu.VMEM((tokens, outs), BF16), dma((8,)), dma], flops,
        )

    def own_part(member, x_blocks, gt, got, after):
        sent, kept_blocks = call(
            own_kernel, "fisher_of_own_core", [pair, kept_shape], [], [], [x_blocks, gt, got, after], flops=flops
        )
        return lax.ppermute(sent, "tok", x_pairs(flips[member][0])), kept_blocks

    def middle(member, got, kept_blocks, after):
        sent, own = call(
            middle_kernel, "fisher_over_first_swap", [block, own_shape], [], [], [kept_blocks, got, after], flops=30 * outs * wide
        )
        return own, lax.ppermute(sent, "tok", x_pairs(flips[member][1]))

    def other_part(member, after):
        return call(
            lambda *refs: send_kernel(member, *refs), "fisher_for_other_core", [send_shape, gt_shape], [], [],
            [xs[member], other, after], flops=flops,
        )

    def weigh(phase, one, two, after):
        which = ((core ^ half) ^ phase).astype(jnp.int32).reshape(1)
        words = ((2 * Z, 3, wide // Z, outs // 2), BF16)
        begun = call(begin_kernel, "weigh_first", [sums, sums], [which], [], [*one, *moved, after], flops=20 * outs * wide)
        return call(finish_kernel, "weigh_second", words, [which], [], [*two, *moved, *begun], flops=40 * outs * wide)

    other = lax.ppermute(grads, "col", [(0, 1), (1, 0)])
    arrived = lax.ppermute(weights, ("tok", "col"), weight_pairs())

    send0, x0, gt0 = load(0, [])
    got0 = swap_cores(send0)
    send1, x1, gt1 = load(1, [gt0])
    got1 = swap_cores(send1)
    xs = (x0, x1)
    swap00, kept00 = own_part(0, x0, gt0, got0, gt1)
    swap01, kept01 = own_part(1, x1, gt1, got1, kept00)
    part00 = middle(0, swap00, kept00, kept01)
    part01 = middle(1, swap01, kept01, part00[0])
    rows = weights.shape[1] // 2
    w_own, w_send = call(
        split_kernel, "split_weights", [((2, rows, outs), BF16)] * 2, [core.astype(jnp.int32).reshape(1)], [],
        [arrived, part01[0]],
    )
    moved = (w_own, swap_cores(w_send))

    send0, gt0 = other_part(0, w_own)
    got0 = swap_cores(send0)
    send1, gt1 = other_part(1, gt0)
    got1 = swap_cores(send1)
    swap10, kept10 = own_part(0, x0, gt0, got0, gt1)
    swap11, kept11 = own_part(1, x1, gt1, got1, kept10)

    out = ((wide // Z, outs // 2), F32)
    words = weigh(0, part00, part01, kept11)
    merged = call(merge_kernel, "merge_members", out, [], [], [lax.all_to_all(words, "member", 0, 0, tiled=True)])
    part10 = middle(0, swap10, kept10, words)
    part11 = middle(1, swap11, kept11, part10[0])
    words = weigh(1, part10, part11, part11[0])
    got = lax.all_to_all(words, "member", 0, 0, tiled=True)
    swap = (y_lo ^ half).astype(jnp.int32).reshape(1)
    near, far = call(merge_last_kernel, "merge_members", [out, out], [swap], [], [got, merged])

    names = ("member", "tok", "col")
    near = lax.ppermute(near, names, result_pairs(0))
    far = lax.ppermute(far, names, result_pairs(1))
    left = jnp.where(half == 0, near, far)
    right = jnp.where(half == 0, far, near)
    return jnp.concatenate([left, right], axis=1)


def solution(mesh):
    in_specs = (P("member", "tok", "col"), P("member", "tok", "col"), P("member", "tok", "col"))
    out_specs = P(("tok", "member"), "col")
    return jax.shard_map(shards, mesh=mesh, in_specs=in_specs, out_specs=out_specs, check_vma=False)
```

```python
import jax
import jax.numpy as jnp
from jax import lax
from jax.experimental import pallas as pl
from jax.experimental.pallas import tpu as pltpu
from jax.sharding import PartitionSpec as P

F32 = jnp.float32
BF16 = jnp.bfloat16
HBM = pl.BlockSpec(memory_space=pltpu.HBM)
VMEM = pl.BlockSpec(memory_space=pltpu.VMEM)
VMEM_LIMIT = 16 << 20

GRID = 1.00297
BIG = 2.0**28
SMALL = 2.0**16
EDGE = 2.0**-40
EDGE_CODE = 2.0**-24

X, CORES, Z = 4, 2, 4

ORDERS = ((1, 2, 0, 3), (3, 2, 0, 1))


def code_of(values):
    scaled = values * BIG
    return jnp.where(values >= EDGE, scaled * scaled, values * SMALL)


def value_of(code):
    return jnp.where(code >= EDGE_CODE, jnp.sqrt(code) * (1.0 / BIG), code * (1.0 / SMALL))


def encode(values):
    return code_of(values).astype(BF16)


def decode(sent):
    return value_of(sent.astype(F32))


def encode_fine(values):
    code = code_of(values)
    first = code.astype(BF16).astype(F32)
    second = (code * (1.0 / GRID)).astype(BF16).astype(F32)
    near = jnp.abs(first - code) <= jnp.abs(second * GRID - code)
    return jnp.where(near, first, -second).astype(BF16)


def decode_fine(sent):
    code = sent.astype(F32)
    return value_of(jnp.where(code < 0.0, code * (-GRID), code))


def in_vmem(array):
    return pltpu.with_memory_space_constraint(array, pltpu.VMEM)


def in_hbm(array):
    return pltpu.with_memory_space_constraint(array, pltpu.HBM)


def call(kernel, name, outs, hbm, vmem, scratch=(), flops=0):
    single = not isinstance(outs, list)
    shapes = [pltpu.VMEM(shape, kind) for shape, kind in ([outs] if single else outs)]
    moved = sum(a.size * 2 for a in vmem) + sum(a.size * 2 for a in hbm)
    result = pl.pallas_call(
        kernel,
        out_shape=shapes,
        in_specs=[HBM] * len(hbm) + [VMEM] * len(vmem),
        out_specs=[VMEM] * len(shapes),
        scratch_shapes=list(scratch),
        compiler_params=pltpu.CompilerParams(vmem_limit_bytes=VMEM_LIMIT),
        cost_estimate=pl.CostEstimate(flops=flops, bytes_accessed=moved, transcendentals=0),
        name=name,
    )(*[in_hbm(a) for a in hbm], *[in_vmem(a) for a in vmem])
    return result[0] if single else result


def squared_transposed(g):
    g = g.astype(F32)
    return (g * g).T.astype(BF16)


def fisher_block(x, gt_ref):
    return jnp.dot(gt_ref[...], x * x, preferred_element_type=F32)


def where_am_i():
    tok, half, member = lax.axis_index("tok"), lax.axis_index("col"), lax.axis_index("member")
    return tok // 2, tok % 2, half, member // Z, member % Z


def column_block(flip, part):
    x, _, half, _, _ = where_am_i()
    owner = x ^ flip
    local = jnp.where(owner // 2 == half, 2 * (owner % 2), 2 * ((3 - owner) % 2) + 1)
    return 2 * local + part


def load_inputs(member, part, x_ref, x_out, sem):
    wide = x_out.shape[2]
    copies = []
    for s, flip in enumerate(ORDERS[part]):
        at = pl.multiple_of(column_block(flip, part) * wide, wide)
        copies.append(pltpu.make_async_copy(x_ref.at[member, :, pl.ds(at, wide)], x_out.at[s], sem.at[s]))
        copies[s].start()
    return copies


def load_first_kernel(x_ref, g_ref, x_out, g_out, g_own_out, sem, g_sem):
    core = where_am_i()[1]
    loads = [
        pltpu.make_async_copy(g_ref.at[1 - core], g_out, g_sem.at[0]),
        pltpu.make_async_copy(g_ref.at[core], g_own_out, g_sem.at[1]),
    ]
    for copy in loads:
        copy.start()
    for copy in load_inputs(1 - core, 0, x_ref, x_out, sem) + loads:
        copy.wait()


def load_second_kernel(x_ref, after, x_out, sem):
    for copy in load_inputs(1 - where_am_i()[1], 1, x_ref, x_out, sem):
        copy.wait()


def pair_kernel(own, got, after, out):
    out[0], out[1] = own[...], got[...]


def own_tokens(copies, x_out, gt_ref, part_out):
    for s in range(4):
        copies[s].wait()
        part_out[s] = fisher_block(x_out[s], gt_ref)


def own_first_kernel(x_ref, g_ref, after, x_out, gt_out, part_out, sem):
    copies = load_inputs(where_am_i()[1], 0, x_ref, x_out, sem)
    gt_out[...] = squared_transposed(g_ref[...])
    own_tokens(copies, x_out, gt_out, part_out)


def own_second_kernel(x_ref, gt_ref, after, x_out, part_out, sem):
    copies = load_inputs(where_am_i()[1], 1, x_ref, x_out, sem)
    own_tokens(copies, x_out, gt_ref, part_out)


def put(s, block, sent_out, kept_out):
    if s < 2:
        sent_out[s] = encode(block)
    else:
        kept_out[s - 2] = block


def add_first_kernel(x_ref, g_ref, part_ref, sent_out, kept_out, gt_out):
    gt_out[...] = squared_transposed(g_ref[...])
    for s in range(4):
        put(s, part_ref[s] + fisher_block(x_ref[s], gt_out), sent_out, kept_out)


def add_second_kernel(x_ref, gt_ref, part_ref, after, sent_out, kept_out):
    for s in range(4):
        put(s, part_ref[s] + fisher_block(x_ref[s], gt_ref), sent_out, kept_out)


def both_first_kernel(xa_ref, xb_ref, g_ref, after, sent_out, kept_out, gta_out, gtb_out):
    gta_out[...] = squared_transposed(g_ref[0])
    gtb_out[...] = squared_transposed(g_ref[1])
    for s in range(4):
        put(s, fisher_block(xa_ref[s], gta_out) + fisher_block(xb_ref[s], gtb_out), sent_out, kept_out)


def both_second_kernel(xa_ref, xb_ref, gta_ref, gtb_ref, after, sent_out, kept_out):
    for s in range(4):
        put(s, fisher_block(xa_ref[s], gta_ref) + fisher_block(xb_ref[s], gtb_ref), sent_out, kept_out)


def middle_kernel(kept_ref, got_ref, after, sent_out, own_out):
    sent_out[...] = encode_fine(kept_ref[1] + decode(got_ref[1]))
    own_out[...] = kept_ref[0] + decode(got_ref[0])


def join_kernel(own_a, got_a, own_b, got_b, after, kept_out, sent_out):
    first = own_a[...] + decode_fine(got_a[...])
    second = own_b[...] + decode_fine(got_b[...])
    core = where_am_i()[1]
    kept_out[...] = jnp.where(core == 0, first, second)
    sent_out[...] = jnp.where(core == 0, second, first)


def split_kernel(w_ref, after, own_out, send_out):
    rows, core = own_out.shape[1], where_am_i()[1]
    own_out[...] = w_ref[:, pl.ds(pl.multiple_of(core * rows, rows), rows), :]
    send_out[...] = w_ref[:, pl.ds(pl.multiple_of((1 - core) * rows, rows), rows), :]


def to_words(weighted, total, out):
    high = weighted.astype(BF16)
    out[0] = high
    out[1] = (weighted - high.astype(F32)).astype(BF16)
    out[2] = encode_fine(total)


def from_words(words):
    return words[0].astype(F32) + words[1].astype(F32), decode_fine(words[2])


def weigh_kernel(phase, own, other, w_a, w_b, after, one_out, two_out, three_out, sums_out):
    _, core, half, _, z = where_am_i()
    part = own.shape[1] // Z
    first = (core ^ half ^ phase) == 0
    for d, out in ((2, two_out), (1, one_out), (3, three_out), (0, sums_out)):
        cols = pl.ds(pl.multiple_of((z + d) % Z * part, part), part)
        weighted = total = 0.0
        for values, m in ((own, core), (other, 1 - core)):
            fisher = values[:, cols].T
            weight = jnp.where(first, w_a[m, cols, :].astype(F32), w_b[m, cols, :].astype(F32))
            weighted += fisher * weight
            total += fisher
        if d == 0:
            out[0], out[1] = weighted, total
        else:
            to_words(weighted, total, out)


def over_z(sums, words):
    weighted, total = sums[0], sums[1]
    for ref in words:
        more, added = from_words(ref)
        weighted += more
        total += added
    return weighted, total


def sum_kernel(one, two, three, sums, out):
    to_words(*over_z(sums, (one, two, three)), out)


def sum_last_kernel(one, two, three, sums, first, near_out, far_out):
    y_lo = where_am_i()[3]

    @pl.when(y_lo == 0)
    def _():
        to_words(*over_z(sums, (one, two, three)), far_out)
        near_out[...] = first[...]

    @pl.when(y_lo != 0)
    def _():
        to_words(*over_z(sums, (one, two, three)), near_out)
        far_out[...] = first[...]


def merge_kernel(near, far, out):
    weighted, total = from_words(near)
    more, added = from_words(far)
    out[...] = (weighted + more) / (total + added)


def keeper(local, half):
    home = 2 * half + local // 2
    return home if local % 2 == 0 else 3 - home


def kept(x, half):
    return 2 * (x % 2) if x // 2 == half else 2 * ((3 - x) % 2) + 1


def weight_pairs():
    pairs = []
    for tok in range(X * CORES):
        half, local = divmod(tok, 4)
        for col in range(2):
            pairs.append((tok * 2 + col, (keeper(local, half) * 2 + col) * 2 + half))
    return pairs


def result_pairs(flip):
    pairs = []
    for member in range(8):
        y_lo, z = divmod(member, 4)
        for tok in range(8):
            x, core = divmod(tok, 2)
            for half in range(2):
                to_member = core * 4 + z
                to_tok = 4 * half + kept(x, half)
                to_col = half ^ y_lo ^ flip
                pairs.append(((member * 8 + tok) * 2 + half, (to_member * 8 + to_tok) * 2 + to_col))
    return pairs


def x_pairs(flip):
    return [(t, ((t // 2) ^ flip) * 2 + t % 2) for t in range(X * CORES)]


def z_pairs(distance):
    return [(m, m // Z * Z + (m + distance) % Z) for m in range(2 * Z)]


def shards(inputs, grads, weights):
    tokens, outs = grads.shape[1:]
    wide = inputs.shape[2] // 8
    x_shape, g_shape, gt_shape = ((4, tokens, wide), BF16), ((tokens, outs), BF16), ((outs, tokens), BF16)
    part_shape, sent_shape, kept_shape = ((4, outs, wide), F32), ((2, outs, wide), BF16), ((2, outs, wide), F32)
    code_shape, own_shape = ((outs, wide), BF16), ((outs, wide), F32)
    words, sums = ((3, wide // Z, outs), BF16), ((2, wide // Z, outs), F32)
    dma = pltpu.SemaphoreType.DMA
    flops = 8 * outs * wide * tokens

    def swap_cores(send):
        return lax.ppermute(send, "tok", [(t, t ^ 1) for t in range(8)])

    def swap_cols(send):
        return lax.ppermute(send, "col", [(0, 1), (1, 0)])

    def first_swap(part, sent):
        return lax.ppermute(sent, "tok", x_pairs(ORDERS[part][0]))

    def middle(part, got, kept_blocks, after):
        sent, own = call(middle_kernel, "fisher_over_first_swap", [code_shape, own_shape], [], [kept_blocks, got, after])
        return own, lax.ppermute(sent, "tok", x_pairs(ORDERS[part][3]))

    def join(one, two, after):
        kept_block, sent = call(join_kernel, "fisher_over_tokens", [own_shape, own_shape], [], [*one, *two, after])
        return kept_block, swap_cores(sent)

    def weigh(phase, own, other, after):
        one, two, three, own_sums = call(
            lambda *refs: weigh_kernel(phase, *refs), "weigh_members", [words] * 3 + [sums], [], [own, other, *moved, after]
        )
        send = ((1, one), (2, two), (3, three))
        return [lax.ppermute(v, "member", z_pairs(d)) for d, v in send] + [own_sums]

    x_send0, g_send, g_own = call(
        load_first_kernel, "load_to_swap", [x_shape, g_shape, g_shape], [inputs, grads], [], [dma((4,)), dma((2,))]
    )
    x_got0 = swap_cores(x_send0)
    g_got = swap_cores(g_send)
    x_send1 = call(load_second_kernel, "load_to_swap", x_shape, [inputs], [g_own], [dma((4,))])
    x_got1 = swap_cores(x_send1)
    g_pair = call(pair_kernel, "pair_grads", ((2, tokens, outs), BF16), [], [g_own, g_got, x_send1])
    g_other = swap_cols(g_pair)

    x_own0, gt_own, part0 = call(
        own_first_kernel, "fisher_of_own_tokens", [x_shape, gt_shape, part_shape], [inputs], [g_own, g_pair],
        [dma((4,))], flops,
    )
    sent, kept00, gt_got = call(
        add_first_kernel, "fisher_of_both_cores", [sent_shape, kept_shape, gt_shape], [], [x_got0, g_got, part0], flops=flops
    )
    swap00 = first_swap(0, sent)
    x_own1, part1 = call(
        own_second_kernel, "fisher_of_own_tokens", [x_shape, part_shape], [inputs], [gt_own, kept00], [dma((4,))], flops
    )
    sent, kept01 = call(
        add_second_kernel, "fisher_of_both_cores", [sent_shape, kept_shape], [], [x_got1, gt_got, part1, x_own1], flops=flops
    )
    swap01 = first_swap(1, sent)
    part00 = middle(0, swap00, kept00, kept01)
    part01 = middle(1, swap01, kept01, part00[0])

    sent, kept10, gt_own, gt_got = call(
        both_first_kernel, "fisher_of_other_grads", [sent_shape, kept_shape, gt_shape, gt_shape], [],
        [x_own0, x_got0, g_other, part01[0]], flops=2 * flops,
    )
    swap10 = first_swap(0, sent)
    sent, kept11 = call(
        both_second_kernel, "fisher_of_other_grads", [sent_shape, kept_shape], [],
        [x_own1, x_got1, gt_own, gt_got, kept10], flops=2 * flops,
    )
    swap11 = first_swap(1, sent)
    own0, other0 = join(part00, part01, kept11)
    part10 = middle(0, swap10, kept10, own0)
    part11 = middle(1, swap11, kept11, part10[0])

    arrived = lax.ppermute(weights, ("tok", "col"), weight_pairs())
    rows = weights.shape[1] // 2
    w_own, w_send = call(split_kernel, "split_weights", [((2, rows, outs), BF16)] * 2, [], [arrived, part11[0]])
    moved = (w_own, swap_cores(w_send))
    words0 = weigh(0, own0, other0, w_own)
    own1, other1 = join(part10, part11, words0[3])
    words1 = weigh(1, own1, other1, own1)
    first = call(sum_kernel, "sum_over_z", words, [], words0)
    near, far = call(sum_last_kernel, "sum_over_z", [words, words], [], [*words1, first])

    names = ("member", "tok", "col")
    near = lax.ppermute(near, names, result_pairs(0))
    far = lax.ppermute(far, names, result_pairs(1))
    return pl.pallas_call(
        merge_kernel,
        out_shape=jax.ShapeDtypeStruct((wide // Z, outs), F32),
        in_specs=[VMEM, VMEM],
        out_specs=VMEM,
        compiler_params=pltpu.CompilerParams(vmem_limit_bytes=VMEM_LIMIT),
        name="merge_members",
    )(in_vmem(near), in_vmem(far))


def solution(mesh):
    in_specs = (P("member", "tok", "col"), P("member", "tok", "col"), P("member", "tok", "col"))
    out_specs = P(("tok", "member"), "col")
    return jax.shard_map(shards, mesh=mesh, in_specs=in_specs, out_specs=out_specs, check_vma=False)
```

```python
import jax
import jax.numpy as jnp
from jax import lax
from jax.experimental import pallas as pl
from jax.experimental.pallas import tpu as pltpu
from jax.sharding import PartitionSpec as P

F32 = jnp.float32
BF16 = jnp.bfloat16
HBM = pl.BlockSpec(memory_space=pltpu.HBM)
VMEM = pl.BlockSpec(memory_space=pltpu.VMEM)
VMEM_LIMIT = 16 << 20

GRID = 1.00297
BIG = 2.0**28
SMALL = 2.0**16
EDGE = 2.0**-40
EDGE_CODE = 2.0**-24

X, CORES, Z = 4, 2, 4

ORDER = (1, 2, 0, 3)
BACK = (3, 1, 2, 0)


def code_of(values):
    scaled = values * BIG
    return jnp.where(values >= EDGE, scaled * scaled, values * SMALL)


def value_of(code):
    return jnp.where(code >= EDGE_CODE, jnp.sqrt(code) * (1.0 / BIG), code * (1.0 / SMALL))


def encode(values):
    return code_of(values).astype(BF16)


def decode(sent):
    return value_of(sent.astype(F32))


def encode_fine(values):
    code = code_of(values)
    first = code.astype(BF16).astype(F32)
    second = (code * (1.0 / GRID)).astype(BF16).astype(F32)
    near = jnp.abs(first - code) <= jnp.abs(second * GRID - code)
    return jnp.where(near, first, -second).astype(BF16)


def decode_fine(sent):
    code = sent.astype(F32)
    return value_of(jnp.where(code < 0.0, code * (-GRID), code))


def in_vmem(array):
    return pltpu.with_memory_space_constraint(array, pltpu.VMEM)


def in_hbm(array):
    return pltpu.with_memory_space_constraint(array, pltpu.HBM)


def call(kernel, name, outs, hbm, vmem, scratch=(), flops=0):
    single = not isinstance(outs, list)
    shapes = [pltpu.VMEM(shape, kind) for shape, kind in ([outs] if single else outs)]
    result = pl.pallas_call(
        kernel,
        out_shape=shapes,
        in_specs=[HBM] * len(hbm) + [VMEM] * len(vmem),
        out_specs=[VMEM] * len(shapes),
        scratch_shapes=list(scratch),
        compiler_params=pltpu.CompilerParams(vmem_limit_bytes=VMEM_LIMIT),
        cost_estimate=pl.CostEstimate(flops=1, bytes_accessed=1, transcendentals=0),
        name=name,
    )(*[in_hbm(a) for a in hbm], *[in_vmem(a) for a in vmem])
    return result[0] if single else result


def squared_transposed(g):
    g = g.astype(F32)
    return (g * g).T.astype(BF16)


def fisher_block(x, gt_ref):
    return jnp.dot(gt_ref[...], x * x, preferred_element_type=F32)


def where_am_i():
    tok, half, member = lax.axis_index("tok"), lax.axis_index("col"), lax.axis_index("member")
    return tok // 2, tok % 2, half, member // Z, member % Z


def column_block(flip, part):
    x, _, half, _, _ = where_am_i()
    owner = x ^ flip
    local = jnp.where(owner // 2 == half, 2 * (owner % 2), 2 * ((3 - owner) % 2) + 1)
    return 2 * local + part


def load_inputs(member, part, x_ref, x_out, sem):
    wide = x_out.shape[2]
    copies = []
    for s, flip in enumerate(ORDER):
        at = pl.multiple_of(column_block(flip, part) * wide, wide)
        copies.append(pltpu.make_async_copy(x_ref.at[member, :, pl.ds(at, wide)], x_out.at[s], sem.at[s]))
        copies[s].start()
    return copies


def load_grads_kernel(g_ref, g_out, g_own_out, sem):
    core = where_am_i()[1]
    loads = [
        pltpu.make_async_copy(g_ref, g_out.at[:, pl.ds(0, g_ref.shape[1])], sem.at[0]),
        pltpu.make_async_copy(g_ref.at[core], g_own_out, sem.at[1]),
    ]
    for copy in loads:
        copy.start()
    for copy in loads:
        copy.wait()


def load_first_kernel(x_ref, g_ref, after, out, sem, g_sem):
    core = where_am_i()[1]
    wide = x_ref.shape[2] // 8
    copies = [pltpu.make_async_copy(g_ref.at[1 - core], out.at[:, pl.ds(4 * wide, g_ref.shape[2])], g_sem)]
    for s, flip in enumerate(ORDER):
        at = pl.multiple_of(column_block(flip, 0) * wide, wide)
        copies.append(
            pltpu.make_async_copy(x_ref.at[1 - core, :, pl.ds(at, wide)], out.at[:, pl.ds(s * wide, wide)], sem.at[s])
        )
    for copy in copies:
        copy.start()
    for copy in copies:
        copy.wait()


def load_second_kernel(x_ref, after, x_out, sem):
    for copy in load_inputs(1 - where_am_i()[1], 1, x_ref, x_out, sem):
        copy.wait()


def pick_grads_kernel(g_ref, after, kept_out, sent_out):
    core = where_am_i()[1]
    rows = kept_out.shape[0]
    kept_out[...] = g_ref[core, :rows]
    sent_out[...] = g_ref[1 - core, :rows]


def own_tokens(copies, x_out, gt_ref, part_out):
    for s in range(4):
        copies[s].wait()
        part_out[s] = fisher_block(x_out[s], gt_ref)


def own_first_kernel(x_ref, g_ref, after, x_out, gt_out, part_out, sem):
    copies = load_inputs(where_am_i()[1], 0, x_ref, x_out, sem)
    gt_out[...] = squared_transposed(g_ref[...])
    own_tokens(copies, x_out, gt_out, part_out)


def own_second_kernel(x_ref, gt_ref, after, x_out, part_out, sem):
    copies = load_inputs(where_am_i()[1], 1, x_ref, x_out, sem)
    own_tokens(copies, x_out, gt_ref, part_out)


def put(s, block, sent_out, kept_out):
    if s < 2:
        sent_out[s] = encode(block)
    else:
        kept_out[s - 2] = block


def add_first_kernel(x_ref, part_ref, sent_out, kept_out, gt_out):
    wide = part_ref.shape[2]
    gt_out[...] = squared_transposed(x_ref[:, 4 * wide :])
    for s in range(4):
        block = fisher_block(x_ref[:, s * wide : (s + 1) * wide], gt_out)
        put(s, part_ref[s] + block, sent_out, kept_out)


def add_second_kernel(x_ref, gt_ref, part_ref, after, sent_out, kept_out):
    for s in range(4):
        put(s, part_ref[s] + fisher_block(x_ref[s], gt_ref), sent_out, kept_out)


def both_first_kernel(xa_ref, xb_ref, ga_ref, gb_ref, after, sent_out, kept_out, gta_out, gtb_out):
    wide = kept_out.shape[2]
    gta_out[...] = squared_transposed(ga_ref[...])
    gtb_out[...] = squared_transposed(gb_ref[...])
    for s in range(4):
        block = fisher_block(xb_ref[:, s * wide : (s + 1) * wide], gtb_out)
        put(s, fisher_block(xa_ref[s], gta_out) + block, sent_out, kept_out)


def both_second_kernel(xa_ref, xb_ref, gta_ref, gtb_ref, after, sent_out, kept_out):
    for s, block in enumerate(BACK):
        put(s, fisher_block(xa_ref[block], gta_ref) + fisher_block(xb_ref[block], gtb_ref), sent_out, kept_out)


def middle_kernel(kept_ref, got_ref, after, sent_out, own_out):
    sent_out[...] = encode_fine(kept_ref[1] + decode(got_ref[1]))
    own_out[...] = kept_ref[0] + decode(got_ref[0])


def settle_kernel(own, got, out):
    out[...] = own[...] + decode_fine(got[...])


def join_kernel(first_ref, own, got, after, kept_out, sent_out):
    first = first_ref[...]
    second = own[...] + decode_fine(got[...])
    core = where_am_i()[1]
    kept_out[...] = jnp.where(core == 0, first, second)
    sent_out[...] = jnp.where(core == 0, second, first)


def split_kernel(w_ref, after, own_out, send_out):
    rows, core = own_out.shape[1], where_am_i()[1]
    own_out[...] = w_ref[:, pl.ds(pl.multiple_of(core * rows, rows), rows), :]
    send_out[...] = w_ref[:, pl.ds(pl.multiple_of((1 - core) * rows, rows), rows), :]


def to_words(weighted, total, out):
    high = weighted.astype(BF16)
    out[0] = high
    out[1] = (weighted - high.astype(F32)).astype(BF16)
    out[2] = encode_fine(total)


def from_words(words):
    return words[0].astype(F32) + words[1].astype(F32), decode_fine(words[2])


def weigh_kernel(phase, own, other, w_a, w_b, after, one_out, two_out, three_out, sums_out):
    _, core, half, _, z = where_am_i()
    part = own.shape[1] // Z
    first = (core ^ half ^ phase) == 0
    for d, out in ((2, two_out), (1, one_out), (3, three_out), (0, sums_out)):
        cols = pl.ds(pl.multiple_of((z + d) % Z * part, part), part)
        weighted = total = 0.0
        for values, m in ((own, core), (other, 1 - core)):
            fisher = values[:, cols].T
            weight = jnp.where(first, w_a[m, cols, :].astype(F32), w_b[m, cols, :].astype(F32))
            weighted += fisher * weight
            total += fisher
        if d == 0:
            out[0], out[1] = weighted, total
        else:
            to_words(weighted, total, out)


def over_z(sums, words):
    weighted, total = sums[0], sums[1]
    for ref in words:
        more, added = from_words(ref)
        weighted += more
        total += added
    return weighted, total


def sum_kernel(one, two, three, sums, out):
    to_words(*over_z(sums, (one, two, three)), out)


def meet_kernel(near, far, after, out):
    (weighted, total), (more, added) = from_words(near), from_words(far)
    out[0], out[1] = weighted + more, total + added


def merge_kernel(near, far, sums, out):
    (weighted, total), (more, added) = from_words(near), from_words(far)
    out[...] = (weighted + more + sums[0]) / (total + added + sums[1])


def keeper(local, half):
    home = 2 * half + local // 2
    return home if local % 2 == 0 else 3 - home


def kept(x, half):
    return 2 * (x % 2) if x // 2 == half else 2 * ((3 - x) % 2) + 1


def weight_pairs():
    pairs = []
    for tok in range(X * CORES):
        half, local = divmod(tok, 4)
        for col in range(2):
            pairs.append((tok * 2 + col, (keeper(local, half) * 2 + col) * 2 + half))
    return pairs


def result_pairs(phase, sender):
    pairs = []
    for z in range(Z):
        for tok in range(X * CORES):
            x, core = divmod(tok, 2)
            for half in range(2):
                to_tok = 4 * half + kept(x, half)
                to = ((core * Z + z) * 8 + to_tok) * 2 + (half ^ phase)
                pairs.append((((sender * Z + z) * 8 + tok) * 2 + half, to))
    return pairs


def x_pairs(flip):
    return [(t, ((t // 2) ^ flip) * 2 + t % 2) for t in range(X * CORES)]


def z_pairs(distance):
    return [(m, m // Z * Z + (m + distance) % Z) for m in range(2 * Z)]


def shards(inputs, grads, weights):
    tokens, outs = grads.shape[1:]
    wide = inputs.shape[2] // 8
    x_shape, g_shape, gt_shape = ((4, tokens, wide), BF16), ((tokens, outs), BF16), ((outs, tokens), BF16)
    part_shape, sent_shape, kept_shape = ((4, outs, wide), F32), ((2, outs, wide), BF16), ((2, outs, wide), F32)
    code_shape, own_shape = ((outs, wide), BF16), ((outs, wide), F32)
    words, sums = ((3, wide // Z, outs), BF16), ((2, wide // Z, outs), F32)
    dma = pltpu.SemaphoreType.DMA
    flops = 8 * outs * wide * tokens

    def swap_cores(send):
        return lax.ppermute(send, "tok", [(t, t ^ 1) for t in range(8)])

    def swap_cols(send):
        return lax.ppermute(send, "col", [(0, 1), (1, 0)])

    def swap_x(flip, sent):
        return lax.ppermute(sent, "tok", x_pairs(flip))

    def middle(flip, got, kept_blocks, after):
        sent, own = call(middle_kernel, "fisher_over_first_swap", [code_shape, own_shape], [], [kept_blocks, got, after])
        return own, swap_x(flip, sent)

    def settle(one):
        return call(settle_kernel, "fisher_over_tokens", own_shape, [], [*one])

    def join(first, two, after):
        kept_block, sent = call(join_kernel, "fisher_over_tokens", [own_shape, own_shape], [], [first, *two, after])
        return kept_block, swap_cores(sent)

    def results(phase, sums):
        return [lax.ppermute(sums, ("member", "tok", "col"), result_pairs(phase, y_lo)) for y_lo in range(2)]

    def weigh(phase, own, other, after):
        one, two, three, own_sums = call(
            lambda *refs: weigh_kernel(phase, *refs), "weigh_members", [words] * 3 + [sums], [], [own, other, *moved, after]
        )
        send = ((1, one), (2, two), (3, three))
        return [lax.ppermute(v, "member", z_pairs(d)) for d, v in send] + [own_sums]

    g_pair, g_own = call(
        load_grads_kernel, "load_grads", [((2, tokens + 64, outs), BF16), g_shape], [grads], [], [dma((2,))]
    )
    g_other = swap_cols(g_pair)
    x_send0 = call(
        load_first_kernel, "load_to_swap", ((tokens, 4 * wide + outs), BF16), [inputs, grads], [g_own], [dma((4,)), dma]
    )
    x_got0 = swap_cores(x_send0)
    x_send1 = call(load_second_kernel, "load_to_swap", x_shape, [inputs], [x_send0], [dma((4,))])
    x_got1 = swap_cores(x_send1)

    x_own0, gt_own, part0 = call(
        own_first_kernel, "fisher_of_own_tokens", [x_shape, gt_shape, part_shape], [inputs], [g_own, x_send1],
        [dma((4,))], flops,
    )
    sent, kept00, gt_got = call(
        add_first_kernel, "fisher_of_both_cores", [sent_shape, kept_shape, gt_shape], [], [x_got0, part0], flops=flops
    )
    swap00 = swap_x(1, sent)
    x_own1, part1 = call(
        own_second_kernel, "fisher_of_own_tokens", [x_shape, part_shape], [inputs], [gt_own, kept00], [dma((4,))], flops
    )
    sent, kept01 = call(
        add_second_kernel, "fisher_of_both_cores", [sent_shape, kept_shape], [], [x_got1, gt_got, part1, x_own1], flops=flops
    )
    swap01 = swap_x(1, sent)
    settled0 = settle(middle(3, swap00, kept00, kept01))
    part01 = middle(3, swap01, kept01, settled0)

    arrived = lax.ppermute(weights, ("tok", "col"), weight_pairs())
    rows = weights.shape[1] // 2
    w_own, w_send = call(split_kernel, "split_weights", [((2, rows, outs), BF16)] * 2, [], [arrived, part01[0]])
    moved = (w_own, swap_cores(w_send))

    g_kept, g_sent = call(pick_grads_kernel, "pick_grads", [g_shape, g_shape], [], [g_other, part01[0]])
    sent, kept10, gt_own, gt_got = call(
        both_first_kernel, "fisher_of_other_grads", [sent_shape, kept_shape, gt_shape, gt_shape], [],
        [x_own0, x_got0, g_kept, swap_cores(g_sent), w_own], flops=2 * flops,
    )
    swap10 = swap_x(1, sent)
    sent, kept11 = call(
        both_second_kernel, "fisher_of_other_grads", [sent_shape, kept_shape], [],
        [x_own1, x_got1, gt_own, gt_got, kept10], flops=2 * flops,
    )
    swap11 = swap_x(3, sent)
    own0, other0 = join(settled0, part01, kept11)
    part10 = middle(3, swap10, kept10, own0)
    part11 = middle(1, swap11, kept11, part10[0])

    words0 = weigh(0, own0, other0, part11[0])
    first = call(sum_kernel, "sum_over_z", words, [], words0)
    own1, other1 = join(settle(part10), part11, first)
    words1 = weigh(1, own1, other1, own1)
    met = call(meet_kernel, "meet_over_y", sums, [], [*results(0, first), own1])
    second = call(sum_kernel, "sum_over_z", words, [], [*words1])
    near, far = results(1, second)
    return pl.pallas_call(
        merge_kernel,
        out_shape=jax.ShapeDtypeStruct((wide // Z, outs), F32),
        in_specs=[VMEM] * 3,
        out_specs=VMEM,
        compiler_params=pltpu.CompilerParams(vmem_limit_bytes=VMEM_LIMIT),
        name="merge_members",
    )(in_vmem(near), in_vmem(far), in_vmem(met))


def solution(mesh):
    in_specs = (P("member", "tok", "col"), P("member", "tok", "col"), P("member", "tok", "col"))
    out_specs = P(("tok", "member"), "col")
    return jax.shard_map(shards, mesh=mesh, in_specs=in_specs, out_specs=out_specs, check_vma=False)
```

```python
import jax
import jax.numpy as jnp
from jax import lax
from jax.experimental import pallas as pl
from jax.experimental.pallas import tpu as pltpu
from jax.sharding import PartitionSpec as P

F32 = jnp.float32
BF16 = jnp.bfloat16
HBM = pl.BlockSpec(memory_space=pltpu.HBM)
VMEM = pl.BlockSpec(memory_space=pltpu.VMEM)
VMEM_LIMIT = 16 << 20

GRID = 1.00297
BIG = 2.0**28
SMALL = 2.0**16
EDGE = 2.0**-40
EDGE_CODE = 2.0**-24

X, CORES, Z = 4, 2, 4

ORDER = (1, 2, 0, 3)
BACK = (3, 1, 2, 0)


def code_of(values):
    scaled = values * BIG
    return jnp.where(values >= EDGE, scaled * scaled, values * SMALL)


def value_of(code):
    return jnp.where(code >= EDGE_CODE, jnp.sqrt(code) * (1.0 / BIG), code * (1.0 / SMALL))


def encode(values):
    return code_of(values).astype(BF16)


def decode(sent):
    return value_of(sent.astype(F32))


def encode_fine(values):
    code = code_of(values)
    first = code.astype(BF16).astype(F32)
    second = (code * (1.0 / GRID)).astype(BF16).astype(F32)
    near = jnp.abs(first - code) <= jnp.abs(second * GRID - code)
    return jnp.where(near, first, -second).astype(BF16)


def decode_fine(sent):
    code = sent.astype(F32)
    return value_of(jnp.where(code < 0.0, code * (-GRID), code))


def in_vmem(array):
    return pltpu.with_memory_space_constraint(array, pltpu.VMEM)


def in_hbm(array):
    return pltpu.with_memory_space_constraint(array, pltpu.HBM)


def call(kernel, name, outs, hbm, vmem, scratch=()):
    single = not isinstance(outs, list)
    shapes = [pltpu.VMEM(shape, kind) for shape, kind in ([outs] if single else outs)]
    result = pl.pallas_call(
        kernel,
        out_shape=shapes,
        in_specs=[HBM] * len(hbm) + [VMEM] * len(vmem),
        out_specs=[VMEM] * len(shapes),
        scratch_shapes=list(scratch),
        compiler_params=pltpu.CompilerParams(vmem_limit_bytes=VMEM_LIMIT),
        cost_estimate=pl.CostEstimate(flops=1, bytes_accessed=1, transcendentals=0),
        name=name,
    )(*[in_hbm(a) for a in hbm], *[in_vmem(a) for a in vmem])
    return result[0] if single else result


def squared_transposed(g):
    g = g.astype(F32)
    return (g * g).T.astype(BF16)


def fisher_block(x, gt_ref):
    return jnp.dot(gt_ref[...], x * x, preferred_element_type=F32)


def where_am_i():
    tok, half, member = lax.axis_index("tok"), lax.axis_index("col"), lax.axis_index("member")
    return tok // 2, tok % 2, half, member // Z, member % Z


def column_block(flip, part):
    x, _, half, _, _ = where_am_i()
    owner = x ^ flip
    local = jnp.where(owner // 2 == half, 2 * (owner % 2), 2 * ((3 - owner) % 2) + 1)
    return 2 * local + part


def load_inputs(member, part, x_ref, x_out, sem):
    wide = x_out.shape[2]
    copies = []
    for s, flip in enumerate(ORDER):
        at = pl.multiple_of(column_block(flip, part) * wide, wide)
        copies.append(pltpu.make_async_copy(x_ref.at[member, :, pl.ds(at, wide)], x_out.at[s], sem.at[s]))
        copies[s].start()
    return copies


def load_grads_kernel(g_ref, g_out, g_own_out, sem):
    core = where_am_i()[1]
    loads = [
        pltpu.make_async_copy(g_ref, g_out.at[:, pl.ds(0, g_ref.shape[1])], sem.at[0]),
        pltpu.make_async_copy(g_ref.at[core], g_own_out, sem.at[1]),
    ]
    for copy in loads:
        copy.start()
    for copy in loads:
        copy.wait()


def load_first_kernel(x_ref, g_ref, after, out, sem, g_sem):
    core = where_am_i()[1]
    wide = x_ref.shape[2] // 8
    copies = [pltpu.make_async_copy(g_ref.at[1 - core], out.at[:, pl.ds(4 * wide, g_ref.shape[2])], g_sem)]
    for s, flip in enumerate(ORDER):
        at = pl.multiple_of(column_block(flip, 0) * wide, wide)
        copies.append(
            pltpu.make_async_copy(x_ref.at[1 - core, :, pl.ds(at, wide)], out.at[:, pl.ds(s * wide, wide)], sem.at[s])
        )
    for copy in copies:
        copy.start()
    for copy in copies:
        copy.wait()


def load_second_kernel(x_ref, after, x_out, sem):
    for copy in load_inputs(1 - where_am_i()[1], 1, x_ref, x_out, sem):
        copy.wait()


def pick_grads_kernel(g_ref, after, kept_out, sent_out):
    core = where_am_i()[1]
    rows = kept_out.shape[0]
    kept_out[...] = g_ref[core, :rows]
    sent_out[...] = g_ref[1 - core, :rows]


def own_tokens(copies, x_out, gt_ref, part_out):
    for s in range(4):
        copies[s].wait()
        part_out[s] = fisher_block(x_out[s], gt_ref)


def own_first_kernel(x_ref, g_ref, after, x_out, gt_out, part_out, sem):
    copies = load_inputs(where_am_i()[1], 0, x_ref, x_out, sem)
    gt_out[...] = squared_transposed(g_ref[...])
    own_tokens(copies, x_out, gt_out, part_out)


def own_second_kernel(x_ref, gt_ref, after, x_out, part_out, sem):
    copies = load_inputs(where_am_i()[1], 1, x_ref, x_out, sem)
    own_tokens(copies, x_out, gt_ref, part_out)


def put(s, block, sent_out, kept_out):
    if s < 2:
        sent_out[s] = encode(block)
    else:
        kept_out[s - 2] = block


def add_first_kernel(x_ref, part_ref, after, sent_out, kept_out, gt_out):
    wide = part_ref.shape[2]
    gt_out[...] = squared_transposed(x_ref[:, 4 * wide :])
    for s in range(4):
        block = fisher_block(x_ref[:, s * wide : (s + 1) * wide], gt_out)
        put(s, part_ref[s] + block, sent_out, kept_out)


def add_second_kernel(x_ref, gt_ref, part_ref, after, sent_out, kept_out):
    for s in range(4):
        put(s, part_ref[s] + fisher_block(x_ref[s], gt_ref), sent_out, kept_out)


def both_first_kernel(xa_ref, xb_ref, ga_ref, gb_ref, after, sent_out, kept_out, gta_out, gtb_out):
    wide = kept_out.shape[2]
    gta_out[...] = squared_transposed(ga_ref[...])
    gtb_out[...] = squared_transposed(gb_ref[...])
    for s in range(4):
        block = fisher_block(xb_ref[:, s * wide : (s + 1) * wide], gtb_out)
        put(s, fisher_block(xa_ref[s], gta_out) + block, sent_out, kept_out)


def both_second_kernel(xa_ref, xb_ref, gta_ref, gtb_ref, after, sent_out, kept_out):
    for s, block in enumerate(BACK):
        put(s, fisher_block(xa_ref[block], gta_ref) + fisher_block(xb_ref[block], gtb_ref), sent_out, kept_out)


def middle_kernel(kept_ref, got_ref, after, sent_out, own_out):
    sent_out[...] = encode_fine(kept_ref[1] + decode(got_ref[1]))
    own_out[...] = kept_ref[0] + decode(got_ref[0])


def settle_kernel(own, got, after, out):
    out[...] = own[...] + decode_fine(got[...])


def join_kernel(first_ref, own, got, after, kept_out, sent_out):
    first = first_ref[...]
    second = own[...] + decode_fine(got[...])
    core = where_am_i()[1]
    kept_out[...] = jnp.where(core == 0, first, second)
    sent_out[...] = encode_fine(jnp.where(core == 0, second, first))


def split_kernel(w_ref, after, own_out, send_out):
    rows, core = own_out.shape[1], where_am_i()[1]
    own_out[...] = w_ref[:, pl.ds(pl.multiple_of(core * rows, rows), rows), :]
    send_out[...] = w_ref[:, pl.ds(pl.multiple_of((1 - core) * rows, rows), rows), :]


def to_words(weighted, total, out):
    high = weighted.astype(BF16)
    out[0] = high
    out[1] = (weighted - high.astype(F32)).astype(BF16)
    out[2] = encode_fine(total)


def from_words(words):
    return words[0].astype(F32) + words[1].astype(F32), decode_fine(words[2])


def weigh_kernel(phase, own, other, w_a, w_b, after, one_out, two_out, three_out, sums_out):
    _, core, half, _, z = where_am_i()
    part = own.shape[1] // Z
    first = (core ^ half ^ phase) == 0
    for d, out in ((2, two_out), (1, one_out), (3, three_out), (0, sums_out)):
        cols = pl.ds(pl.multiple_of((z + d) % Z * part, part), part)
        weighted = total = 0.0
        for values, m in ((own[:, cols], core), (decode_fine(other[:, cols]), 1 - core)):
            fisher = values.T
            weight = jnp.where(first, w_a[m, cols, :].astype(F32), w_b[m, cols, :].astype(F32))
            weighted += fisher * weight
            total += fisher
        if d == 0:
            out[0], out[1] = weighted, total
        else:
            to_words(weighted, total, out)


def over_z(sums, words):
    weighted, total = sums[0], sums[1]
    for ref in words:
        more, added = from_words(ref)
        weighted += more
        total += added
    return weighted, total


def sum_kernel(one, two, three, sums, after, out):
    to_words(*over_z(sums, (one, two, three)), out)


def meet_kernel(near, far, after, out):
    (weighted, total), (more, added) = from_words(near), from_words(far)
    out[0], out[1] = weighted + more, total + added


def merge_kernel(near, far, sums, out):
    (weighted, total), (more, added) = from_words(near), from_words(far)
    out[...] = (weighted + more + sums[0]) / (total + added + sums[1])


def keeper(local, half):
    home = 2 * half + local // 2
    return home if local % 2 == 0 else 3 - home


def kept(x, half):
    return 2 * (x % 2) if x // 2 == half else 2 * ((3 - x) % 2) + 1


def weight_pairs():
    pairs = []
    for tok in range(X * CORES):
        half, local = divmod(tok, 4)
        for col in range(2):
            pairs.append((tok * 2 + col, (keeper(local, half) * 2 + col) * 2 + half))
    return pairs


def result_pairs(phase, sender):
    pairs = []
    for z in range(Z):
        for tok in range(X * CORES):
            x, core = divmod(tok, 2)
            for half in range(2):
                to_tok = 4 * half + kept(x, half)
                to = ((core * Z + z) * 8 + to_tok) * 2 + (half ^ phase)
                pairs.append((((sender * Z + z) * 8 + tok) * 2 + half, to))
    return pairs


def x_pairs(flip):
    return [(t, ((t // 2) ^ flip) * 2 + t % 2) for t in range(X * CORES)]


def z_pairs(distance):
    return [(m, m // Z * Z + (m + distance) % Z) for m in range(2 * Z)]


def shards(inputs, grads, weights):
    tokens, outs = grads.shape[1:]
    wide = inputs.shape[2] // 8
    x_shape, g_shape, gt_shape = ((4, tokens, wide), BF16), ((tokens, outs), BF16), ((outs, tokens), BF16)
    part_shape, sent_shape, kept_shape = ((4, outs, wide), F32), ((2, outs, wide), BF16), ((2, outs, wide), F32)
    code_shape, own_shape = ((outs, wide), BF16), ((outs, wide), F32)
    words, sums = ((3, wide // Z, outs), BF16), ((2, wide // Z, outs), F32)
    dma = pltpu.SemaphoreType.DMA

    def swap_cores(send):
        return lax.ppermute(send, "tok", [(t, t ^ 1) for t in range(8)])

    def swap_cols(send):
        return lax.ppermute(send, "col", [(0, 1), (1, 0)])

    def swap_x(flip, sent):
        return lax.ppermute(sent, "tok", x_pairs(flip))

    def middle(flip, got, kept_blocks, after):
        sent, own = call(middle_kernel, "fisher_over_first_swap", [code_shape, own_shape], [], [kept_blocks, got, after])
        return own, swap_x(flip, sent)

    def settle(one, after):
        return call(settle_kernel, "fisher_over_tokens", own_shape, [], [*one, after])

    def join(first, two, after):
        kept_block, sent = call(join_kernel, "fisher_over_tokens", [own_shape, code_shape], [], [first, *two, after])
        return kept_block, swap_cores(sent)

    def results(phase, sums):
        return [lax.ppermute(sums, ("member", "tok", "col"), result_pairs(phase, y_lo)) for y_lo in range(2)]

    def weigh(phase, own, other, after):
        one, two, three, own_sums = call(
            lambda *refs: weigh_kernel(phase, *refs), "weigh_members", [words] * 3 + [sums], [], [own, other, *moved, after]
        )
        send = ((1, one), (2, two), (3, three))
        return [lax.ppermute(v, "member", z_pairs(d)) for d, v in send] + [own_sums]

    g_pair, g_own = call(
        load_grads_kernel, "load_grads", [((2, tokens + 64, outs), BF16), g_shape], [grads], [], [dma((2,))]
    )
    g_other = swap_cols(g_pair)
    x_send0 = call(
        load_first_kernel, "load_to_swap", ((tokens, 4 * wide + outs), BF16), [inputs, grads], [g_own], [dma((4,)), dma]
    )
    x_got0 = swap_cores(x_send0)
    x_own0, gt_own, part0 = call(
        own_first_kernel, "fisher_of_own_tokens", [x_shape, gt_shape, part_shape], [inputs], [g_own, x_send0], [dma((4,))]
    )
    x_send1 = call(load_second_kernel, "load_to_swap", x_shape, [inputs], [gt_own], [dma((4,))])
    x_got1 = swap_cores(x_send1)
    sent, kept00, gt_got = call(
        add_first_kernel, "fisher_of_both_cores", [sent_shape, kept_shape, gt_shape], [], [x_got0, part0, x_send1]
    )
    swap00 = swap_x(1, sent)
    x_own1, part1 = call(
        own_second_kernel, "fisher_of_own_tokens", [x_shape, part_shape], [inputs], [gt_own, kept00], [dma((4,))]
    )
    sent, kept01 = call(
        add_second_kernel, "fisher_of_both_cores", [sent_shape, kept_shape], [], [x_got1, gt_got, part1, x_own1]
    )
    swap01 = swap_x(1, sent)
    part00 = middle(3, swap00, kept00, kept01)
    part01 = middle(3, swap01, kept01, part00[0])
    settled0 = settle(part00, part01[0])

    arrived = lax.ppermute(weights, ("tok", "col"), weight_pairs())
    rows = weights.shape[1] // 2
    w_own, w_send = call(split_kernel, "split_weights", [((2, rows, outs), BF16)] * 2, [], [arrived, settled0])
    moved = (w_own, swap_cores(w_send))

    g_kept, g_sent = call(pick_grads_kernel, "pick_grads", [g_shape, g_shape], [], [g_other, settled0])
    sent, kept10, gt_own, gt_got = call(
        both_first_kernel, "fisher_of_other_grads", [sent_shape, kept_shape, gt_shape, gt_shape], [],
        [x_own0, x_got0, g_kept, swap_cores(g_sent), w_own],
    )
    swap10 = swap_x(1, sent)
    sent, kept11 = call(
        both_second_kernel, "fisher_of_other_grads", [sent_shape, kept_shape], [],
        [x_own1, x_got1, gt_own, gt_got, kept10],
    )
    swap11 = swap_x(3, sent)
    own0, other0 = join(settled0, part01, kept11)
    words0 = weigh(0, own0, other0, kept11)
    part10 = middle(3, swap10, kept10, words0[3])
    first = call(sum_kernel, "sum_over_z", words, [], [*words0, part10[0]])
    part11 = middle(1, swap11, kept11, first)

    own1, other1 = join(settle(part10, part11[0]), part11, first)
    words1 = weigh(1, own1, other1, own1)
    met = call(meet_kernel, "meet_over_y", sums, [], [*results(0, first), own1])
    second = call(sum_kernel, "sum_over_z", words, [], [*words1, own1])
    near, far = results(1, second)
    return pl.pallas_call(
        merge_kernel,
        out_shape=jax.ShapeDtypeStruct((wide // Z, outs), F32),
        in_specs=[VMEM] * 3,
        out_specs=VMEM,
        compiler_params=pltpu.CompilerParams(vmem_limit_bytes=VMEM_LIMIT),
        name="merge_members",
    )(in_vmem(near), in_vmem(far), in_vmem(met))


def solution(mesh):
    in_specs = (P("member", "tok", "col"), P("member", "tok", "col"), P("member", "tok", "col"))
    out_specs = P(("tok", "member"), "col")
    return jax.shard_map(shards, mesh=mesh, in_specs=in_specs, out_specs=out_specs, check_vma=False)
```

```python
import jax
import jax.numpy as jnp
from jax import lax
from jax.experimental import pallas as pl
from jax.experimental.pallas import tpu as pltpu
from jax.sharding import PartitionSpec as P

F32 = jnp.float32
BF16 = jnp.bfloat16
HBM = pl.BlockSpec(memory_space=pltpu.HBM)
VMEM = pl.BlockSpec(memory_space=pltpu.VMEM)
VMEM_LIMIT = 16 << 20

GRID = 1.00297
BIG = 2.0**28
SMALL = 2.0**16
EDGE = 2.0**-40
EDGE_CODE = 2.0**-24

X, CORES, Z = 4, 2, 4

ORDER = (1, 2, 0, 3)
BACK = (3, 1, 2, 0)


def code_of(values):
    scaled = values * BIG
    return jnp.where(values >= EDGE, scaled * scaled, values * SMALL)


def value_of(code):
    return jnp.where(code >= EDGE_CODE, jnp.sqrt(code) * (1.0 / BIG), code * (1.0 / SMALL))


def encode(values):
    return code_of(values).astype(BF16)


def decode(sent):
    return value_of(sent.astype(F32))


def encode_fine(values):
    code = code_of(values)
    first = code.astype(BF16).astype(F32)
    second = (code * (1.0 / GRID)).astype(BF16).astype(F32)
    near = jnp.abs(first - code) <= jnp.abs(second * GRID - code)
    return jnp.where(near, first, -second).astype(BF16)


def decode_fine(sent):
    code = sent.astype(F32)
    return value_of(jnp.where(code < 0.0, code * (-GRID), code))


def in_vmem(array):
    return pltpu.with_memory_space_constraint(array, pltpu.VMEM)


def in_hbm(array):
    return pltpu.with_memory_space_constraint(array, pltpu.HBM)


def call(kernel, name, outs, hbm, vmem, scratch=()):
    single = not isinstance(outs, list)
    shapes = [pltpu.VMEM(shape, kind) for shape, kind in ([outs] if single else outs)]
    result = pl.pallas_call(
        kernel,
        out_shape=shapes,
        in_specs=[HBM] * len(hbm) + [VMEM] * len(vmem),
        out_specs=[VMEM] * len(shapes),
        scratch_shapes=list(scratch),
        compiler_params=pltpu.CompilerParams(vmem_limit_bytes=VMEM_LIMIT),
        cost_estimate=pl.CostEstimate(flops=1, bytes_accessed=1, transcendentals=0),
        name=name,
    )(*[in_hbm(a) for a in hbm], *[in_vmem(a) for a in vmem])
    return result[0] if single else result


def squared_transposed(g):
    g = g.astype(F32)
    return (g * g).T.astype(BF16)


def fisher_block(x, gt_ref):
    return jnp.dot(gt_ref[...], x * x, preferred_element_type=F32)


def where_am_i():
    tok, half, member = lax.axis_index("tok"), lax.axis_index("col"), lax.axis_index("member")
    return tok // 2, tok % 2, half, member // Z, member % Z


def column_block(flip, part):
    x, _, half, _, _ = where_am_i()
    owner = x ^ flip
    local = jnp.where(owner // 2 == half, 2 * (owner % 2), 2 * ((3 - owner) % 2) + 1)
    return 2 * local + part


def load_inputs(member, part, x_ref, x_out, sem):
    wide = x_out.shape[2]
    copies = []
    for s, flip in enumerate(ORDER):
        at = pl.multiple_of(column_block(flip, part) * wide, wide)
        copies.append(pltpu.make_async_copy(x_ref.at[member, :, pl.ds(at, wide)], x_out.at[s], sem.at[s]))
        copies[s].start()
    return copies


def load_first_kernel(x_ref, g_ref, out, sem, g_sem):
    core = where_am_i()[1]
    wide = x_ref.shape[2] // 8
    copies = [pltpu.make_async_copy(g_ref.at[1 - core], out.at[:, pl.ds(4 * wide, g_ref.shape[2])], g_sem)]
    for s, flip in enumerate(ORDER):
        at = pl.multiple_of(column_block(flip, 0) * wide, wide)
        copies.append(
            pltpu.make_async_copy(x_ref.at[1 - core, :, pl.ds(at, wide)], out.at[:, pl.ds(s * wide, wide)], sem.at[s])
        )
    for copy in copies:
        copy.start()
    for copy in copies:
        copy.wait()


def load_second_kernel(x_ref, after, x_out, sem):
    for copy in load_inputs(1 - where_am_i()[1], 1, x_ref, x_out, sem):
        copy.wait()


def pair_kernel(own, got, after, out):
    outs = own.shape[1]
    out[0], out[1] = own[...], got[:, got.shape[1] - outs :]


def own_tokens(copies, x_out, gt_ref, part_out):
    for s in range(4):
        copies[s].wait()
        part_out[s] = fisher_block(x_out[s], gt_ref)


def own_first_kernel(x_ref, g_ref, after, x_out, g_out, gt_out, part_out, sem, g_sem):
    core = where_am_i()[1]
    load = pltpu.make_async_copy(g_ref.at[core], g_out, g_sem)
    load.start()
    copies = load_inputs(core, 0, x_ref, x_out, sem)
    load.wait()
    gt_out[...] = squared_transposed(g_out[...])
    own_tokens(copies, x_out, gt_out, part_out)


def own_second_kernel(x_ref, gt_ref, after, x_out, part_out, sem):
    copies = load_inputs(where_am_i()[1], 1, x_ref, x_out, sem)
    own_tokens(copies, x_out, gt_ref, part_out)


def put(s, block, sent_out, kept_out):
    if s < 2:
        sent_out[s] = encode(block)
    else:
        kept_out[s - 2] = block


def add_first_kernel(x_ref, part_ref, after, sent_out, kept_out, gt_out):
    wide = part_ref.shape[2]
    gt_out[...] = squared_transposed(x_ref[:, 4 * wide :])
    for s in range(4):
        block = fisher_block(x_ref[:, s * wide : (s + 1) * wide], gt_out)
        put(s, part_ref[s] + block, sent_out, kept_out)


def add_second_kernel(x_ref, gt_ref, part_ref, after, sent_out, kept_out):
    for s in range(4):
        put(s, part_ref[s] + fisher_block(x_ref[s], gt_ref), sent_out, kept_out)


def both_first_kernel(xa_ref, xb_ref, g_ref, after, sent_out, kept_out, gta_out, gtb_out):
    wide = kept_out.shape[2]
    gta_out[...] = squared_transposed(g_ref[0])
    gtb_out[...] = squared_transposed(g_ref[1])
    for s in range(4):
        block = fisher_block(xb_ref[:, s * wide : (s + 1) * wide], gtb_out)
        put(s, fisher_block(xa_ref[s], gta_out) + block, sent_out, kept_out)


def both_second_kernel(xa_ref, xb_ref, gta_ref, gtb_ref, after, sent_out, kept_out):
    for s, block in enumerate(BACK):
        put(s, fisher_block(xa_ref[block], gta_ref) + fisher_block(xb_ref[block], gtb_ref), sent_out, kept_out)


def middle_kernel(kept_ref, got_ref, after, sent_out, own_out):
    sent_out[...] = encode_fine(kept_ref[1] + decode(got_ref[1]))
    own_out[...] = kept_ref[0] + decode(got_ref[0])


def settle_kernel(own, got, after, out):
    out[...] = own[...] + decode_fine(got[...])


def join_kernel(first_ref, own, got, after, kept_out, sent_out):
    first = first_ref[...]
    second = own[...] + decode_fine(got[...])
    core = where_am_i()[1]
    kept_out[...] = jnp.where(core == 0, first, second)
    sent_out[...] = encode_fine(jnp.where(core == 0, second, first))


def split_kernel(w_ref, after, own_out, send_out):
    rows, core = own_out.shape[1], where_am_i()[1]
    own_out[...] = w_ref[:, pl.ds(pl.multiple_of(core * rows, rows), rows), :]
    send_out[...] = w_ref[:, pl.ds(pl.multiple_of((1 - core) * rows, rows), rows), :]


def to_words(weighted, total, out):
    high = weighted.astype(BF16)
    out[0] = high
    out[1] = (weighted - high.astype(F32)).astype(BF16)
    out[2] = encode_fine(total)


def from_words(words):
    return words[0].astype(F32) + words[1].astype(F32), decode_fine(words[2])


def weigh_kernel(phase, own, other, w_own, w_other, after, one_out, two_out, three_out, sums_out):
    _, core, half, _, z = where_am_i()
    part = own.shape[1] // Z
    mine = (core ^ half ^ phase) == 0
    for d, out in ((2, two_out), (1, one_out), (3, three_out), (0, sums_out)):
        cols = pl.ds(pl.multiple_of((z + d) % Z * part, part), part)
        weighted = total = 0.0
        for values, m in ((own[:, cols], core), (decode_fine(other[:, cols]), 1 - core)):
            fisher = values.T
            weight = jnp.where(mine, w_own[m, cols, :].astype(F32), w_other[m, cols, :].astype(F32))
            weighted += fisher * weight
            total += fisher
        if d == 0:
            out[0], out[1] = weighted, total
        else:
            to_words(weighted, total, out)


def over_z(sums, words):
    weighted, total = sums[0], sums[1]
    for ref in words:
        more, added = from_words(ref)
        weighted += more
        total += added
    return weighted, total


def sum_kernel(one, two, three, sums, after, out):
    to_words(*over_z(sums, (one, two, three)), out)


def meet_kernel(near, far, after, out):
    (weighted, total), (more, added) = from_words(near), from_words(far)
    out[0], out[1] = weighted + more, total + added


def merge_kernel(near, far, sums, out):
    (weighted, total), (more, added) = from_words(near), from_words(far)
    out[...] = (weighted + more + sums[0]) / (total + added + sums[1])


def keeper(local, half):
    home = 2 * half + local // 2
    return home if local % 2 == 0 else 3 - home


def kept(x, half):
    return 2 * (x % 2) if x // 2 == half else 2 * ((3 - x) % 2) + 1


def weight_pairs(phase):
    pairs = []
    for tok in range(X * CORES):
        half, local = divmod(tok, 4)
        col = half ^ phase
        pairs.append((tok * 2 + col, (keeper(local, half) * 2 + col) * 2 + half))
    return pairs


def result_pairs(phase, sender):
    pairs = []
    for z in range(Z):
        for tok in range(X * CORES):
            x, core = divmod(tok, 2)
            for half in range(2):
                to_tok = 4 * half + kept(x, half)
                to = ((core * Z + z) * 8 + to_tok) * 2 + (half ^ phase)
                pairs.append((((sender * Z + z) * 8 + tok) * 2 + half, to))
    return pairs


def x_pairs(flip):
    return [(t, ((t // 2) ^ flip) * 2 + t % 2) for t in range(X * CORES)]


def z_pairs(distance):
    return [(m, m // Z * Z + (m + distance) % Z) for m in range(2 * Z)]


def shards(inputs, grads, weights):
    tokens, outs = grads.shape[1:]
    wide = inputs.shape[2] // 8
    x_shape, g_shape, gt_shape = ((4, tokens, wide), BF16), ((tokens, outs), BF16), ((outs, tokens), BF16)
    part_shape, sent_shape, kept_shape = ((4, outs, wide), F32), ((2, outs, wide), BF16), ((2, outs, wide), F32)
    code_shape, own_shape = ((outs, wide), BF16), ((outs, wide), F32)
    words, sums = ((3, wide // Z, outs), BF16), ((2, wide // Z, outs), F32)
    dma = pltpu.SemaphoreType.DMA

    def swap_cores(send):
        return lax.ppermute(send, "tok", [(t, t ^ 1) for t in range(8)])

    def swap_cols(send):
        return lax.ppermute(send, "col", [(0, 1), (1, 0)])

    def swap_x(flip, sent):
        return lax.ppermute(sent, "tok", x_pairs(flip))

    def middle(flip, got, kept_blocks, after):
        sent, own = call(middle_kernel, "fisher_over_first_swap", [code_shape, own_shape], [], [kept_blocks, got, after])
        return own, swap_x(flip, sent)

    def settle(one, after):
        return call(settle_kernel, "fisher_over_tokens", own_shape, [], [*one, after])

    def join(first, two, after):
        kept_block, sent = call(join_kernel, "fisher_over_tokens", [own_shape, code_shape], [], [first, *two, after])
        return kept_block, swap_cores(sent)

    def results(phase, sums):
        return [lax.ppermute(sums, ("member", "tok", "col"), result_pairs(phase, y_lo)) for y_lo in range(2)]

    def bring_weights(phase, after):
        arrived = lax.ppermute(weights, ("tok", "col"), weight_pairs(phase))
        half_shape = ((2, weights.shape[1] // 2, outs), BF16)
        own, send = call(split_kernel, "split_weights", [half_shape, half_shape], [], [arrived, after])
        return own, swap_cores(send)

    def weigh(phase, own, other, moved, after):
        one, two, three, own_sums = call(
            lambda *refs: weigh_kernel(phase, *refs), "weigh_members", [words] * 3 + [sums], [], [own, other, *moved, after]
        )
        send = ((1, one), (2, two), (3, three))
        return [lax.ppermute(v, "member", z_pairs(d)) for d, v in send] + [own_sums]

    x_send0 = call(
        load_first_kernel, "load_to_swap", ((tokens, 4 * wide + outs), BF16), [inputs, grads], [], [dma((4,)), dma]
    )
    x_got0 = swap_cores(x_send0)
    x_own0, g_own, gt_own, part0 = call(
        own_first_kernel, "fisher_of_own_tokens", [x_shape, g_shape, gt_shape, part_shape], [inputs, grads], [x_send0],
        [dma((4,)), dma],
    )
    x_send1 = call(load_second_kernel, "load_to_swap", x_shape, [inputs], [gt_own], [dma((4,))])
    x_got1 = swap_cores(x_send1)
    g_pair = call(pair_kernel, "pair_grads", ((2, tokens, outs), BF16), [], [g_own, x_got0, x_send1])
    g_other = swap_cols(g_pair)
    sent, kept00, gt_got = call(
        add_first_kernel, "fisher_of_both_cores", [sent_shape, kept_shape, gt_shape], [], [x_got0, part0, g_pair]
    )
    swap00 = swap_x(1, sent)
    x_own1, part1 = call(
        own_second_kernel, "fisher_of_own_tokens", [x_shape, part_shape], [inputs], [gt_own, kept00], [dma((4,))]
    )
    sent, kept01 = call(
        add_second_kernel, "fisher_of_both_cores", [sent_shape, kept_shape], [], [x_got1, gt_got, part1, x_own1]
    )
    swap01 = swap_x(1, sent)
    part00 = middle(3, swap00, kept00, kept01)
    w0 = bring_weights(0, part00[0])

    sent, kept10, gt_own, gt_got = call(
        both_first_kernel, "fisher_of_other_grads", [sent_shape, kept_shape, gt_shape, gt_shape], [],
        [x_own0, x_got0, g_other, w0[0]],
    )
    swap10 = swap_x(1, sent)
    part01 = middle(3, swap01, kept01, kept10)
    sent, kept11 = call(
        both_second_kernel, "fisher_of_other_grads", [sent_shape, kept_shape], [],
        [x_own1, x_got1, gt_own, gt_got, part01[0]],
    )
    swap11 = swap_x(3, sent)

    settled0 = settle(part00, kept11)
    own0, other0 = join(settled0, part01, kept11)
    words0 = weigh(0, own0, other0, w0, own0)
    part10 = middle(3, swap10, kept10, words0[3])
    first = call(sum_kernel, "sum_over_z", words, [], [*words0, part10[0]])
    part11 = middle(1, swap11, kept11, first)
    own1, other1 = join(settle(part10, part11[0]), part11, first)
    w1 = bring_weights(1, own1)
    words1 = weigh(1, own1, other1, w1, w1[0])
    met = call(meet_kernel, "meet_over_y", sums, [], [*results(0, first), own1])
    second = call(sum_kernel, "sum_over_z", words, [], [*words1, own1])
    near, far = results(1, second)
    return pl.pallas_call(
        merge_kernel,
        out_shape=jax.ShapeDtypeStruct((wide // Z, outs), F32),
        in_specs=[VMEM] * 3,
        out_specs=VMEM,
        compiler_params=pltpu.CompilerParams(vmem_limit_bytes=VMEM_LIMIT),
        name="merge_members",
    )(in_vmem(near), in_vmem(far), in_vmem(met))


def solution(mesh):
    in_specs = (P("member", "tok", "col"), P("member", "tok", "col"), P("member", "tok", "col"))
    out_specs = P(("tok", "member"), "col")
    return jax.shard_map(shards, mesh=mesh, in_specs=in_specs, out_specs=out_specs, check_vma=False)
```

```python
import jax
import jax.numpy as jnp
from jax import lax
from jax.experimental import pallas as pl
from jax.experimental.pallas import tpu as pltpu
from jax.sharding import PartitionSpec as P

F32 = jnp.float32
BF16 = jnp.bfloat16
HBM = pl.BlockSpec(memory_space=pltpu.HBM)
VMEM = pl.BlockSpec(memory_space=pltpu.VMEM)
VMEM_LIMIT = 16 << 20

GRID = 1.00297
BIG = 2.0**28
SMALL = 2.0**16
EDGE = 2.0**-40
EDGE_CODE = 2.0**-24

X, CORES, Z = 4, 2, 4

ORDER = ((2, 1), (3, 0))


def code_of(values):
    scaled = values * BIG
    return jnp.where(values >= EDGE, scaled * scaled, values * SMALL)


def value_of(code):
    return jnp.where(code >= EDGE_CODE, jnp.sqrt(code) * (1.0 / BIG), code * (1.0 / SMALL))


def encode(values):
    return code_of(values).astype(BF16)


def decode(sent):
    return value_of(sent.astype(F32))


def encode_fine(values):
    code = code_of(values)
    first = code.astype(BF16).astype(F32)
    second = (code * (1.0 / GRID)).astype(BF16).astype(F32)
    near = jnp.abs(first - code) <= jnp.abs(second * GRID - code)
    return jnp.where(near, first, -second).astype(BF16)


def decode_fine(sent):
    code = sent.astype(F32)
    return value_of(jnp.where(code < 0.0, code * (-GRID), code))


def in_vmem(array):
    return pltpu.with_memory_space_constraint(array, pltpu.VMEM)


def in_hbm(array):
    return pltpu.with_memory_space_constraint(array, pltpu.HBM)


def call(kernel, name, outs, hbm, vmem, scratch=()):
    single = not isinstance(outs, list)
    shapes = [pltpu.VMEM(shape, kind) for shape, kind in ([outs] if single else outs)]
    result = pl.pallas_call(
        kernel,
        out_shape=shapes,
        in_specs=[HBM] * len(hbm) + [VMEM] * len(vmem),
        out_specs=[VMEM] * len(shapes),
        scratch_shapes=list(scratch),
        compiler_params=pltpu.CompilerParams(vmem_limit_bytes=VMEM_LIMIT),
        cost_estimate=pl.CostEstimate(flops=1, bytes_accessed=1, transcendentals=0),
        name=name,
    )(*[in_hbm(a) for a in hbm], *[in_vmem(a) for a in vmem])
    return result[0] if single else result


def squared_transposed(g):
    g = g.astype(F32)
    return (g * g).T.astype(BF16)


def fisher_block(x, gt_ref):
    return jnp.dot(gt_ref[...], x * x, preferred_element_type=F32)


def where_am_i():
    tok, half, member = lax.axis_index("tok"), lax.axis_index("col"), lax.axis_index("member")
    return tok // 2, tok % 2, half, member // Z, member % Z


def load_inputs(member, pair, x_ref, x_out, sem):
    x, _, half, _, _ = where_am_i()
    wide = x_ref.shape[2] // 4
    copies = []
    for s, distance in enumerate(ORDER[pair]):
        owner = (x + distance) % X
        local = jnp.where(owner // 2 == half, 2 * (owner % 2), 2 * ((3 - owner) % 2) + 1)
        at = pl.multiple_of(local * wide, wide)
        source = x_ref.at[member, :, pl.ds(at, wide)]
        copies.append(pltpu.make_async_copy(source, x_out.at[:, pl.ds(s * wide, wide)], sem.at[s]))
        copies[s].start()
    return copies


def load_first_kernel(x_ref, g_ref, out, sem, g_sem):
    core = where_am_i()[1]
    outs = g_ref.shape[2]
    load = pltpu.make_async_copy(g_ref.at[1 - core], out.at[:, pl.ds(out.shape[1] - outs, outs)], g_sem)
    load.start()
    for copy in load_inputs(1 - core, 0, x_ref, out, sem) + [load]:
        copy.wait()


def load_second_kernel(x_ref, after, x_out, sem):
    for copy in load_inputs(1 - where_am_i()[1], 1, x_ref, x_out, sem):
        copy.wait()


def pair_kernel(own, got, after, out):
    outs = own.shape[1]
    out[0], out[1] = own[...], got[:, got.shape[1] - outs :]


def columns(s, x_ref, wide):
    return x_ref[:, s * wide : (s + 1) * wide]


def own_tokens(copies, x_out, gt_ref, part_out):
    for s in range(2):
        copies[s].wait()
        part_out[s] = fisher_block(columns(s, x_out, part_out.shape[2]), gt_ref)


def own_first_kernel(x_ref, g_ref, after, x_out, g_out, gt_out, part_out, sem, g_sem):
    core = where_am_i()[1]
    load = pltpu.make_async_copy(g_ref.at[core], g_out, g_sem)
    load.start()
    copies = load_inputs(core, 0, x_ref, x_out, sem)
    load.wait()
    gt_out[...] = squared_transposed(g_out[...])
    own_tokens(copies, x_out, gt_out, part_out)


def own_second_kernel(x_ref, gt_ref, after, x_out, part_out, sem):
    copies = load_inputs(where_am_i()[1], 1, x_ref, x_out, sem)
    own_tokens(copies, x_out, gt_ref, part_out)


def add_first_kernel(x_ref, part_ref, after, two_out, one_out, gt_out):
    wide, outs = part_ref.shape[2], part_ref.shape[1]
    gt_out[...] = squared_transposed(x_ref[:, 2 * wide :])
    for s, out in enumerate((two_out, one_out)):
        out[...] = encode(part_ref[s] + fisher_block(columns(s, x_ref, wide), gt_out))


def add_second_kernel(x_ref, gt_ref, part_ref, after, three_out, own_out):
    wide = part_ref.shape[2]
    three_out[...] = encode(part_ref[0] + fisher_block(columns(0, x_ref, wide), gt_ref))
    own_out[...] = part_ref[1] + fisher_block(columns(1, x_ref, wide), gt_ref)


def both(s, xa_ref, xb_ref, gta_ref, gtb_ref, wide):
    return fisher_block(columns(s, xa_ref, wide), gta_ref) + fisher_block(columns(s, xb_ref, wide), gtb_ref)


def both_first_kernel(xa_ref, xb_ref, g_ref, after, two_out, one_out, gta_out, gtb_out):
    gta_out[...] = squared_transposed(g_ref[0])
    gtb_out[...] = squared_transposed(g_ref[1])
    for s, out in enumerate((two_out, one_out)):
        out[...] = encode(both(s, xa_ref, xb_ref, gta_out, gtb_out, out.shape[1]))


def both_second_kernel(xa_ref, xb_ref, gta_ref, gtb_ref, after, three_out, own_out):
    wide = own_out.shape[1]
    three_out[...] = encode(both(0, xa_ref, xb_ref, gta_ref, gtb_ref, wide))
    own_out[...] = both(1, xa_ref, xb_ref, gta_ref, gtb_ref, wide)


def join_kernel(own, one, two, three, after, kept_out, sent_out):
    wide = kept_out.shape[1]
    halves = []
    for s in range(2):
        got = [decode(columns(s, ref, wide)) for ref in (one, two, three)]
        halves.append(columns(s, own, wide) + got[0] + got[1] + got[2])
    core = where_am_i()[1]
    kept_out[...] = jnp.where(core == 0, halves[0], halves[1])
    sent_out[...] = encode_fine(jnp.where(core == 0, halves[1], halves[0]))


def split_kernel(w_ref, after, own_out, send_out):
    rows, core = own_out.shape[1], where_am_i()[1]
    own_out[...] = w_ref[:, pl.ds(pl.multiple_of(core * rows, rows), rows), :]
    send_out[...] = w_ref[:, pl.ds(pl.multiple_of((1 - core) * rows, rows), rows), :]


def to_words(weighted, total, out):
    high = weighted.astype(BF16)
    out[0] = high
    out[1] = (weighted - high.astype(F32)).astype(BF16)
    out[2] = encode_fine(total)


def from_words(words):
    return words[0].astype(F32) + words[1].astype(F32), decode_fine(words[2])


def weigh_kernel(phase, own, other, w_own, w_other, after, one_out, two_out, three_out, sums_out):
    _, core, half, _, z = where_am_i()
    part = own.shape[1] // Z
    mine = (core ^ half ^ phase) == 0
    for d, out in ((2, two_out), (1, one_out), (3, three_out), (0, sums_out)):
        cols = pl.ds(pl.multiple_of((z + d) % Z * part, part), part)
        weighted = total = 0.0
        for values, m in ((own[:, cols], core), (decode_fine(other[:, cols]), 1 - core)):
            fisher = values.T
            weight = jnp.where(mine, w_own[m, cols, :].astype(F32), w_other[m, cols, :].astype(F32))
            weighted += fisher * weight
            total += fisher
        if d == 0:
            out[0], out[1] = weighted, total
        else:
            to_words(weighted, total, out)


def weigh_all_kernel(phase, own, other, w_own, w_other, after, out):
    _, core, half, _, _ = where_am_i()
    part = own.shape[1] // Z
    mine = (core ^ half ^ phase) == 0
    for z in range(Z):
        cols = slice(z * part, (z + 1) * part)
        weighted = total = 0.0
        for values, m in ((own[:, cols], core), (decode_fine(other[:, cols]), 1 - core)):
            fisher = values.T
            weight = jnp.where(mine, w_own[m, cols, :].astype(F32), w_other[m, cols, :].astype(F32))
            weighted += fisher * weight
            total += fisher
        to_words(weighted, total, out.at[z])


def sum_all_kernel(got, after, out):
    weighted = total = 0.0
    for z in range(Z):
        more, added = from_words(got.at[z])
        weighted += more
        total += added
    to_words(weighted, total, out)


def over_z(sums, words):
    weighted, total = sums[0], sums[1]
    for ref in words:
        more, added = from_words(ref)
        weighted += more
        total += added
    return weighted, total


def sum_kernel(one, two, three, sums, after, out):
    to_words(*over_z(sums, (one, two, three)), out)


def meet_kernel(near, far, after, out):
    (weighted, total), (more, added) = from_words(near), from_words(far)
    out[0], out[1] = weighted + more, total + added


def merge_kernel(near, far, sums, out):
    (weighted, total), (more, added) = from_words(near), from_words(far)
    out[...] = (weighted + more + sums[0]) / (total + added + sums[1])


def keeper(local, half):
    home = 2 * half + local // 2
    return home if local % 2 == 0 else 3 - home


def kept(x, half):
    return 2 * (x % 2) if x // 2 == half else 2 * ((3 - x) % 2) + 1


def weight_pairs(phase):
    pairs = []
    for tok in range(X * CORES):
        half, local = divmod(tok, 4)
        col = half ^ phase
        pairs.append((tok * 2 + col, (keeper(local, half) * 2 + col) * 2 + half))
    return pairs


def result_pairs(phase, sender):
    pairs = []
    for z in range(Z):
        for tok in range(X * CORES):
            x, core = divmod(tok, 2)
            for half in range(2):
                to_tok = 4 * half + kept(x, half)
                to = ((core * Z + z) * 8 + to_tok) * 2 + (half ^ phase)
                pairs.append((((sender * Z + z) * 8 + tok) * 2 + half, to))
    return pairs


def x_pairs(distance):
    return [(t, ((t // 2 + distance) % X) * 2 + t % 2) for t in range(X * CORES)]


def z_pairs(distance):
    return [(m, m // Z * Z + (m + distance) % Z) for m in range(2 * Z)]


def shards(inputs, grads, weights):
    tokens, outs = grads.shape[1:]
    wide = inputs.shape[2] // 8
    x_shape, g_shape, gt_shape = ((tokens, 4 * wide), BF16), ((tokens, outs), BF16), ((outs, tokens), BF16)
    part_shape, sent_shape, sum_shape = ((2, outs, 2 * wide), F32), ((outs, 2 * wide), BF16), ((outs, 2 * wide), F32)
    code_shape, own_shape = ((outs, wide), BF16), ((outs, wide), F32)
    words, sums = ((3, wide // Z, outs), BF16), ((2, wide // Z, outs), F32)
    dma = pltpu.SemaphoreType.DMA

    def swap_cores(send):
        return lax.ppermute(send, "tok", [(t, t ^ 1) for t in range(8)])

    def swap_cols(send):
        return lax.ppermute(send, "col", [(0, 1), (1, 0)])

    def send_x(distance, sent):
        return lax.ppermute(sent, "tok", x_pairs(distance))

    def join(own, got, after):
        kept_block, sent = call(
            join_kernel, "fisher_over_tokens", [own_shape, code_shape], [], [own, got[1], got[2], got[3], after]
        )
        return kept_block, swap_cores(sent)

    def results(phase, sums):
        return [lax.ppermute(sums, ("member", "tok", "col"), result_pairs(phase, y_lo)) for y_lo in range(2)]

    def bring_weights(phase, after):
        arrived = lax.ppermute(weights, ("tok", "col"), weight_pairs(phase))
        half_shape = ((2, weights.shape[1] // 2, outs), BF16)
        own, send = call(split_kernel, "split_weights", [half_shape, half_shape], [], [arrived, after])
        return own, swap_cores(send)

    def weigh(phase, own, other, moved, after):
        one, two, three, own_sums = call(
            lambda *refs: weigh_kernel(phase, *refs), "weigh_members", [words] * 3 + [sums], [], [own, other, *moved, after]
        )
        send = ((1, one), (2, two), (3, three))
        return [lax.ppermute(v, "member", z_pairs(d)) for d, v in send] + [own_sums]

    x_send0 = call(
        load_first_kernel, "load_to_swap", ((tokens, 4 * wide + outs), BF16), [inputs, grads], [], [dma((2,)), dma]
    )
    x_got0 = swap_cores(x_send0)
    x_own0, g_own, gt_own, part0 = call(
        own_first_kernel, "fisher_of_own_tokens", [x_shape, g_shape, gt_shape, part_shape], [inputs, grads], [x_send0],
        [dma((2,)), dma],
    )
    x_send1 = call(load_second_kernel, "load_to_swap", x_shape, [inputs], [gt_own], [dma((2,))])
    x_got1 = swap_cores(x_send1)
    g_pair = call(pair_kernel, "pair_grads", ((2, tokens, outs), BF16), [], [g_own, x_got0, x_send1])
    g_other = swap_cols(g_pair)
    two, one, gt_got = call(
        add_first_kernel, "fisher_of_both_cores", [sent_shape, sent_shape, gt_shape], [], [x_got0, part0, g_pair]
    )
    got0 = {2: send_x(2, two), 1: send_x(1, one)}
    x_own1, part1 = call(
        own_second_kernel, "fisher_of_own_tokens", [x_shape, part_shape], [inputs], [gt_own, two], [dma((2,))]
    )
    three, sum0 = call(
        add_second_kernel, "fisher_of_both_cores", [sent_shape, sum_shape], [], [x_got1, gt_got, part1, x_own1]
    )
    got0[3] = send_x(3, three)
    w0 = bring_weights(0, three)

    two, one, gt_own, gt_got = call(
        both_first_kernel, "fisher_of_other_grads", [sent_shape, sent_shape, gt_shape, gt_shape], [],
        [x_own0, x_got0, g_other, w0[0]],
    )
    got1 = {2: send_x(2, two), 1: send_x(1, one)}
    three, sum1 = call(
        both_second_kernel, "fisher_of_other_grads", [sent_shape, sum_shape], [], [x_own1, x_got1, gt_own, gt_got, two]
    )
    got1[3] = send_x(3, three)

    own0, other0 = join(sum0, got0, three)
    words0 = call(
        lambda *refs: weigh_all_kernel(0, *refs), "weigh_members", ((Z, 3, wide // Z, outs), BF16), [],
        [own0, other0, *w0, own0],
    )
    groups = [[y * Z + z for z in range(Z)] for y in range(2)]
    words0 = lax.all_to_all(words0, "member", 0, 0, axis_index_groups=groups, tiled=True)
    first = call(sum_all_kernel, "sum_over_z", words, [], [words0, own0])
    own1, other1 = join(sum1, got1, first)
    w1 = bring_weights(1, own1)
    words1 = weigh(1, own1, other1, w1, w1[0])
    met = call(meet_kernel, "meet_over_y", sums, [], [*results(0, first), own1])
    second = call(sum_kernel, "sum_over_z", words, [], [*words1, own1])
    near, far = results(1, second)
    return pl.pallas_call(
        merge_kernel,
        out_shape=jax.ShapeDtypeStruct((wide // Z, outs), F32),
        in_specs=[VMEM] * 3,
        out_specs=VMEM,
        compiler_params=pltpu.CompilerParams(vmem_limit_bytes=VMEM_LIMIT),
        name="merge_members",
    )(in_vmem(near), in_vmem(far), in_vmem(met))


def solution(mesh):
    in_specs = (P("member", "tok", "col"), P("member", "tok", "col"), P("member", "tok", "col"))
    out_specs = P(("tok", "member"), "col")
    return jax.shard_map(shards, mesh=mesh, in_specs=in_specs, out_specs=out_specs, check_vma=False)
```

```python
import jax
import jax.numpy as jnp
from jax import lax
from jax.experimental import pallas as pl
from jax.experimental.pallas import tpu as pltpu
from jax.sharding import PartitionSpec as P

F32 = jnp.float32
BF16 = jnp.bfloat16
HBM = pl.BlockSpec(memory_space=pltpu.HBM)
VMEM = pl.BlockSpec(memory_space=pltpu.VMEM)
VMEM_LIMIT = 16 << 20

GRID = 1.00297
BIG = 2.0**28
SMALL = 2.0**16
EDGE = 2.0**-40
EDGE_CODE = 2.0**-24

X, CORES, Z = 4, 2, 4

ORDER = (1, 2, 0, 3)
BACK = (3, 1, 2, 0)


def code_of(values):
    scaled = values * BIG
    return jnp.where(values >= EDGE, scaled * scaled, values * SMALL)


def value_of(code):
    return jnp.where(code >= EDGE_CODE, jnp.sqrt(code) * (1.0 / BIG), code * (1.0 / SMALL))


def encode(values):
    return code_of(values).astype(BF16)


def decode(sent):
    return value_of(sent.astype(F32))


def encode_fine(values):
    code = code_of(values)
    first = code.astype(BF16).astype(F32)
    second = (code * (1.0 / GRID)).astype(BF16).astype(F32)
    near = jnp.abs(first - code) <= jnp.abs(second * GRID - code)
    return jnp.where(near, first, -second).astype(BF16)


def decode_fine(sent):
    code = sent.astype(F32)
    return value_of(jnp.where(code < 0.0, code * (-GRID), code))


def in_vmem(array):
    return pltpu.with_memory_space_constraint(array, pltpu.VMEM)


def in_hbm(array):
    return pltpu.with_memory_space_constraint(array, pltpu.HBM)


def call(kernel, name, outs, hbm, vmem, scratch=()):
    single = not isinstance(outs, list)
    shapes = [pltpu.VMEM(shape, kind) for shape, kind in ([outs] if single else outs)]
    result = pl.pallas_call(
        kernel,
        out_shape=shapes,
        in_specs=[HBM] * len(hbm) + [VMEM] * len(vmem),
        out_specs=[VMEM] * len(shapes),
        scratch_shapes=list(scratch),
        compiler_params=pltpu.CompilerParams(vmem_limit_bytes=VMEM_LIMIT),
        cost_estimate=pl.CostEstimate(flops=1, bytes_accessed=1, transcendentals=0),
        name=name,
    )(*[in_hbm(a) for a in hbm], *[in_vmem(a) for a in vmem])
    return result[0] if single else result


def squared_transposed(g):
    g = g.astype(F32)
    return (g * g).T.astype(BF16)


def fisher_block(x, gt_ref):
    return jnp.dot(gt_ref[...], x * x, preferred_element_type=F32)


def where_am_i():
    tok, half, member = lax.axis_index("tok"), lax.axis_index("col"), lax.axis_index("member")
    return tok // 2, tok % 2, half, member // Z, member % Z


def column_block(flip, part):
    x, _, half, _, _ = where_am_i()
    owner = x ^ flip
    local = jnp.where(owner // 2 == half, 2 * (owner % 2), 2 * ((3 - owner) % 2) + 1)
    return 2 * local + part


def load_inputs(member, part, x_ref, x_out, sem):
    wide = x_out.shape[2]
    copies = []
    for s, flip in enumerate(ORDER):
        at = pl.multiple_of(column_block(flip, part) * wide, wide)
        copies.append(pltpu.make_async_copy(x_ref.at[member, :, pl.ds(at, wide)], x_out.at[s], sem.at[s]))
        copies[s].start()
    return copies


def load_first_kernel(x_ref, g_ref, out, sem, g_sem):
    core = where_am_i()[1]
    wide = x_ref.shape[2] // 8
    copies = [pltpu.make_async_copy(g_ref.at[1 - core], out.at[:, pl.ds(4 * wide, g_ref.shape[2])], g_sem)]
    for s, flip in enumerate(ORDER):
        at = pl.multiple_of(column_block(flip, 0) * wide, wide)
        copies.append(
            pltpu.make_async_copy(x_ref.at[1 - core, :, pl.ds(at, wide)], out.at[:, pl.ds(s * wide, wide)], sem.at[s])
        )
    for copy in copies:
        copy.start()
    for copy in copies:
        copy.wait()


def load_second_kernel(x_ref, after, x_out, sem):
    for copy in load_inputs(1 - where_am_i()[1], 1, x_ref, x_out, sem):
        copy.wait()


def pair_kernel(own, got, after, out):
    outs = own.shape[1]
    out[0], out[1] = own[...], got[:, got.shape[1] - outs :]


def own_tokens(copies, x_out, gt_ref, part_out):
    for s in range(4):
        copies[s].wait()
        part_out[s] = fisher_block(x_out[s], gt_ref)


def own_first_kernel(x_ref, g_ref, after, x_out, g_out, gt_out, part_out, sem, g_sem):
    core = where_am_i()[1]
    load = pltpu.make_async_copy(g_ref.at[core], g_out, g_sem)
    load.start()
    copies = load_inputs(core, 0, x_ref, x_out, sem)
    load.wait()
    gt_out[...] = squared_transposed(g_out[...])
    own_tokens(copies, x_out, gt_out, part_out)


def own_second_kernel(x_ref, gt_ref, after, x_out, part_out, sem):
    copies = load_inputs(where_am_i()[1], 1, x_ref, x_out, sem)
    own_tokens(copies, x_out, gt_ref, part_out)


def put(s, block, sent_out, kept_out):
    if s < 2:
        sent_out[s] = encode(block)
    else:
        kept_out[s - 2] = block


def add_first_kernel(x_ref, part_ref, after, sent_out, kept_out, gt_out):
    wide = part_ref.shape[2]
    gt_out[...] = squared_transposed(x_ref[:, 4 * wide :])
    for s in range(4):
        block = fisher_block(x_ref[:, s * wide : (s + 1) * wide], gt_out)
        put(s, part_ref[s] + block, sent_out, kept_out)


def add_second_kernel(x_ref, gt_ref, part_ref, after, sent_out, kept_out):
    for s in range(4):
        put(s, part_ref[s] + fisher_block(x_ref[s], gt_ref), sent_out, kept_out)


def both_first_kernel(xa_ref, xb_ref, g_ref, after, sent_out, kept_out, gta_out, gtb_out):
    wide = kept_out.shape[2]
    gta_out[...] = squared_transposed(g_ref[0])
    gtb_out[...] = squared_transposed(g_ref[1])
    for s in range(4):
        block = fisher_block(xb_ref[:, s * wide : (s + 1) * wide], gtb_out)
        put(s, fisher_block(xa_ref[s], gta_out) + block, sent_out, kept_out)


def both_second_kernel(xa_ref, xb_ref, gta_ref, gtb_ref, after, sent_out, kept_out):
    for s, block in enumerate(BACK):
        put(s, fisher_block(xa_ref[block], gta_ref) + fisher_block(xb_ref[block], gtb_ref), sent_out, kept_out)


def middle_kernel(kept_ref, got_ref, after, sent_out, own_out):
    sent_out[...] = encode_fine(kept_ref[1] + decode(got_ref[1]))
    own_out[...] = kept_ref[0] + decode(got_ref[0])


def settle_kernel(own, got, after, out):
    out[...] = own[...] + decode_fine(got[...])


def join_kernel(first_ref, own, got, after, kept_out, sent_out):
    first = first_ref[...]
    second = own[...] + decode_fine(got[...])
    core = where_am_i()[1]
    kept_out[...] = jnp.where(core == 0, first, second)
    sent_out[...] = encode_fine(jnp.where(core == 0, second, first))


def split_kernel(w_ref, after, own_out, send_out):
    rows, core = own_out.shape[1], where_am_i()[1]
    own_out[...] = w_ref[:, pl.ds(pl.multiple_of(core * rows, rows), rows), :]
    send_out[...] = w_ref[:, pl.ds(pl.multiple_of((1 - core) * rows, rows), rows), :]


def to_words(weighted, total, out):
    high = weighted.astype(BF16)
    out[0] = high
    out[1] = (weighted - high.astype(F32)).astype(BF16)
    out[2] = encode_fine(total)


def from_words(words):
    return words[0].astype(F32) + words[1].astype(F32), decode_fine(words[2])


def weigh_kernel(phase, own, other, w_own, w_other, after, one_out, two_out, three_out, sums_out):
    _, core, half, _, z = where_am_i()
    part = own.shape[1] // Z
    mine = (core ^ half ^ phase) == 0
    for d, out in ((2, two_out), (1, one_out), (3, three_out), (0, sums_out)):
        cols = pl.ds(pl.multiple_of((z + d) % Z * part, part), part)
        weighted = total = 0.0
        for values, m in ((own[:, cols], core), (decode_fine(other[:, cols]), 1 - core)):
            fisher = values.T
            weight = jnp.where(mine, w_own[m, cols, :].astype(F32), w_other[m, cols, :].astype(F32))
            weighted += fisher * weight
            total += fisher
        if d == 0:
            out[0], out[1] = weighted, total
        else:
            to_words(weighted, total, out)


def over_z(sums, words):
    weighted, total = sums[0], sums[1]
    for ref in words:
        more, added = from_words(ref)
        weighted += more
        total += added
    return weighted, total


def sum_kernel(one, two, three, sums, after, out):
    to_words(*over_z(sums, (one, two, three)), out)


def meet_kernel(near, far, after, out):
    (weighted, total), (more, added) = from_words(near), from_words(far)
    out[0], out[1] = weighted + more, total + added


def merge_kernel(near, far, sums, out):
    (weighted, total), (more, added) = from_words(near), from_words(far)
    out[...] = (weighted + more + sums[0]) / (total + added + sums[1])


def keeper(local, half):
    home = 2 * half + local // 2
    return home if local % 2 == 0 else 3 - home


def kept(x, half):
    return 2 * (x % 2) if x // 2 == half else 2 * ((3 - x) % 2) + 1


def weight_pairs():
    pairs = []
    for tok in range(X * CORES):
        half, local = divmod(tok, 4)
        for col in range(2):
            pairs.append((tok * 2 + col, (keeper(local, half) * 2 + col) * 2 + half))
    return pairs


def result_pairs(phase, sender):
    pairs = []
    for z in range(Z):
        for tok in range(X * CORES):
            x, core = divmod(tok, 2)
            for half in range(2):
                to_tok = 4 * half + kept(x, half)
                to = ((core * Z + z) * 8 + to_tok) * 2 + (half ^ phase)
                pairs.append((((sender * Z + z) * 8 + tok) * 2 + half, to))
    return pairs


def x_pairs(flip):
    return [(t, ((t // 2) ^ flip) * 2 + t % 2) for t in range(X * CORES)]


def z_pairs(distance):
    return [(m, m // Z * Z + (m + distance) % Z) for m in range(2 * Z)]


def shards(inputs, grads, weights):
    tokens, outs = grads.shape[1:]
    wide = inputs.shape[2] // 8
    x_shape, g_shape, gt_shape = ((4, tokens, wide), BF16), ((tokens, outs), BF16), ((outs, tokens), BF16)
    part_shape, sent_shape, kept_shape = ((4, outs, wide), F32), ((2, outs, wide), BF16), ((2, outs, wide), F32)
    code_shape, own_shape = ((outs, wide), BF16), ((outs, wide), F32)
    words, sums = ((3, wide // Z, outs), BF16), ((2, wide // Z, outs), F32)
    dma = pltpu.SemaphoreType.DMA

    def swap_cores(send):
        return lax.ppermute(send, "tok", [(t, t ^ 1) for t in range(8)])

    def swap_cols(send):
        return lax.ppermute(send, "col", [(0, 1), (1, 0)])

    def swap_x(flip, sent):
        return lax.ppermute(sent, "tok", x_pairs(flip))

    def middle(flip, got, kept_blocks, after):
        sent, own = call(middle_kernel, "fisher_over_first_swap", [code_shape, own_shape], [], [kept_blocks, got, after])
        return own, swap_x(flip, sent)

    def settle(one, after):
        return call(settle_kernel, "fisher_over_tokens", own_shape, [], [*one, after])

    def join(first, two, after):
        kept_block, sent = call(join_kernel, "fisher_over_tokens", [own_shape, code_shape], [], [first, *two, after])
        return kept_block, swap_cores(sent)

    def results(phase, sums):
        return [lax.ppermute(sums, ("member", "tok", "col"), result_pairs(phase, y_lo)) for y_lo in range(2)]

    def bring_weights(after):
        arrived = lax.ppermute(weights, ("tok", "col"), weight_pairs())
        half_shape = ((2, weights.shape[1] // 2, outs), BF16)
        own, send = call(split_kernel, "split_weights", [half_shape, half_shape], [], [arrived, after])
        return own, swap_cores(send)

    def weigh(phase, own, other, moved, after):
        one, two, three, own_sums = call(
            lambda *refs: weigh_kernel(phase, *refs), "weigh_members", [words] * 3 + [sums], [], [own, other, *moved, after]
        )
        send = ((1, one), (2, two), (3, three))
        return [lax.ppermute(v, "member", z_pairs(d)) for d, v in send] + [own_sums]

    x_send0 = call(
        load_first_kernel, "load_to_swap", ((tokens, 4 * wide + outs), BF16), [inputs, grads], [], [dma((4,)), dma]
    )
    x_got0 = swap_cores(x_send0)
    x_send1 = call(load_second_kernel, "load_to_swap", x_shape, [inputs], [x_send0], [dma((4,))])
    x_got1 = swap_cores(x_send1)
    x_own0, g_own, gt_own, part0 = call(
        own_first_kernel, "fisher_of_own_tokens", [x_shape, g_shape, gt_shape, part_shape], [inputs, grads], [x_send1],
        [dma((4,)), dma],
    )
    g_pair = call(pair_kernel, "pair_grads", ((2, tokens, outs), BF16), [], [g_own, x_got0, gt_own])
    g_other = swap_cols(g_pair)
    sent, kept00, gt_got = call(
        add_first_kernel, "fisher_of_both_cores", [sent_shape, kept_shape, gt_shape], [], [x_got0, part0, g_pair]
    )
    swap00 = swap_x(1, sent)
    x_own1, part1 = call(
        own_second_kernel, "fisher_of_own_tokens", [x_shape, part_shape], [inputs], [gt_own, kept00], [dma((4,))]
    )
    sent, kept01 = call(
        add_second_kernel, "fisher_of_both_cores", [sent_shape, kept_shape], [], [x_got1, gt_got, part1, x_own1]
    )
    swap01 = swap_x(1, sent)
    part00 = middle(3, swap00, kept00, kept01)

    sent, kept10, gt_own, gt_got = call(
        both_first_kernel, "fisher_of_other_grads", [sent_shape, kept_shape, gt_shape, gt_shape], [],
        [x_own0, x_got0, g_other, part00[0]],
    )
    swap10 = swap_x(1, sent)
    moved = bring_weights(kept10)
    part01 = middle(3, swap01, kept01, moved[0])
    sent, kept11 = call(
        both_second_kernel, "fisher_of_other_grads", [sent_shape, kept_shape], [],
        [x_own1, x_got1, gt_own, gt_got, part01[0]],
    )
    swap11 = swap_x(3, sent)

    settled0 = settle(part00, kept11)
    own0, other0 = join(settled0, part01, kept11)
    words0 = weigh(0, own0, other0, moved, own0)
    part10 = middle(3, swap10, kept10, words0[3])
    first = call(sum_kernel, "sum_over_z", words, [], [*words0, part10[0]])
    part11 = middle(1, swap11, kept11, first)
    own1, other1 = join(settle(part10, part11[0]), part11, first)
    words1 = weigh(1, own1, other1, moved, own1)
    met = call(meet_kernel, "meet_over_y", sums, [], [*results(0, first), own1])
    second = call(sum_kernel, "sum_over_z", words, [], [*words1, own1])
    near, far = results(1, second)
    return pl.pallas_call(
        merge_kernel,
        out_shape=jax.ShapeDtypeStruct((wide // Z, outs), F32),
        in_specs=[VMEM] * 3,
        out_specs=VMEM,
        compiler_params=pltpu.CompilerParams(vmem_limit_bytes=VMEM_LIMIT),
        name="merge_members",
    )(in_vmem(near), in_vmem(far), in_vmem(met))


def solution(mesh):
    in_specs = (P("member", "tok", "col"), P("member", "tok", "col"), P("member", "tok", "col"))
    out_specs = P(("tok", "member"), "col")
    return jax.shard_map(shards, mesh=mesh, in_specs=in_specs, out_specs=out_specs, check_vma=False)
```

```python
import jax
import jax.numpy as jnp
from jax import lax
from jax.experimental import pallas as pl
from jax.experimental.pallas import tpu as pltpu
from jax.sharding import PartitionSpec as P

F32 = jnp.float32
BF16 = jnp.bfloat16
HBM = pl.BlockSpec(memory_space=pltpu.HBM)
VMEM = pl.BlockSpec(memory_space=pltpu.VMEM)
VMEM_LIMIT = 16 << 20

GRID = 1.00297
BIG = 2.0**28
SMALL = 2.0**16
EDGE = 2.0**-40
EDGE_CODE = 2.0**-24

X, CORES, Z = 4, 2, 4

ORDER = (1, 2, 0, 3)
BACK = (3, 1, 2, 0)


def code_of(values):
    scaled = values * BIG
    return jnp.where(values >= EDGE, scaled * scaled, values * SMALL)


def value_of(code):
    return jnp.where(code >= EDGE_CODE, jnp.sqrt(code) * (1.0 / BIG), code * (1.0 / SMALL))


def encode(values):
    return code_of(values).astype(BF16)


def decode(sent):
    return value_of(sent.astype(F32))


def encode_fine(values):
    code = code_of(values)
    first = code.astype(BF16).astype(F32)
    second = (code * (1.0 / GRID)).astype(BF16).astype(F32)
    near = jnp.abs(first - code) <= jnp.abs(second * GRID - code)
    return jnp.where(near, first, -second).astype(BF16)


def decode_fine(sent):
    code = sent.astype(F32)
    return value_of(jnp.where(code < 0.0, code * (-GRID), code))


def in_vmem(array):
    return pltpu.with_memory_space_constraint(array, pltpu.VMEM)


def in_hbm(array):
    return pltpu.with_memory_space_constraint(array, pltpu.HBM)


def call(kernel, name, outs, hbm, vmem, scratch=()):
    single = not isinstance(outs, list)
    shapes = [pltpu.VMEM(shape, kind) for shape, kind in ([outs] if single else outs)]
    result = pl.pallas_call(
        kernel,
        out_shape=shapes,
        in_specs=[HBM] * len(hbm) + [VMEM] * len(vmem),
        out_specs=[VMEM] * len(shapes),
        scratch_shapes=list(scratch),
        compiler_params=pltpu.CompilerParams(vmem_limit_bytes=VMEM_LIMIT),
        cost_estimate=pl.CostEstimate(flops=1, bytes_accessed=1, transcendentals=0),
        name=name,
    )(*[in_hbm(a) for a in hbm], *[in_vmem(a) for a in vmem])
    return result[0] if single else result


def squared_transposed(g):
    g = g.astype(F32)
    return (g * g).T.astype(BF16)


def fisher_block(x, gt_ref):
    return jnp.dot(gt_ref[...], x * x, preferred_element_type=F32)


def where_am_i():
    tok, half, member = lax.axis_index("tok"), lax.axis_index("col"), lax.axis_index("member")
    return tok // 2, tok % 2, half, member // Z, member % Z


def column_block(flip, part):
    x, _, half, _, _ = where_am_i()
    owner = x ^ flip
    local = jnp.where(owner // 2 == half, 2 * (owner % 2), 2 * ((3 - owner) % 2) + 1)
    return 2 * local + part


def load_inputs(member, part, x_ref, x_out, sem):
    wide = x_out.shape[2]
    copies = []
    for s, flip in enumerate(ORDER):
        at = pl.multiple_of(column_block(flip, part) * wide, wide)
        copies.append(pltpu.make_async_copy(x_ref.at[member, :, pl.ds(at, wide)], x_out.at[s], sem.at[s]))
        copies[s].start()
    return copies


def load_first_kernel(x_ref, g_ref, out, sem, g_sem):
    core = where_am_i()[1]
    wide = x_ref.shape[2] // 8
    copies = [pltpu.make_async_copy(g_ref.at[1 - core], out.at[:, pl.ds(4 * wide, g_ref.shape[2])], g_sem)]
    for s, flip in enumerate(ORDER):
        at = pl.multiple_of(column_block(flip, 0) * wide, wide)
        copies.append(
            pltpu.make_async_copy(x_ref.at[1 - core, :, pl.ds(at, wide)], out.at[:, pl.ds(s * wide, wide)], sem.at[s])
        )
    for copy in copies:
        copy.start()
    for copy in copies:
        copy.wait()


def load_second_kernel(x_ref, after, x_out, sem):
    for copy in load_inputs(1 - where_am_i()[1], 1, x_ref, x_out, sem):
        copy.wait()


def pair_kernel(own, got, after, out):
    outs = own.shape[1]
    out[0], out[1] = own[...], got[:, got.shape[1] - outs :]


def own_tokens(copies, x_out, gt_ref, part_out):
    for s in range(4):
        copies[s].wait()
        part_out[s] = fisher_block(x_out[s], gt_ref)


def own_first_kernel(x_ref, g_ref, after, x_out, g_out, gt_out, part_out, sem, g_sem):
    core = where_am_i()[1]
    load = pltpu.make_async_copy(g_ref.at[core], g_out, g_sem)
    load.start()
    copies = load_inputs(core, 0, x_ref, x_out, sem)
    load.wait()
    gt_out[...] = squared_transposed(g_out[...])
    own_tokens(copies, x_out, gt_out, part_out)


def own_second_kernel(x_ref, gt_ref, after, x_out, part_out, sem):
    copies = load_inputs(where_am_i()[1], 1, x_ref, x_out, sem)
    own_tokens(copies, x_out, gt_ref, part_out)


def put(s, block, sent_out, kept_out):
    if s < 2:
        sent_out[s] = encode(block)
    else:
        kept_out[s - 2] = block


def add_first_kernel(x_ref, part_ref, after, sent_out, kept_out, gt_out):
    wide = part_ref.shape[2]
    gt_out[...] = squared_transposed(x_ref[:, 4 * wide :])
    for s in range(4):
        block = fisher_block(x_ref[:, s * wide : (s + 1) * wide], gt_out)
        put(s, part_ref[s] + block, sent_out, kept_out)


def add_second_kernel(x_ref, gt_ref, part_ref, after, sent_out, kept_out):
    for s in range(4):
        put(s, part_ref[s] + fisher_block(x_ref[s], gt_ref), sent_out, kept_out)


def both_first_kernel(xa_ref, xb_ref, g_ref, after, sent_out, kept_out, gta_out, gtb_out):
    wide = kept_out.shape[2]
    gta_out[...] = squared_transposed(g_ref[0])
    gtb_out[...] = squared_transposed(g_ref[1])
    for s in range(4):
        block = fisher_block(xb_ref[:, s * wide : (s + 1) * wide], gtb_out)
        put(s, fisher_block(xa_ref[s], gta_out) + block, sent_out, kept_out)


def both_second_kernel(xa_ref, xb_ref, gta_ref, gtb_ref, after, sent_out, kept_out):
    for s, block in enumerate(BACK):
        put(s, fisher_block(xa_ref[block], gta_ref) + fisher_block(xb_ref[block], gtb_ref), sent_out, kept_out)


def middle_kernel(kept_ref, got_ref, after, sent_out, own_out):
    sent_out[...] = encode_fine(kept_ref[1] + decode(got_ref[1]))
    own_out[...] = kept_ref[0] + decode(got_ref[0])


def settle_kernel(own, got, after, out):
    out[...] = own[...] + decode_fine(got[...])


def join_kernel(first_ref, own, got, after, kept_out, sent_out):
    first = first_ref[...]
    second = own[...] + decode_fine(got[...])
    core = where_am_i()[1]
    kept_out[...] = jnp.where(core == 0, first, second)
    sent_out[...] = encode_fine(jnp.where(core == 0, second, first))


def split_kernel(w_ref, after, own_out, send_out):
    rows, core = own_out.shape[1], where_am_i()[1]
    own_out[...] = w_ref[:, pl.ds(pl.multiple_of(core * rows, rows), rows), :]
    send_out[...] = w_ref[:, pl.ds(pl.multiple_of((1 - core) * rows, rows), rows), :]


def to_words(weighted, total, out):
    high = weighted.astype(BF16)
    out[0] = high
    out[1] = (weighted - high.astype(F32)).astype(BF16)
    out[2] = encode_fine(total)


def from_words(words):
    return words[0].astype(F32) + words[1].astype(F32), decode_fine(words[2])


def weigh_kernel(phase, own, other, w_own, w_other, after, one_out, two_out, three_out, sums_out):
    _, core, half, _, z = where_am_i()
    part = own.shape[1] // Z
    mine = (core ^ half ^ phase) == 0
    for d, out in ((2, two_out), (1, one_out), (3, three_out), (0, sums_out)):
        cols = pl.ds(pl.multiple_of((z + d) % Z * part, part), part)
        weighted = total = 0.0
        for values, m in ((own[:, cols], core), (decode_fine(other[:, cols]), 1 - core)):
            fisher = values.T
            weight = jnp.where(mine, w_own[m, cols, :].astype(F32), w_other[m, cols, :].astype(F32))
            weighted += fisher * weight
            total += fisher
        if d == 0:
            out[0], out[1] = weighted, total
        else:
            to_words(weighted, total, out)


def over_z(sums, words):
    weighted, total = sums[0], sums[1]
    for ref in words:
        more, added = from_words(ref)
        weighted += more
        total += added
    return weighted, total


def sum_kernel(one, two, three, sums, after, out):
    to_words(*over_z(sums, (one, two, three)), out)


def meet_kernel(near, far, after, out):
    (weighted, total), (more, added) = from_words(near), from_words(far)
    out[0], out[1] = weighted + more, total + added


def merge_kernel(near, far, sums, out):
    (weighted, total), (more, added) = from_words(near), from_words(far)
    out[...] = (weighted + more + sums[0]) / (total + added + sums[1])


def keeper(local, half):
    home = 2 * half + local // 2
    return home if local % 2 == 0 else 3 - home


def kept(x, half):
    return 2 * (x % 2) if x // 2 == half else 2 * ((3 - x) % 2) + 1


def weight_pairs():
    pairs = []
    for tok in range(X * CORES):
        half, local = divmod(tok, 4)
        for col in range(2):
            pairs.append((tok * 2 + col, (keeper(local, half) * 2 + col) * 2 + half))
    return pairs


def result_pairs(phase, sender):
    pairs = []
    for z in range(Z):
        for tok in range(X * CORES):
            x, core = divmod(tok, 2)
            for half in range(2):
                to_tok = 4 * half + kept(x, half)
                to = ((core * Z + z) * 8 + to_tok) * 2 + (half ^ phase)
                pairs.append((((sender * Z + z) * 8 + tok) * 2 + half, to))
    return pairs


def x_pairs(flip):
    return [(t, ((t // 2) ^ flip) * 2 + t % 2) for t in range(X * CORES)]


def z_pairs(distance):
    return [(m, m // Z * Z + (m + distance) % Z) for m in range(2 * Z)]


def shards(inputs, grads, weights):
    tokens, outs = grads.shape[1:]
    wide = inputs.shape[2] // 8
    x_shape, g_shape, gt_shape = ((4, tokens, wide), BF16), ((tokens, outs), BF16), ((outs, tokens), BF16)
    part_shape, sent_shape, kept_shape = ((4, outs, wide), F32), ((2, outs, wide), BF16), ((2, outs, wide), F32)
    code_shape, own_shape = ((outs, wide), BF16), ((outs, wide), F32)
    words, sums = ((3, wide // Z, outs), BF16), ((2, wide // Z, outs), F32)
    dma = pltpu.SemaphoreType.DMA

    def swap_cores(send):
        return lax.ppermute(send, "tok", [(t, t ^ 1) for t in range(8)])

    def swap_cols(send):
        return lax.ppermute(send, "col", [(0, 1), (1, 0)])

    def swap_x(flip, sent):
        return lax.ppermute(sent, "tok", x_pairs(flip))

    def middle(flip, got, kept_blocks, after):
        sent, own = call(middle_kernel, "fisher_over_first_swap", [code_shape, own_shape], [], [kept_blocks, got, after])
        return own, swap_x(flip, sent)

    def settle(one, after):
        return call(settle_kernel, "fisher_over_tokens", own_shape, [], [*one, after])

    def join(first, two, after):
        kept_block, sent = call(join_kernel, "fisher_over_tokens", [own_shape, code_shape], [], [first, *two, after])
        return kept_block, swap_cores(sent)

    def results(phase, sums):
        return [lax.ppermute(sums, ("member", "tok", "col"), result_pairs(phase, y_lo)) for y_lo in range(2)]

    def bring_weights(after):
        arrived = lax.ppermute(weights, ("tok", "col"), weight_pairs())
        half_shape = ((2, weights.shape[1] // 2, outs), BF16)
        own, send = call(split_kernel, "split_weights", [half_shape, half_shape], [], [arrived, after])
        return own, swap_cores(send)

    def weigh(phase, own, other, moved, after):
        one, two, three, own_sums = call(
            lambda *refs: weigh_kernel(phase, *refs), "weigh_members", [words] * 3 + [sums], [], [own, other, *moved, after]
        )
        send = ((1, one), (2, two), (3, three))
        return [lax.ppermute(v, "member", z_pairs(d)) for d, v in send] + [own_sums]

    x_send0 = call(
        load_first_kernel, "load_to_swap", ((tokens, 4 * wide + outs), BF16), [inputs, grads], [], [dma((4,)), dma]
    )
    x_got0 = swap_cores(x_send0)
    x_send1 = call(load_second_kernel, "load_to_swap", x_shape, [inputs], [x_send0], [dma((4,))])
    x_got1 = swap_cores(x_send1)
    x_own0, g_own, gt_own, part0 = call(
        own_first_kernel, "fisher_of_own_tokens", [x_shape, g_shape, gt_shape, part_shape], [inputs, grads], [x_send1],
        [dma((4,)), dma],
    )
    g_pair = call(pair_kernel, "pair_grads", ((2, tokens, outs), BF16), [], [g_own, x_got0, gt_own])
    g_other = swap_cols(g_pair)
    sent, kept00, gt_got = call(
        add_first_kernel, "fisher_of_both_cores", [sent_shape, kept_shape, gt_shape], [], [x_got0, part0, g_pair]
    )
    swap00 = swap_x(1, sent)
    x_own1, part1 = call(
        own_second_kernel, "fisher_of_own_tokens", [x_shape, part_shape], [inputs], [gt_own, kept00], [dma((4,))]
    )
    sent, kept01 = call(
        add_second_kernel, "fisher_of_both_cores", [sent_shape, kept_shape], [], [x_got1, gt_got, part1, x_own1]
    )
    swap01 = swap_x(1, sent)
    part00 = middle(3, swap00, kept00, kept01)

    sent, kept10, gt_own, gt_got = call(
        both_first_kernel, "fisher_of_other_grads", [sent_shape, kept_shape, gt_shape, gt_shape], [],
        [x_own0, x_got0, g_other, part00[0]],
    )
    swap10 = swap_x(1, sent)
    part01 = middle(3, swap01, kept01, kept10)
    sent, kept11 = call(
        both_second_kernel, "fisher_of_other_grads", [sent_shape, kept_shape], [],
        [x_own1, x_got1, gt_own, gt_got, part01[0]],
    )
    swap11 = swap_x(3, sent)

    settled0 = settle(part00, kept11)
    own0, other0 = join(settled0, part01, kept11)
    part10 = middle(3, swap10, kept10, own0)
    part11 = middle(1, swap11, kept11, part10[0])
    moved = bring_weights(part11[0])
    words0 = weigh(0, own0, other0, moved, moved[0])
    first = call(sum_kernel, "sum_over_z", words, [], [*words0, words0[3]])
    own1, other1 = join(settle(part10, first), part11, first)
    words1 = weigh(1, own1, other1, moved, own1)
    met = call(meet_kernel, "meet_over_y", sums, [], [*results(0, first), own1])
    second = call(sum_kernel, "sum_over_z", words, [], [*words1, own1])
    near, far = results(1, second)
    return pl.pallas_call(
        merge_kernel,
        out_shape=jax.ShapeDtypeStruct((wide // Z, outs), F32),
        in_specs=[VMEM] * 3,
        out_specs=VMEM,
        compiler_params=pltpu.CompilerParams(vmem_limit_bytes=VMEM_LIMIT),
        name="merge_members",
    )(in_vmem(near), in_vmem(far), in_vmem(met))


def solution(mesh):
    in_specs = (P("member", "tok", "col"), P("member", "tok", "col"), P("member", "tok", "col"))
    out_specs = P(("tok", "member"), "col")
    return jax.shard_map(shards, mesh=mesh, in_specs=in_specs, out_specs=out_specs, check_vma=False)
```

```python
import jax
import jax.numpy as jnp
from jax import lax
from jax.experimental import pallas as pl
from jax.experimental.pallas import tpu as pltpu
from jax.sharding import PartitionSpec as P

F32 = jnp.float32
BF16 = jnp.bfloat16
HBM = pl.BlockSpec(memory_space=pltpu.HBM)
VMEM = pl.BlockSpec(memory_space=pltpu.VMEM)
VMEM_LIMIT = 16 << 20

GRID = 1.00297
BIG = 2.0**28
SMALL = 2.0**16
EDGE = 2.0**-40
EDGE_CODE = 2.0**-24

X, CORES, Z = 4, 2, 4

ORDER = ((2, 1), (3, 0))


def code_of(values):
    scaled = values * BIG
    return jnp.where(values >= EDGE, scaled * scaled, values * SMALL)


def value_of(code):
    return jnp.where(code >= EDGE_CODE, jnp.sqrt(code) * (1.0 / BIG), code * (1.0 / SMALL))


def encode(values):
    return code_of(values).astype(BF16)


def decode(sent):
    return value_of(sent.astype(F32))


def encode_fine(values):
    code = code_of(values)
    first = code.astype(BF16).astype(F32)
    second = (code * (1.0 / GRID)).astype(BF16).astype(F32)
    near = jnp.abs(first - code) <= jnp.abs(second * GRID - code)
    return jnp.where(near, first, -second).astype(BF16)


def decode_fine(sent):
    code = sent.astype(F32)
    return value_of(jnp.where(code < 0.0, code * (-GRID), code))


def in_vmem(array):
    return pltpu.with_memory_space_constraint(array, pltpu.VMEM)


def in_hbm(array):
    return pltpu.with_memory_space_constraint(array, pltpu.HBM)


def call(kernel, name, outs, hbm, vmem, scratch=()):
    single = not isinstance(outs, list)
    shapes = [pltpu.VMEM(shape, kind) for shape, kind in ([outs] if single else outs)]
    result = pl.pallas_call(
        kernel,
        out_shape=shapes,
        in_specs=[HBM] * len(hbm) + [VMEM] * len(vmem),
        out_specs=[VMEM] * len(shapes),
        scratch_shapes=list(scratch),
        compiler_params=pltpu.CompilerParams(vmem_limit_bytes=VMEM_LIMIT),
        cost_estimate=pl.CostEstimate(flops=1, bytes_accessed=1, transcendentals=0),
        name=name,
    )(*[in_hbm(a) for a in hbm], *[in_vmem(a) for a in vmem])
    return result[0] if single else result


def squared_transposed(g):
    g = g.astype(F32)
    return (g * g).T.astype(BF16)


def fisher_block(x, gt_ref):
    return jnp.dot(gt_ref[...], x * x, preferred_element_type=F32)


def where_am_i():
    tok, half, member = lax.axis_index("tok"), lax.axis_index("col"), lax.axis_index("member")
    return tok // 2, tok % 2, half, member // Z, member % Z


def load_inputs(member, pair, x_ref, x_out, sem):
    x, _, half, _, _ = where_am_i()
    wide = x_ref.shape[2] // 4
    copies = []
    for s, flip in enumerate(ORDER[pair]):
        owner = x ^ flip
        local = jnp.where(owner // 2 == half, 2 * (owner % 2), 2 * ((3 - owner) % 2) + 1)
        at = pl.multiple_of(local * wide, wide)
        source = x_ref.at[member, :, pl.ds(at, wide)]
        copies.append(pltpu.make_async_copy(source, x_out.at[:, pl.ds(s * wide, wide)], sem.at[s]))
        copies[s].start()
    return copies


def load_first_kernel(x_ref, g_ref, out, sem, g_sem):
    core = where_am_i()[1]
    outs = g_ref.shape[2]
    load = pltpu.make_async_copy(g_ref.at[1 - core], out.at[:, pl.ds(out.shape[1] - outs, outs)], g_sem)
    load.start()
    for copy in load_inputs(1 - core, 0, x_ref, out, sem) + [load]:
        copy.wait()


def load_second_kernel(x_ref, after, x_out, sem):
    for copy in load_inputs(1 - where_am_i()[1], 1, x_ref, x_out, sem):
        copy.wait()


def pair_kernel(own, got, after, out):
    outs = own.shape[1]
    out[0], out[1] = own[...], got[:, got.shape[1] - outs :]


def columns(s, x_ref, wide):
    return x_ref[:, s * wide : (s + 1) * wide]


def own_tokens(copies, x_out, gt_ref, part_out):
    for s in range(2):
        copies[s].wait()
        part_out[s] = fisher_block(columns(s, x_out, part_out.shape[2]), gt_ref)


def own_first_kernel(x_ref, g_ref, after, x_out, g_out, gt_out, part_out, sem, g_sem):
    core = where_am_i()[1]
    load = pltpu.make_async_copy(g_ref.at[core], g_out, g_sem)
    load.start()
    copies = load_inputs(core, 0, x_ref, x_out, sem)
    load.wait()
    gt_out[...] = squared_transposed(g_out[...])
    own_tokens(copies, x_out, gt_out, part_out)


def own_second_kernel(x_ref, gt_ref, after, x_out, part_out, sem):
    copies = load_inputs(where_am_i()[1], 1, x_ref, x_out, sem)
    own_tokens(copies, x_out, gt_ref, part_out)


def add_first_kernel(x_ref, part_ref, after, two_out, one_out, gt_out):
    wide, outs = part_ref.shape[2], part_ref.shape[1]
    gt_out[...] = squared_transposed(x_ref[:, 2 * wide :])
    for s, out in enumerate((two_out, one_out)):
        out[...] = encode(part_ref[s] + fisher_block(columns(s, x_ref, wide), gt_out))


def add_second_kernel(x_ref, gt_ref, part_ref, after, three_out, own_out):
    wide = part_ref.shape[2]
    three_out[...] = encode(part_ref[0] + fisher_block(columns(0, x_ref, wide), gt_ref))
    own_out[...] = part_ref[1] + fisher_block(columns(1, x_ref, wide), gt_ref)


def half_block(flip, part, x_refs, gt_refs, wide):
    pair = 0 if flip in ORDER[0] else 1
    at = (2 * ORDER[pair].index(flip) + part) * wide
    own, got = x_refs[2 * pair : 2 * pair + 2]
    return fisher_block(own[:, at : at + wide], gt_refs[0]) + fisher_block(got[:, at : at + wide], gt_refs[1])


def both_first_kernel(own_a, got_a, own_b, got_b, g_ref, after, sent_out, kept_out, gta_out, gtb_out):
    gta_out[...] = squared_transposed(g_ref[0])
    gtb_out[...] = squared_transposed(g_ref[1])
    for s, flip in enumerate((1, 2, 0, 3)):
        put(s, half_block(flip, 0, (own_a, got_a, own_b, got_b), (gta_out, gtb_out), sent_out.shape[2]), sent_out, kept_out)


def both_second_kernel(own_a, got_a, own_b, got_b, gta_ref, gtb_ref, after, sent_out, kept_out):
    for s, flip in enumerate((3, 2, 0, 1)):
        put(s, half_block(flip, 1, (own_a, got_a, own_b, got_b), (gta_ref, gtb_ref), sent_out.shape[2]), sent_out, kept_out)


def put(s, block, sent_out, kept_out):
    if s < 2:
        sent_out[s] = encode(block)
    else:
        kept_out[s - 2] = block


def middle_kernel(kept_ref, got_ref, after, sent_out, own_out):
    sent_out[...] = encode_fine(kept_ref[1] + decode(got_ref[1]))
    own_out[...] = kept_ref[0] + decode(got_ref[0])


def settle_kernel(own, got, after, out):
    out[...] = own[...] + decode_fine(got[...])


def join_kernel(first_ref, own, got, after, kept_out, sent_out):
    first = first_ref[...]
    second = own[...] + decode_fine(got[...])
    core = where_am_i()[1]
    kept_out[...] = jnp.where(core == 0, first, second)
    sent_out[...] = encode_fine(jnp.where(core == 0, second, first))


def join_direct_kernel(own, one, two, three, after, kept_out, sent_out):
    wide = kept_out.shape[1]
    halves = []
    for s in range(2):
        got = [decode(columns(s, ref, wide)) for ref in (one, two, three)]
        halves.append(columns(s, own, wide) + got[0] + got[1] + got[2])
    core = where_am_i()[1]
    kept_out[...] = jnp.where(core == 0, halves[0], halves[1])
    sent_out[...] = encode_fine(jnp.where(core == 0, halves[1], halves[0]))


def split_kernel(w_ref, after, own_out, send_out):
    rows, core = own_out.shape[1], where_am_i()[1]
    own_out[...] = w_ref[:, pl.ds(pl.multiple_of(core * rows, rows), rows), :]
    send_out[...] = w_ref[:, pl.ds(pl.multiple_of((1 - core) * rows, rows), rows), :]


def to_words(weighted, total, out):
    high = weighted.astype(BF16)
    out[0] = high
    out[1] = (weighted - high.astype(F32)).astype(BF16)
    out[2] = encode_fine(total)


def from_words(words):
    return words[0].astype(F32) + words[1].astype(F32), decode_fine(words[2])


def weigh_kernel(phase, own, other, w_own, w_other, after, one_out, two_out, three_out, sums_out):
    _, core, half, _, z = where_am_i()
    part = own.shape[1] // Z
    mine = (core ^ half ^ phase) == 0
    for d, out in ((2, two_out), (1, one_out), (3, three_out), (0, sums_out)):
        cols = pl.ds(pl.multiple_of((z + d) % Z * part, part), part)
        weighted = total = 0.0
        for values, m in ((own[:, cols], core), (decode_fine(other[:, cols]), 1 - core)):
            fisher = values.T
            weight = jnp.where(mine, w_own[m, cols, :].astype(F32), w_other[m, cols, :].astype(F32))
            weighted += fisher * weight
            total += fisher
        if d == 0:
            out[0], out[1] = weighted, total
        else:
            to_words(weighted, total, out)


def over_z(sums, words):
    weighted, total = sums[0], sums[1]
    for ref in words:
        more, added = from_words(ref)
        weighted += more
        total += added
    return weighted, total


def sum_kernel(one, two, three, sums, after, out):
    to_words(*over_z(sums, (one, two, three)), out)


def meet_kernel(near, far, after, out):
    (weighted, total), (more, added) = from_words(near), from_words(far)
    out[0], out[1] = weighted + more, total + added


def merge_kernel(near, far, sums, out):
    (weighted, total), (more, added) = from_words(near), from_words(far)
    out[...] = (weighted + more + sums[0]) / (total + added + sums[1])


def keeper(local, half):
    home = 2 * half + local // 2
    return home if local % 2 == 0 else 3 - home


def kept(x, half):
    return 2 * (x % 2) if x // 2 == half else 2 * ((3 - x) % 2) + 1


def weight_pairs():
    pairs = []
    for tok in range(X * CORES):
        half, local = divmod(tok, 4)
        for col in range(2):
            pairs.append((tok * 2 + col, (keeper(local, half) * 2 + col) * 2 + half))
    return pairs


def result_pairs(phase, sender):
    pairs = []
    for z in range(Z):
        for tok in range(X * CORES):
            x, core = divmod(tok, 2)
            for half in range(2):
                to_tok = 4 * half + kept(x, half)
                to = ((core * Z + z) * 8 + to_tok) * 2 + (half ^ phase)
                pairs.append((((sender * Z + z) * 8 + tok) * 2 + half, to))
    return pairs


def x_pairs(flip):
    return [(t, ((t // 2) ^ flip) * 2 + t % 2) for t in range(X * CORES)]


def z_pairs(distance):
    return [(m, m // Z * Z + (m + distance) % Z) for m in range(2 * Z)]


def shards(inputs, grads, weights):
    tokens, outs = grads.shape[1:]
    wide = inputs.shape[2] // 8
    x_shape, g_shape, gt_shape = ((tokens, 4 * wide), BF16), ((tokens, outs), BF16), ((outs, tokens), BF16)
    part_shape, sent_shape, sum_shape = ((2, outs, 2 * wide), F32), ((outs, 2 * wide), BF16), ((outs, 2 * wide), F32)
    code_shape, own_shape = ((outs, wide), BF16), ((outs, wide), F32)
    pair_shape, kept_shape = ((2, outs, wide), BF16), ((2, outs, wide), F32)
    words, sums = ((3, wide // Z, outs), BF16), ((2, wide // Z, outs), F32)
    dma = pltpu.SemaphoreType.DMA

    def swap_cores(send):
        return lax.ppermute(send, "tok", [(t, t ^ 1) for t in range(8)])

    def swap_cols(send):
        return lax.ppermute(send, "col", [(0, 1), (1, 0)])

    def swap_x(flip, sent):
        return lax.ppermute(sent, "tok", x_pairs(flip))

    def middle(flip, got, kept_blocks, after):
        sent, own = call(middle_kernel, "fisher_over_first_swap", [code_shape, own_shape], [], [kept_blocks, got, after])
        return own, swap_x(flip, sent)

    def settle(one, after):
        return call(settle_kernel, "fisher_over_tokens", own_shape, [], [*one, after])

    def join_direct(own, got, after):
        kept_block, sent = call(
            join_direct_kernel, "fisher_over_tokens", [own_shape, code_shape], [], [own, got[1], got[2], got[3], after]
        )
        return kept_block, swap_cores(sent)

    def join(first, two, after):
        kept_block, sent = call(join_kernel, "fisher_over_tokens", [own_shape, code_shape], [], [first, *two, after])
        return kept_block, swap_cores(sent)

    def results(phase, sums):
        return [lax.ppermute(sums, ("member", "tok", "col"), result_pairs(phase, y_lo)) for y_lo in range(2)]

    def bring_weights(after):
        arrived = lax.ppermute(weights, ("tok", "col"), weight_pairs())
        half_shape = ((2, weights.shape[1] // 2, outs), BF16)
        own, send = call(split_kernel, "split_weights", [half_shape, half_shape], [], [arrived, after])
        return own, swap_cores(send)

    def weigh(phase, own, other, moved, after):
        one, two, three, own_sums = call(
            lambda *refs: weigh_kernel(phase, *refs), "weigh_members", [words] * 3 + [sums], [], [own, other, *moved, after]
        )
        send = ((1, one), (2, two), (3, three))
        return [lax.ppermute(v, "member", z_pairs(d)) for d, v in send] + [own_sums]

    x_send0 = call(
        load_first_kernel, "load_to_swap", ((tokens, 4 * wide + outs), BF16), [inputs, grads], [], [dma((2,)), dma]
    )
    x_got0 = swap_cores(x_send0)
    x_send1 = call(load_second_kernel, "load_to_swap", x_shape, [inputs], [x_send0], [dma((2,))])
    x_got1 = swap_cores(x_send1)
    x_own0, g_own, gt_own, part0 = call(
        own_first_kernel, "fisher_of_own_tokens", [x_shape, g_shape, gt_shape, part_shape], [inputs, grads], [x_send1],
        [dma((2,)), dma],
    )
    g_pair = call(pair_kernel, "pair_grads", ((2, tokens, outs), BF16), [], [g_own, x_got0, gt_own])
    g_other = swap_cols(g_pair)
    two, one, gt_got = call(
        add_first_kernel, "fisher_of_both_cores", [sent_shape, sent_shape, gt_shape], [], [x_got0, part0, g_pair]
    )
    got0 = {2: swap_x(2, two), 1: swap_x(1, one)}
    x_own1, part1 = call(
        own_second_kernel, "fisher_of_own_tokens", [x_shape, part_shape], [inputs], [gt_own, two], [dma((2,))]
    )
    three, sum0 = call(
        add_second_kernel, "fisher_of_both_cores", [sent_shape, sum_shape], [], [x_got1, gt_got, part1, x_own1]
    )
    got0[3] = swap_x(3, three)

    xs = [x_own0, x_got0, x_own1, x_got1]
    sent, kept10, gt_own, gt_got = call(
        both_first_kernel, "fisher_of_other_grads", [pair_shape, kept_shape, gt_shape, gt_shape], [], [*xs, g_other, three]
    )
    swap10 = swap_x(1, sent)
    moved = bring_weights(kept10)
    sent, kept11 = call(
        both_second_kernel, "fisher_of_other_grads", [pair_shape, kept_shape], [], [*xs, gt_own, gt_got, moved[0]]
    )
    swap11 = swap_x(3, sent)

    own0, other0 = join_direct(sum0, got0, kept11)
    words0 = weigh(0, own0, other0, moved, own0)
    part10 = middle(3, swap10, kept10, words0[3])
    first = call(sum_kernel, "sum_over_z", words, [], [*words0, part10[0]])
    part11 = middle(1, swap11, kept11, first)
    own1, other1 = join(settle(part10, part11[0]), part11, first)
    words1 = weigh(1, own1, other1, moved, own1)
    met = call(meet_kernel, "meet_over_y", sums, [], [*results(0, first), own1])
    second = call(sum_kernel, "sum_over_z", words, [], [*words1, own1])
    near, far = results(1, second)
    return pl.pallas_call(
        merge_kernel,
        out_shape=jax.ShapeDtypeStruct((wide // Z, outs), F32),
        in_specs=[VMEM] * 3,
        out_specs=VMEM,
        compiler_params=pltpu.CompilerParams(vmem_limit_bytes=VMEM_LIMIT),
        name="merge_members",
    )(in_vmem(near), in_vmem(far), in_vmem(met))


def solution(mesh):
    in_specs = (P("member", "tok", "col"), P("member", "tok", "col"), P("member", "tok", "col"))
    out_specs = P(("tok", "member"), "col")
    return jax.shard_map(shards, mesh=mesh, in_specs=in_specs, out_specs=out_specs, check_vma=False)
```

```python
import jax
import jax.numpy as jnp
from jax import lax
from jax.experimental import pallas as pl
from jax.experimental.pallas import tpu as pltpu
from jax.sharding import PartitionSpec as P

F32 = jnp.float32
BF16 = jnp.bfloat16
HBM = pl.BlockSpec(memory_space=pltpu.HBM)
VMEM = pl.BlockSpec(memory_space=pltpu.VMEM)
VMEM_LIMIT = 16 << 20

GRID = 1.00297
BIG = 2.0**28
SMALL = 2.0**16
EDGE = 2.0**-40
EDGE_CODE = 2.0**-24

X, CORES, Z = 4, 2, 4

ORDER = ((2, 1), (3, 0))


def code_of(values):
    scaled = values * BIG
    return jnp.where(values >= EDGE, scaled * scaled, values * SMALL)


def value_of(code):
    return jnp.where(code >= EDGE_CODE, jnp.sqrt(code) * (1.0 / BIG), code * (1.0 / SMALL))


def encode(values):
    return code_of(values).astype(BF16)


def decode(sent):
    return value_of(sent.astype(F32))


def encode_fine(values):
    code = code_of(values)
    first = code.astype(BF16).astype(F32)
    second = (code * (1.0 / GRID)).astype(BF16).astype(F32)
    near = jnp.abs(first - code) <= jnp.abs(second * GRID - code)
    return jnp.where(near, first, -second).astype(BF16)


def decode_fine(sent):
    code = sent.astype(F32)
    return value_of(jnp.where(code < 0.0, code * (-GRID), code))


def in_vmem(array):
    return pltpu.with_memory_space_constraint(array, pltpu.VMEM)


def in_hbm(array):
    return pltpu.with_memory_space_constraint(array, pltpu.HBM)


def call(kernel, name, outs, hbm, vmem, scratch=()):
    single = not isinstance(outs, list)
    shapes = [pltpu.VMEM(shape, kind) for shape, kind in ([outs] if single else outs)]
    result = pl.pallas_call(
        kernel,
        out_shape=shapes,
        in_specs=[HBM] * len(hbm) + [VMEM] * len(vmem),
        out_specs=[VMEM] * len(shapes),
        scratch_shapes=list(scratch),
        compiler_params=pltpu.CompilerParams(vmem_limit_bytes=VMEM_LIMIT),
        cost_estimate=pl.CostEstimate(flops=1, bytes_accessed=1, transcendentals=0),
        name=name,
    )(*[in_hbm(a) for a in hbm], *[in_vmem(a) for a in vmem])
    return result[0] if single else result


def squared_transposed(g):
    g = g.astype(F32)
    return (g * g).T.astype(BF16)


def fisher_block(x, gt_ref):
    return jnp.dot(gt_ref[...], x * x, preferred_element_type=F32)


def where_am_i():
    tok, half, member = lax.axis_index("tok"), lax.axis_index("col"), lax.axis_index("member")
    return tok // 2, tok % 2, half, member // Z, member % Z


def load_inputs(member, pair, x_ref, x_out, sem):
    x, _, half, _, _ = where_am_i()
    wide = x_ref.shape[2] // 4
    copies = []
    for s, flip in enumerate(ORDER[pair]):
        owner = x ^ flip
        local = jnp.where(owner // 2 == half, 2 * (owner % 2), 2 * ((3 - owner) % 2) + 1)
        at = pl.multiple_of(local * wide, wide)
        source = x_ref.at[member, :, pl.ds(at, wide)]
        copies.append(pltpu.make_async_copy(source, x_out.at[:, pl.ds(s * wide, wide)], sem.at[s]))
        copies[s].start()
    return copies


def load_first_kernel(x_ref, g_ref, out, sem, g_sem):
    core = where_am_i()[1]
    outs = g_ref.shape[2]
    load = pltpu.make_async_copy(g_ref.at[1 - core], out.at[:, pl.ds(out.shape[1] - outs, outs)], g_sem)
    load.start()
    for copy in load_inputs(1 - core, 0, x_ref, out, sem) + [load]:
        copy.wait()


def load_second_kernel(x_ref, after, x_out, sem):
    for copy in load_inputs(1 - where_am_i()[1], 1, x_ref, x_out, sem):
        copy.wait()


def pair_kernel(own, got, after, out):
    outs = own.shape[1]
    out[0], out[1] = own[...], got[:, got.shape[1] - outs :]


def columns(s, x_ref, wide):
    return x_ref[:, s * wide : (s + 1) * wide]


def own_tokens(copies, x_out, gt_ref, part_out):
    for s in range(2):
        copies[s].wait()
        part_out[s] = fisher_block(columns(s, x_out, part_out.shape[2]), gt_ref)


def own_first_kernel(x_ref, g_ref, after, x_out, g_out, gt_out, part_out, sem, g_sem):
    core = where_am_i()[1]
    load = pltpu.make_async_copy(g_ref.at[core], g_out, g_sem)
    load.start()
    copies = load_inputs(core, 0, x_ref, x_out, sem)
    load.wait()
    gt_out[...] = squared_transposed(g_out[...])
    own_tokens(copies, x_out, gt_out, part_out)


def own_second_kernel(x_ref, gt_ref, after, x_out, part_out, sem):
    copies = load_inputs(where_am_i()[1], 1, x_ref, x_out, sem)
    own_tokens(copies, x_out, gt_ref, part_out)


def add_first_kernel(x_ref, part_ref, after, two_out, one_out, gt_out):
    wide, outs = part_ref.shape[2], part_ref.shape[1]
    gt_out[...] = squared_transposed(x_ref[:, 2 * wide :])
    for s, out in enumerate((two_out, one_out)):
        out[...] = encode(part_ref[s] + fisher_block(columns(s, x_ref, wide), gt_out))


def add_second_kernel(x_ref, gt_ref, part_ref, after, three_out, own_out):
    wide = part_ref.shape[2]
    three_out[...] = encode(part_ref[0] + fisher_block(columns(0, x_ref, wide), gt_ref))
    own_out[...] = part_ref[1] + fisher_block(columns(1, x_ref, wide), gt_ref)


def half_block(flip, part, x_refs, gt_refs, wide):
    pair = 0 if flip in ORDER[0] else 1
    at = (2 * ORDER[pair].index(flip) + part) * wide
    own, got = x_refs[2 * pair : 2 * pair + 2]
    return fisher_block(own[:, at : at + wide], gt_refs[0]) + fisher_block(got[:, at : at + wide], gt_refs[1])


def both_first_kernel(own_a, got_a, own_b, got_b, g_ref, after, sent_out, kept_out, gta_out, gtb_out):
    gta_out[...] = squared_transposed(g_ref[0])
    gtb_out[...] = squared_transposed(g_ref[1])
    for s, flip in enumerate((1, 2, 0, 3)):
        put(s, half_block(flip, 0, (own_a, got_a, own_b, got_b), (gta_out, gtb_out), sent_out.shape[2]), sent_out, kept_out)


def both_second_kernel(own_a, got_a, own_b, got_b, gta_ref, gtb_ref, after, sent_out, kept_out):
    for s, flip in enumerate((3, 2, 0, 1)):
        put(s, half_block(flip, 1, (own_a, got_a, own_b, got_b), (gta_ref, gtb_ref), sent_out.shape[2]), sent_out, kept_out)


def put(s, block, sent_out, kept_out):
    if s < 2:
        sent_out[s] = encode(block)
    else:
        kept_out[s - 2] = block


def middle_kernel(kept_ref, got_ref, after, sent_out, own_out):
    sent_out[...] = encode_fine(kept_ref[1] + decode(got_ref[1]))
    own_out[...] = kept_ref[0] + decode(got_ref[0])


def settle_kernel(own, got, after, out):
    out[...] = own[...] + decode_fine(got[...])


def join_kernel(first_ref, own, got, after, kept_out, sent_out):
    first = first_ref[...]
    second = own[...] + decode_fine(got[...])
    core = where_am_i()[1]
    kept_out[...] = jnp.where(core == 0, first, second)
    sent_out[...] = encode_fine(jnp.where(core == 0, second, first))


def join_direct_kernel(own, one, two, three, after, kept_out, sent_out):
    wide = kept_out.shape[1]
    halves = []
    for s in range(2):
        got = [decode(columns(s, ref, wide)) for ref in (one, two, three)]
        halves.append(columns(s, own, wide) + got[0] + got[1] + got[2])
    core = where_am_i()[1]
    kept_out[...] = jnp.where(core == 0, halves[0], halves[1])
    sent_out[...] = encode_fine(jnp.where(core == 0, halves[1], halves[0]))


def split_kernel(w_ref, after, own_out, send_out):
    rows, core = own_out.shape[1], where_am_i()[1]
    own_out[...] = w_ref[:, pl.ds(pl.multiple_of(core * rows, rows), rows), :]
    send_out[...] = w_ref[:, pl.ds(pl.multiple_of((1 - core) * rows, rows), rows), :]


def to_words(weighted, total, out):
    high = weighted.astype(BF16)
    out[0] = high
    out[1] = (weighted - high.astype(F32)).astype(BF16)
    out[2] = encode_fine(total)


def from_words(words):
    return words[0].astype(F32) + words[1].astype(F32), decode_fine(words[2])


def weigh_kernel(phase, own, other, w_own, w_other, after, one_out, two_out, three_out, sums_out):
    _, core, half, _, z = where_am_i()
    part = own.shape[1] // Z
    mine = (core ^ half ^ phase) == 0
    for d, out in ((2, two_out), (1, one_out), (3, three_out), (0, sums_out)):
        cols = pl.ds(pl.multiple_of((z + d) % Z * part, part), part)
        weighted = total = 0.0
        for values, m in ((own[:, cols], core), (decode_fine(other[:, cols]), 1 - core)):
            fisher = values.T
            weight = jnp.where(mine, w_own[m, cols, :].astype(F32), w_other[m, cols, :].astype(F32))
            weighted += fisher * weight
            total += fisher
        if d == 0:
            out[0], out[1] = weighted, total
        else:
            to_words(weighted, total, out)


def over_z(sums, words):
    weighted, total = sums[0], sums[1]
    for ref in words:
        more, added = from_words(ref)
        weighted += more
        total += added
    return weighted, total


def sum_kernel(one, two, three, sums, after, out):
    to_words(*over_z(sums, (one, two, three)), out)


def meet_kernel(near, far, after, out):
    (weighted, total), (more, added) = from_words(near), from_words(far)
    out[0], out[1] = weighted + more, total + added


def merge_kernel(near, far, sums, out):
    (weighted, total), (more, added) = from_words(near), from_words(far)
    out[...] = (weighted + more + sums[0]) / (total + added + sums[1])


def keeper(local, half):
    home = 2 * half + local // 2
    return home if local % 2 == 0 else 3 - home


def kept(x, half):
    return 2 * (x % 2) if x // 2 == half else 2 * ((3 - x) % 2) + 1


def weight_pairs(phase):
    pairs = []
    for tok in range(X * CORES):
        half, local = divmod(tok, 4)
        col = half ^ phase
        pairs.append((tok * 2 + col, (keeper(local, half) * 2 + col) * 2 + half))
    return pairs


def result_pairs(phase, sender):
    pairs = []
    for z in range(Z):
        for tok in range(X * CORES):
            x, core = divmod(tok, 2)
            for half in range(2):
                to_tok = 4 * half + kept(x, half)
                to = ((core * Z + z) * 8 + to_tok) * 2 + (half ^ phase)
                pairs.append((((sender * Z + z) * 8 + tok) * 2 + half, to))
    return pairs


def x_pairs(flip):
    return [(t, ((t // 2) ^ flip) * 2 + t % 2) for t in range(X * CORES)]


def z_pairs(distance):
    return [(m, m // Z * Z + (m + distance) % Z) for m in range(2 * Z)]


def shards(inputs, grads, weights):
    tokens, outs = grads.shape[1:]
    wide = inputs.shape[2] // 8
    x_shape, g_shape, gt_shape = ((tokens, 4 * wide), BF16), ((tokens, outs), BF16), ((outs, tokens), BF16)
    part_shape, sent_shape, sum_shape = ((2, outs, 2 * wide), F32), ((outs, 2 * wide), BF16), ((outs, 2 * wide), F32)
    code_shape, own_shape = ((outs, wide), BF16), ((outs, wide), F32)
    pair_shape, kept_shape = ((2, outs, wide), BF16), ((2, outs, wide), F32)
    words, sums = ((3, wide // Z, outs), BF16), ((2, wide // Z, outs), F32)
    dma = pltpu.SemaphoreType.DMA

    def swap_cores(send):
        return lax.ppermute(send, "tok", [(t, t ^ 1) for t in range(8)])

    def swap_cols(send):
        return lax.ppermute(send, "col", [(0, 1), (1, 0)])

    def swap_x(flip, sent):
        return lax.ppermute(sent, "tok", x_pairs(flip))

    def middle(flip, got, kept_blocks, after):
        sent, own = call(middle_kernel, "fisher_over_first_swap", [code_shape, own_shape], [], [kept_blocks, got, after])
        return own, swap_x(flip, sent)

    def settle(one, after):
        return call(settle_kernel, "fisher_over_tokens", own_shape, [], [*one, after])

    def join_direct(own, got, after):
        kept_block, sent = call(
            join_direct_kernel, "fisher_over_tokens", [own_shape, code_shape], [], [own, got[1], got[2], got[3], after]
        )
        return kept_block, swap_cores(sent)

    def join(first, two, after):
        kept_block, sent = call(join_kernel, "fisher_over_tokens", [own_shape, code_shape], [], [first, *two, after])
        return kept_block, swap_cores(sent)

    def results(phase, sums):
        return [lax.ppermute(sums, ("member", "tok", "col"), result_pairs(phase, y_lo)) for y_lo in range(2)]

    def bring_weights(phase, after):
        arrived = lax.ppermute(weights, ("tok", "col"), weight_pairs(phase))
        half_shape = ((2, weights.shape[1] // 2, outs), BF16)
        own, send = call(split_kernel, "split_weights", [half_shape, half_shape], [], [arrived, after])
        return own, swap_cores(send)

    def weigh(phase, own, other, moved, after):
        one, two, three, own_sums = call(
            lambda *refs: weigh_kernel(phase, *refs), "weigh_members", [words] * 3 + [sums], [], [own, other, *moved, after]
        )
        send = ((2, two), (1, one), (3, three))
        return [lax.ppermute(v, "member", z_pairs(d)) for d, v in send] + [own_sums]

    x_send0 = call(
        load_first_kernel, "load_to_swap", ((tokens, 4 * wide + outs), BF16), [inputs, grads], [], [dma((2,)), dma]
    )
    x_got0 = swap_cores(x_send0)
    x_send1 = call(load_second_kernel, "load_to_swap", x_shape, [inputs], [x_send0], [dma((2,))])
    x_got1 = swap_cores(x_send1)
    x_own0, g_own, gt_own, part0 = call(
        own_first_kernel, "fisher_of_own_tokens", [x_shape, g_shape, gt_shape, part_shape], [inputs, grads], [x_send1],
        [dma((2,)), dma],
    )
    g_pair = call(pair_kernel, "pair_grads", ((2, tokens, outs), BF16), [], [g_own, x_got0, gt_own])
    g_other = swap_cols(g_pair)
    two, one, gt_got = call(
        add_first_kernel, "fisher_of_both_cores", [sent_shape, sent_shape, gt_shape], [], [x_got0, part0, g_pair]
    )
    got0 = {2: swap_x(2, two), 1: swap_x(1, one)}
    x_own1, part1 = call(
        own_second_kernel, "fisher_of_own_tokens", [x_shape, part_shape], [inputs], [gt_own, two], [dma((2,))]
    )
    three, sum0 = call(
        add_second_kernel, "fisher_of_both_cores", [sent_shape, sum_shape], [], [x_got1, gt_got, part1, x_own1]
    )
    got0[3] = swap_x(3, three)

    xs = [x_own0, x_got0, x_own1, x_got1]
    sent, kept10, gt_own, gt_got = call(
        both_first_kernel, "fisher_of_other_grads", [pair_shape, kept_shape, gt_shape, gt_shape], [], [*xs, g_other, three]
    )
    swap10 = swap_x(1, sent)
    w0 = bring_weights(0, kept10)
    sent, kept11 = call(
        both_second_kernel, "fisher_of_other_grads", [pair_shape, kept_shape], [], [*xs, gt_own, gt_got, w0[0]]
    )
    swap11 = swap_x(3, sent)

    own0, other0 = join_direct(sum0, got0, kept11)
    words0 = weigh(0, own0, other0, w0, own0)
    part10 = middle(3, swap10, kept10, words0[3])
    first = call(sum_kernel, "sum_over_z", words, [], [*words0, part10[0]])
    part11 = middle(1, swap11, kept11, first)
    own1, other1 = join(settle(part10, part11[0]), part11, first)
    w1 = bring_weights(1, own1)
    words1 = weigh(1, own1, other1, w1, w1[0])
    met = call(meet_kernel, "meet_over_y", sums, [], [*results(0, first), own1])
    second = call(sum_kernel, "sum_over_z", words, [], [*words1, own1])
    near, far = results(1, second)
    return pl.pallas_call(
        merge_kernel,
        out_shape=jax.ShapeDtypeStruct((wide // Z, outs), F32),
        in_specs=[VMEM] * 3,
        out_specs=VMEM,
        compiler_params=pltpu.CompilerParams(vmem_limit_bytes=VMEM_LIMIT),
        name="merge_members",
    )(in_vmem(near), in_vmem(far), in_vmem(met))


def solution(mesh):
    in_specs = (P("member", "tok", "col"), P("member", "tok", "col"), P("member", "tok", "col"))
    out_specs = P(("tok", "member"), "col")
    return jax.shard_map(shards, mesh=mesh, in_specs=in_specs, out_specs=out_specs, check_vma=False)
```

```python
import jax
import jax.numpy as jnp
from jax import lax
from jax.experimental import pallas as pl
from jax.experimental.pallas import tpu as pltpu
from jax.sharding import PartitionSpec as P

F32 = jnp.float32
BF16 = jnp.bfloat16
HBM = pl.BlockSpec(memory_space=pltpu.HBM)
VMEM = pl.BlockSpec(memory_space=pltpu.VMEM)
VMEM_LIMIT = 16 << 20

GRID = 1.00297
BIG = 2.0**28
SMALL = 2.0**16
EDGE = 2.0**-40
EDGE_CODE = 2.0**-24

X, CORES, Z = 4, 2, 4

ORDER = ((2, 1), (3, 0))


def code_of(values):
    scaled = values * BIG
    return jnp.where(values >= EDGE, scaled * scaled, values * SMALL)


def value_of(code):
    return jnp.where(code >= EDGE_CODE, jnp.sqrt(code) * (1.0 / BIG), code * (1.0 / SMALL))


def encode(values):
    return code_of(values).astype(BF16)


def decode(sent):
    return value_of(sent.astype(F32))


def encode_fine(values):
    code = code_of(values)
    first = code.astype(BF16).astype(F32)
    second = (code * (1.0 / GRID)).astype(BF16).astype(F32)
    near = jnp.abs(first - code) <= jnp.abs(second * GRID - code)
    return jnp.where(near, first, -second).astype(BF16)


def decode_fine(sent):
    code = sent.astype(F32)
    return value_of(jnp.where(code < 0.0, code * (-GRID), code))


def in_vmem(array):
    return pltpu.with_memory_space_constraint(array, pltpu.VMEM)


def in_hbm(array):
    return pltpu.with_memory_space_constraint(array, pltpu.HBM)


def call(kernel, name, outs, hbm, vmem, scratch=()):
    single = not isinstance(outs, list)
    shapes = [pltpu.VMEM(shape, kind) for shape, kind in ([outs] if single else outs)]
    result = pl.pallas_call(
        kernel,
        out_shape=shapes,
        in_specs=[HBM] * len(hbm) + [VMEM] * len(vmem),
        out_specs=[VMEM] * len(shapes),
        scratch_shapes=list(scratch),
        compiler_params=pltpu.CompilerParams(vmem_limit_bytes=VMEM_LIMIT),
        cost_estimate=pl.CostEstimate(flops=1, bytes_accessed=1, transcendentals=0),
        name=name,
    )(*[in_hbm(a) for a in hbm], *[in_vmem(a) for a in vmem])
    return result[0] if single else result


def squared_transposed(g):
    g = g.astype(F32)
    return (g * g).T.astype(BF16)


def fisher_block(x, gt_ref):
    return jnp.dot(gt_ref[...], x * x, preferred_element_type=F32)


def where_am_i():
    tok, half, member = lax.axis_index("tok"), lax.axis_index("col"), lax.axis_index("member")
    return tok // 2, tok % 2, half, member // Z, member % Z


def load_inputs(member, pair, x_ref, x_out, sem):
    x, _, half, _, _ = where_am_i()
    wide = x_ref.shape[2] // 4
    copies = []
    for s, flip in enumerate(ORDER[pair]):
        owner = x ^ flip
        local = jnp.where(owner // 2 == half, 2 * (owner % 2), 2 * ((3 - owner) % 2) + 1)
        at = pl.multiple_of(local * wide, wide)
        source = x_ref.at[member, :, pl.ds(at, wide)]
        copies.append(pltpu.make_async_copy(source, x_out.at[:, pl.ds(s * wide, wide)], sem.at[s]))
        copies[s].start()
    return copies


def load_first_kernel(x_ref, g_ref, out, sem, g_sem):
    core = where_am_i()[1]
    outs = g_ref.shape[2]
    load = pltpu.make_async_copy(g_ref.at[1 - core], out.at[:, pl.ds(out.shape[1] - outs, outs)], g_sem)
    load.start()
    for copy in load_inputs(1 - core, 0, x_ref, out, sem) + [load]:
        copy.wait()


def load_second_kernel(x_ref, after, x_out, sem):
    for copy in load_inputs(1 - where_am_i()[1], 1, x_ref, x_out, sem):
        copy.wait()


def pair_kernel(own, got, after, out):
    outs = own.shape[1]
    out[0], out[1] = own[...], got[:, got.shape[1] - outs :]


def columns(s, x_ref, wide):
    return x_ref[:, s * wide : (s + 1) * wide]


def own_tokens(copies, x_out, gt_ref, part_out):
    for s in range(2):
        copies[s].wait()
        part_out[s] = fisher_block(columns(s, x_out, part_out.shape[2]), gt_ref)


def own_first_kernel(x_ref, g_ref, after, x_out, g_out, gt_out, part_out, sem, g_sem):
    core = where_am_i()[1]
    load = pltpu.make_async_copy(g_ref.at[core], g_out, g_sem)
    load.start()
    copies = load_inputs(core, 0, x_ref, x_out, sem)
    load.wait()
    gt_out[...] = squared_transposed(g_out[...])
    own_tokens(copies, x_out, gt_out, part_out)


def own_second_kernel(x_ref, gt_ref, after, x_out, part_out, sem):
    copies = load_inputs(where_am_i()[1], 1, x_ref, x_out, sem)
    own_tokens(copies, x_out, gt_ref, part_out)


def add_first_kernel(x_ref, part_ref, after, two_out, one_out, gt_out):
    wide, outs = part_ref.shape[2], part_ref.shape[1]
    gt_out[...] = squared_transposed(x_ref[:, 2 * wide :])
    for s, out in enumerate((two_out, one_out)):
        out[...] = encode(part_ref[s] + fisher_block(columns(s, x_ref, wide), gt_out))


def add_second_kernel(x_ref, gt_ref, part_ref, after, three_out, own_out):
    wide = part_ref.shape[2]
    three_out[...] = encode(part_ref[0] + fisher_block(columns(0, x_ref, wide), gt_ref))
    own_out[...] = part_ref[1] + fisher_block(columns(1, x_ref, wide), gt_ref)


def half_block(flip, part, x_refs, gt_refs, wide):
    pair = 0 if flip in ORDER[0] else 1
    at = (2 * ORDER[pair].index(flip) + part) * wide
    own, got = x_refs[2 * pair : 2 * pair + 2]
    return fisher_block(own[:, at : at + wide], gt_refs[0]) + fisher_block(got[:, at : at + wide], gt_refs[1])


def both_first_kernel(own_a, got_a, own_b, got_b, g_ref, after, sent_out, kept_out, gta_out, gtb_out):
    gta_out[...] = squared_transposed(g_ref[0])
    gtb_out[...] = squared_transposed(g_ref[1])
    for s, flip in enumerate((1, 2, 0, 3)):
        put(s, half_block(flip, 0, (own_a, got_a, own_b, got_b), (gta_out, gtb_out), sent_out.shape[2]), sent_out, kept_out)


def both_second_kernel(own_a, got_a, own_b, got_b, gta_ref, gtb_ref, after, sent_out, kept_out):
    for s, flip in enumerate((1, 2, 0, 3)):
        put(s, half_block(flip, 1, (own_a, got_a, own_b, got_b), (gta_ref, gtb_ref), sent_out.shape[2]), sent_out, kept_out)


def put(s, block, sent_out, kept_out):
    if s < 2:
        sent_out[s] = encode(block)
    else:
        kept_out[s - 2] = block


def middle_kernel(kept_ref, got_ref, after, sent_out, own_out):
    sent_out[...] = encode_fine(kept_ref[1] + decode(got_ref[1]))
    own_out[...] = kept_ref[0] + decode(got_ref[0])


def settle_kernel(own, got, after, out):
    out[...] = own[...] + decode_fine(got[...])


def join_kernel(first_ref, own, got, after, kept_out, sent_out):
    first = first_ref[...]
    second = own[...] + decode_fine(got[...])
    core = where_am_i()[1]
    kept_out[...] = jnp.where(core == 0, first, second)
    sent_out[...] = encode_fine(jnp.where(core == 0, second, first))


def join_direct_kernel(own, one, two, three, after, kept_out, sent_out):
    wide = kept_out.shape[1]
    halves = []
    for s in range(2):
        got = [decode(columns(s, ref, wide)) for ref in (one, two, three)]
        halves.append(columns(s, own, wide) + got[0] + got[1] + got[2])
    core = where_am_i()[1]
    kept_out[...] = jnp.where(core == 0, halves[0], halves[1])
    sent_out[...] = encode_fine(jnp.where(core == 0, halves[1], halves[0]))


def split_kernel(w_ref, after, own_out, send_out):
    rows, core = own_out.shape[1], where_am_i()[1]
    own_out[...] = w_ref[:, pl.ds(pl.multiple_of(core * rows, rows), rows), :]
    send_out[...] = w_ref[:, pl.ds(pl.multiple_of((1 - core) * rows, rows), rows), :]


def to_words(weighted, total, out):
    high = weighted.astype(BF16)
    out[0] = high
    out[1] = (weighted - high.astype(F32)).astype(BF16)
    out[2] = encode_fine(total)


def from_words(words):
    return words[0].astype(F32) + words[1].astype(F32), decode_fine(words[2])


def weigh_kernel(phase, own, other, w_own, w_other, after, one_out, two_out, three_out, sums_out):
    _, core, half, _, z = where_am_i()
    part = own.shape[1] // Z
    mine = (core ^ half ^ phase) == 0
    for d, out in ((2, two_out), (1, one_out), (3, three_out), (0, sums_out)):
        cols = pl.ds(pl.multiple_of((z + d) % Z * part, part), part)
        weighted = total = 0.0
        for values, m in ((own[:, cols], core), (decode_fine(other[:, cols]), 1 - core)):
            fisher = values.T
            weight = jnp.where(mine, w_own[m, cols, :].astype(F32), w_other[m, cols, :].astype(F32))
            weighted += fisher * weight
            total += fisher
        if d == 0:
            out[0], out[1] = weighted, total
        else:
            to_words(weighted, total, out)


def over_z(sums, words):
    weighted, total = sums[0], sums[1]
    for ref in words:
        more, added = from_words(ref)
        weighted += more
        total += added
    return weighted, total


def sum_kernel(one, two, three, sums, after, out):
    to_words(*over_z(sums, (one, two, three)), out)


def meet_kernel(near, far, after, out):
    (weighted, total), (more, added) = from_words(near), from_words(far)
    out[0], out[1] = weighted + more, total + added


def merge_kernel(near, far, sums, out):
    (weighted, total), (more, added) = from_words(near), from_words(far)
    out[...] = (weighted + more + sums[0]) / (total + added + sums[1])


def keeper(local, half):
    home = 2 * half + local // 2
    return home if local % 2 == 0 else 3 - home


def kept(x, half):
    return 2 * (x % 2) if x // 2 == half else 2 * ((3 - x) % 2) + 1


def weight_pairs(phase):
    pairs = []
    for tok in range(X * CORES):
        half, local = divmod(tok, 4)
        col = half ^ phase
        pairs.append((tok * 2 + col, (keeper(local, half) * 2 + col) * 2 + half))
    return pairs


def result_pairs(phase, sender):
    pairs = []
    for z in range(Z):
        for tok in range(X * CORES):
            x, core = divmod(tok, 2)
            for half in range(2):
                to_tok = 4 * half + kept(x, half)
                to = ((core * Z + z) * 8 + to_tok) * 2 + (half ^ phase)
                pairs.append((((sender * Z + z) * 8 + tok) * 2 + half, to))
    return pairs


def x_pairs(flip):
    return [(t, ((t // 2) ^ flip) * 2 + t % 2) for t in range(X * CORES)]


def z_pairs(distance):
    return [(m, m // Z * Z + (m + distance) % Z) for m in range(2 * Z)]


def shards(inputs, grads, weights):
    tokens, outs = grads.shape[1:]
    wide = inputs.shape[2] // 8
    x_shape, g_shape, gt_shape = ((tokens, 4 * wide), BF16), ((tokens, outs), BF16), ((outs, tokens), BF16)
    part_shape, sent_shape, sum_shape = ((2, outs, 2 * wide), F32), ((outs, 2 * wide), BF16), ((outs, 2 * wide), F32)
    code_shape, own_shape = ((outs, wide), BF16), ((outs, wide), F32)
    pair_shape, kept_shape = ((2, outs, wide), BF16), ((2, outs, wide), F32)
    words, sums = ((3, wide // Z, outs), BF16), ((2, wide // Z, outs), F32)
    dma = pltpu.SemaphoreType.DMA

    def swap_cores(send):
        return lax.ppermute(send, "tok", [(t, t ^ 1) for t in range(8)])

    def swap_cols(send):
        return lax.ppermute(send, "col", [(0, 1), (1, 0)])

    def swap_x(flip, sent):
        return lax.ppermute(sent, "tok", x_pairs(flip))

    def middle(flip, got, kept_blocks, after):
        sent, own = call(middle_kernel, "fisher_over_first_swap", [code_shape, own_shape], [], [kept_blocks, got, after])
        return own, swap_x(flip, sent)

    def settle(one, after):
        return call(settle_kernel, "fisher_over_tokens", own_shape, [], [*one, after])

    def join_direct(own, got, after):
        kept_block, sent = call(
            join_direct_kernel, "fisher_over_tokens", [own_shape, code_shape], [], [own, got[1], got[2], got[3], after]
        )
        return kept_block, swap_cores(sent)

    def join(first, two, after):
        kept_block, sent = call(join_kernel, "fisher_over_tokens", [own_shape, code_shape], [], [first, *two, after])
        return kept_block, swap_cores(sent)

    def results(phase, sums):
        return [lax.ppermute(sums, ("member", "tok", "col"), result_pairs(phase, y_lo)) for y_lo in range(2)]

    def bring_weights(phase, after):
        arrived = lax.ppermute(weights, ("tok", "col"), weight_pairs(phase))
        half_shape = ((2, weights.shape[1] // 2, outs), BF16)
        own, send = call(split_kernel, "split_weights", [half_shape, half_shape], [], [arrived, after])
        return own, swap_cores(send)

    def weigh(phase, own, other, moved, after):
        one, two, three, own_sums = call(
            lambda *refs: weigh_kernel(phase, *refs), "weigh_members", [words] * 3 + [sums], [], [own, other, *moved, after]
        )
        send = ((2, two), (1, one), (3, three))
        return [lax.ppermute(v, "member", z_pairs(d)) for d, v in send] + [own_sums]

    x_send0 = call(
        load_first_kernel, "load_to_swap", ((tokens, 4 * wide + outs), BF16), [inputs, grads], [], [dma((2,)), dma]
    )
    x_got0 = swap_cores(x_send0)
    x_send1 = call(load_second_kernel, "load_to_swap", x_shape, [inputs], [x_send0], [dma((2,))])
    x_got1 = swap_cores(x_send1)
    x_own0, g_own, gt_own, part0 = call(
        own_first_kernel, "fisher_of_own_tokens", [x_shape, g_shape, gt_shape, part_shape], [inputs, grads], [x_send1],
        [dma((2,)), dma],
    )
    g_pair = call(pair_kernel, "pair_grads", ((2, tokens, outs), BF16), [], [g_own, x_got0, gt_own])
    g_other = swap_cols(g_pair)
    two, one, gt_got = call(
        add_first_kernel, "fisher_of_both_cores", [sent_shape, sent_shape, gt_shape], [], [x_got0, part0, g_pair]
    )
    got0 = {2: swap_x(2, two), 1: swap_x(1, one)}
    x_own1, part1 = call(
        own_second_kernel, "fisher_of_own_tokens", [x_shape, part_shape], [inputs], [gt_own, two], [dma((2,))]
    )
    three, sum0 = call(
        add_second_kernel, "fisher_of_both_cores", [sent_shape, sum_shape], [], [x_got1, gt_got, part1, x_own1]
    )
    got0[3] = swap_x(3, three)

    xs = [x_own0, x_got0, x_own1, x_got1]
    sent, kept10, gt_own, gt_got = call(
        both_first_kernel, "fisher_of_other_grads", [pair_shape, kept_shape, gt_shape, gt_shape], [], [*xs, g_other, three]
    )
    swap10 = swap_x(1, sent)
    w0 = bring_weights(0, kept10)
    sent, kept11 = call(
        both_second_kernel, "fisher_of_other_grads", [pair_shape, kept_shape], [], [*xs, gt_own, gt_got, w0[0]]
    )
    swap11 = swap_x(1, sent)

    own0, other0 = join_direct(sum0, got0, kept11)
    words0 = weigh(0, own0, other0, w0, own0)
    part10 = middle(3, swap10, kept10, words0[3])
    first = call(sum_kernel, "sum_over_z", words, [], [*words0, part10[0]])
    part11 = middle(3, swap11, kept11, first)
    own1, other1 = join(settle(part10, part11[0]), part11, first)
    w1 = bring_weights(1, own1)
    words1 = weigh(1, own1, other1, w1, w1[0])
    met = call(meet_kernel, "meet_over_y", sums, [], [*results(0, first), own1])
    second = call(sum_kernel, "sum_over_z", words, [], [*words1, own1])
    near, far = results(1, second)
    return pl.pallas_call(
        merge_kernel,
        out_shape=jax.ShapeDtypeStruct((wide // Z, outs), F32),
        in_specs=[VMEM] * 3,
        out_specs=VMEM,
        compiler_params=pltpu.CompilerParams(vmem_limit_bytes=VMEM_LIMIT),
        name="merge_members",
    )(in_vmem(near), in_vmem(far), in_vmem(met))


def solution(mesh):
    in_specs = (P("member", "tok", "col"), P("member", "tok", "col"), P("member", "tok", "col"))
    out_specs = P(("tok", "member"), "col")
    return jax.shard_map(shards, mesh=mesh, in_specs=in_specs, out_specs=out_specs, check_vma=False)
```

```python
import jax
import jax.numpy as jnp
from jax import lax
from jax.experimental import pallas as pl
from jax.experimental.pallas import tpu as pltpu
from jax.sharding import PartitionSpec as P

F32 = jnp.float32
BF16 = jnp.bfloat16
HBM = pl.BlockSpec(memory_space=pltpu.HBM)
VMEM = pl.BlockSpec(memory_space=pltpu.VMEM)
VMEM_LIMIT = 16 << 20

GRID = 1.00297
BIG = 2.0**28
SMALL = 2.0**16
EDGE = 2.0**-40
EDGE_CODE = 2.0**-24

X, CORES, Z = 4, 2, 4

ORDER = ((2, 1), (3, 0))


def code_of(values):
    scaled = values * BIG
    return jnp.where(values >= EDGE, scaled * scaled, values * SMALL)


def value_of(code):
    return jnp.where(code >= EDGE_CODE, jnp.sqrt(code) * (1.0 / BIG), code * (1.0 / SMALL))


def encode(values):
    return code_of(values).astype(BF16)


def decode(sent):
    return value_of(sent.astype(F32))


def encode_fine(values):
    code = code_of(values)
    first = code.astype(BF16).astype(F32)
    second = (code * (1.0 / GRID)).astype(BF16).astype(F32)
    near = jnp.abs(first - code) <= jnp.abs(second * GRID - code)
    return jnp.where(near, first, -second).astype(BF16)


def decode_fine(sent):
    code = sent.astype(F32)
    return value_of(jnp.where(code < 0.0, code * (-GRID), code))


def in_vmem(array):
    return pltpu.with_memory_space_constraint(array, pltpu.VMEM)


def in_hbm(array):
    return pltpu.with_memory_space_constraint(array, pltpu.HBM)


def call(kernel, name, outs, hbm, vmem, scratch=()):
    single = not isinstance(outs, list)
    shapes = [pltpu.VMEM(shape, kind) for shape, kind in ([outs] if single else outs)]
    result = pl.pallas_call(
        kernel,
        out_shape=shapes,
        in_specs=[HBM] * len(hbm) + [VMEM] * len(vmem),
        out_specs=[VMEM] * len(shapes),
        scratch_shapes=list(scratch),
        compiler_params=pltpu.CompilerParams(vmem_limit_bytes=VMEM_LIMIT),
        cost_estimate=pl.CostEstimate(flops=1, bytes_accessed=1, transcendentals=0),
        name=name,
    )(*[in_hbm(a) for a in hbm], *[in_vmem(a) for a in vmem])
    return result[0] if single else result


def squared_transposed(g):
    g = g.astype(F32)
    return (g * g).T.astype(BF16)


def fisher_block(x, gt_ref):
    return jnp.dot(gt_ref[...], x * x, preferred_element_type=F32)


def where_am_i():
    tok, half, member = lax.axis_index("tok"), lax.axis_index("col"), lax.axis_index("member")
    return tok // 2, tok % 2, half, member // Z, member % Z


def load_inputs(member, pair, x_ref, x_out, sem):
    x, _, half, _, _ = where_am_i()
    wide = x_ref.shape[2] // 4
    copies = []
    for s, flip in enumerate(ORDER[pair]):
        owner = x ^ flip
        local = jnp.where(owner // 2 == half, 2 * (owner % 2), 2 * ((3 - owner) % 2) + 1)
        at = pl.multiple_of(local * wide, wide)
        source = x_ref.at[member, :, pl.ds(at, wide)]
        copies.append(pltpu.make_async_copy(source, x_out.at[:, pl.ds(s * wide, wide)], sem.at[s]))
        copies[s].start()
    return copies


def load_first_kernel(x_ref, g_ref, out, sem, g_sem):
    core = where_am_i()[1]
    outs = g_ref.shape[2]
    load = pltpu.make_async_copy(g_ref.at[1 - core], out.at[:, pl.ds(out.shape[1] - outs, outs)], g_sem)
    load.start()
    for copy in load_inputs(1 - core, 0, x_ref, out, sem) + [load]:
        copy.wait()


def load_second_kernel(x_ref, after, x_out, sem):
    for copy in load_inputs(1 - where_am_i()[1], 1, x_ref, x_out, sem):
        copy.wait()


def pair_kernel(own, got, after, out):
    outs = own.shape[1]
    out[0], out[1] = own[...], got[:, got.shape[1] - outs :]


def columns(s, x_ref, wide):
    return x_ref[:, s * wide : (s + 1) * wide]


def own_tokens(copies, x_out, gt_ref, part_out):
    for s in range(2):
        copies[s].wait()
        part_out[s] = fisher_block(columns(s, x_out, part_out.shape[2]), gt_ref)


def own_first_kernel(x_ref, g_ref, after, x_out, g_out, gt_out, part_out, sem, g_sem):
    core = where_am_i()[1]
    load = pltpu.make_async_copy(g_ref.at[core], g_out, g_sem)
    load.start()
    copies = load_inputs(core, 0, x_ref, x_out, sem)
    load.wait()
    gt_out[...] = squared_transposed(g_out[...])
    own_tokens(copies, x_out, gt_out, part_out)


def own_second_kernel(x_ref, gt_ref, after, x_out, part_out, sem):
    copies = load_inputs(where_am_i()[1], 1, x_ref, x_out, sem)
    own_tokens(copies, x_out, gt_ref, part_out)


def add_first_kernel(x_ref, part_ref, after, two_out, one_out, gt_out):
    wide, outs = part_ref.shape[2], part_ref.shape[1]
    gt_out[...] = squared_transposed(x_ref[:, 2 * wide :])
    for s, out in enumerate((two_out, one_out)):
        out[...] = encode(part_ref[s] + fisher_block(columns(s, x_ref, wide), gt_out))


def add_second_kernel(x_ref, gt_ref, part_ref, after, three_out, own_out):
    wide = part_ref.shape[2]
    three_out[...] = encode(part_ref[0] + fisher_block(columns(0, x_ref, wide), gt_ref))
    own_out[...] = part_ref[1] + fisher_block(columns(1, x_ref, wide), gt_ref)


def half_block(flip, part, x_refs, gt_refs, wide):
    pair = 0 if flip in ORDER[0] else 1
    at = (2 * ORDER[pair].index(flip) + part) * wide
    own, got = x_refs[2 * pair : 2 * pair + 2]
    return fisher_block(own[:, at : at + wide], gt_refs[0]) + fisher_block(got[:, at : at + wide], gt_refs[1])


def both_first_kernel(own_a, got_a, own_b, got_b, g_ref, after, sent_out, kept_out, gta_out, gtb_out):
    gta_out[...] = squared_transposed(g_ref[0])
    gtb_out[...] = squared_transposed(g_ref[1])
    for s, flip in enumerate((1, 2, 0, 3)):
        put(s, half_block(flip, 0, (own_a, got_a, own_b, got_b), (gta_out, gtb_out), sent_out.shape[2]), sent_out, kept_out)


def both_second_kernel(own_a, got_a, own_b, got_b, gta_ref, gtb_ref, after, sent_out, kept_out):
    for s, flip in enumerate((3, 2, 0, 1)):
        put(s, half_block(flip, 1, (own_a, got_a, own_b, got_b), (gta_ref, gtb_ref), sent_out.shape[2]), sent_out, kept_out)


def put(s, block, sent_out, kept_out):
    if s < 2:
        sent_out[s] = encode(block)
    else:
        kept_out[s - 2] = block


def middle_kernel(kept_ref, got_ref, after, sent_out, own_out):
    sent_out[...] = encode_fine(kept_ref[1] + decode(got_ref[1]))
    own_out[...] = kept_ref[0] + decode(got_ref[0])


def settle_kernel(own, got, after, out):
    out[...] = own[...] + decode_fine(got[...])


def join_kernel(first_ref, own, got, after, kept_out, sent_out):
    first = first_ref[...]
    second = own[...] + decode_fine(got[...])
    core = where_am_i()[1]
    kept_out[...] = jnp.where(core == 0, first, second)
    sent_out[...] = encode_fine(jnp.where(core == 0, second, first))


def join_direct_kernel(own, one, two, three, after, kept_out, sent_out):
    wide = kept_out.shape[1]
    halves = []
    for s in range(2):
        got = [decode(columns(s, ref, wide)) for ref in (one, two, three)]
        halves.append(columns(s, own, wide) + got[0] + got[1] + got[2])
    core = where_am_i()[1]
    kept_out[...] = jnp.where(core == 0, halves[0], halves[1])
    sent_out[...] = encode_fine(jnp.where(core == 0, halves[1], halves[0]))


def load_weights_kernel(w_ref, after, out, sem):
    copy = pltpu.make_async_copy(w_ref, out, sem)
    copy.start()
    copy.wait()


def split_kernel(w_ref, after, own_out, send_out):
    rows, core = own_out.shape[1], where_am_i()[1]
    own_out[...] = w_ref[:, pl.ds(pl.multiple_of(core * rows, rows), rows), :]
    send_out[...] = w_ref[:, pl.ds(pl.multiple_of((1 - core) * rows, rows), rows), :]


def to_words(weighted, total, out):
    high = weighted.astype(BF16)
    out[0] = high
    out[1] = (weighted - high.astype(F32)).astype(BF16)
    out[2] = encode_fine(total)


def from_words(words):
    return words[0].astype(F32) + words[1].astype(F32), decode_fine(words[2])


def weigh_kernel(phase, own, other, w_own, w_other, after, one_out, two_out, three_out, sums_out):
    _, core, half, _, z = where_am_i()
    part = own.shape[1] // Z
    mine = (core ^ half ^ phase) == 0
    for d, out in ((2, two_out), (1, one_out), (3, three_out), (0, sums_out)):
        cols = pl.ds(pl.multiple_of((z + d) % Z * part, part), part)
        weighted = total = 0.0
        for values, m in ((own[:, cols], core), (decode_fine(other[:, cols]), 1 - core)):
            fisher = values.T
            weight = jnp.where(mine, w_own[m, cols, :].astype(F32), w_other[m, cols, :].astype(F32))
            weighted += fisher * weight
            total += fisher
        if d == 0:
            out[0], out[1] = weighted, total
        else:
            to_words(weighted, total, out)


def over_z(sums, words):
    weighted, total = sums[0], sums[1]
    for ref in words:
        more, added = from_words(ref)
        weighted += more
        total += added
    return weighted, total


def sum_kernel(one, two, three, sums, after, out):
    to_words(*over_z(sums, (one, two, three)), out)


def meet_kernel(near, far, after, out):
    (weighted, total), (more, added) = from_words(near), from_words(far)
    out[0], out[1] = weighted + more, total + added


def merge_kernel(near, far, sums, out):
    (weighted, total), (more, added) = from_words(near), from_words(far)
    out[...] = (weighted + more + sums[0]) / (total + added + sums[1])


def keeper(local, half):
    home = 2 * half + local // 2
    return home if local % 2 == 0 else 3 - home


def kept(x, half):
    return 2 * (x % 2) if x // 2 == half else 2 * ((3 - x) % 2) + 1


def weight_pairs(phase):
    pairs = []
    for tok in range(X * CORES):
        half, local = divmod(tok, 4)
        col = half ^ phase
        pairs.append((tok * 2 + col, (keeper(local, half) * 2 + col) * 2 + half))
    return pairs


def result_pairs(phase, sender):
    pairs = []
    for z in range(Z):
        for tok in range(X * CORES):
            x, core = divmod(tok, 2)
            for half in range(2):
                to_tok = 4 * half + kept(x, half)
                to = ((core * Z + z) * 8 + to_tok) * 2 + (half ^ phase)
                pairs.append((((sender * Z + z) * 8 + tok) * 2 + half, to))
    return pairs


def x_pairs(flip):
    return [(t, ((t // 2) ^ flip) * 2 + t % 2) for t in range(X * CORES)]


def z_pairs(distance):
    return [(m, m // Z * Z + (m + distance) % Z) for m in range(2 * Z)]


def shards(inputs, grads, weights):
    tokens, outs = grads.shape[1:]
    wide = inputs.shape[2] // 8
    x_shape, g_shape, gt_shape = ((tokens, 4 * wide), BF16), ((tokens, outs), BF16), ((outs, tokens), BF16)
    part_shape, sent_shape, sum_shape = ((2, outs, 2 * wide), F32), ((outs, 2 * wide), BF16), ((outs, 2 * wide), F32)
    code_shape, own_shape = ((outs, wide), BF16), ((outs, wide), F32)
    pair_shape, kept_shape = ((2, outs, wide), BF16), ((2, outs, wide), F32)
    words, sums = ((3, wide // Z, outs), BF16), ((2, wide // Z, outs), F32)
    dma = pltpu.SemaphoreType.DMA

    def swap_cores(send):
        return lax.ppermute(send, "tok", [(t, t ^ 1) for t in range(8)])

    def swap_cols(send):
        return lax.ppermute(send, "col", [(0, 1), (1, 0)])

    def swap_x(flip, sent):
        return lax.ppermute(sent, "tok", x_pairs(flip))

    def middle(flip, got, kept_blocks, after):
        sent, own = call(middle_kernel, "fisher_over_first_swap", [code_shape, own_shape], [], [kept_blocks, got, after])
        return own, swap_x(flip, sent)

    def settle(one, after):
        return call(settle_kernel, "fisher_over_tokens", own_shape, [], [*one, after])

    def join_direct(own, got, after):
        kept_block, sent = call(
            join_direct_kernel, "fisher_over_tokens", [own_shape, code_shape], [], [own, got[1], got[2], got[3], after]
        )
        return kept_block, swap_cores(sent)

    def join(first, two, after):
        kept_block, sent = call(join_kernel, "fisher_over_tokens", [own_shape, code_shape], [], [first, *two, after])
        return kept_block, swap_cores(sent)

    def results(phase, sums):
        return [lax.ppermute(sums, ("member", "tok", "col"), result_pairs(phase, y_lo)) for y_lo in range(2)]

    def bring_weights(phase, source, after):
        arrived = lax.ppermute(source, ("tok", "col"), weight_pairs(phase))
        half_shape = ((2, weights.shape[1] // 2, outs), BF16)
        own, send = call(split_kernel, "split_weights", [half_shape, half_shape], [], [arrived, after])
        return own, swap_cores(send)

    def weigh(phase, own, other, moved, after):
        one, two, three, own_sums = call(
            lambda *refs: weigh_kernel(phase, *refs), "weigh_members", [words] * 3 + [sums], [], [own, other, *moved, after]
        )
        send = ((2, two), (1, one), (3, three))
        return [lax.ppermute(v, "member", z_pairs(d)) for d, v in send] + [own_sums]

    x_send0 = call(
        load_first_kernel, "load_to_swap", ((tokens, 4 * wide + outs), BF16), [inputs, grads], [], [dma((2,)), dma]
    )
    x_got0 = swap_cores(x_send0)
    x_send1 = call(load_second_kernel, "load_to_swap", x_shape, [inputs], [x_send0], [dma((2,))])
    x_got1 = swap_cores(x_send1)
    x_own0, g_own, gt_own, part0 = call(
        own_first_kernel, "fisher_of_own_tokens", [x_shape, g_shape, gt_shape, part_shape], [inputs, grads], [x_send1],
        [dma((2,)), dma],
    )
    g_pair = call(pair_kernel, "pair_grads", ((2, tokens, outs), BF16), [], [g_own, x_got0, gt_own])
    g_other = swap_cols(g_pair)
    two, one, gt_got = call(
        add_first_kernel, "fisher_of_both_cores", [sent_shape, sent_shape, gt_shape], [], [x_got0, part0, g_pair]
    )
    got0 = {2: swap_x(2, two), 1: swap_x(1, one)}
    x_own1, part1 = call(
        own_second_kernel, "fisher_of_own_tokens", [x_shape, part_shape], [inputs], [gt_own, two], [dma((2,))]
    )
    three, sum0 = call(
        add_second_kernel, "fisher_of_both_cores", [sent_shape, sum_shape], [], [x_got1, gt_got, part1, x_own1]
    )
    got0[3] = swap_x(3, three)

    xs = [x_own0, x_got0, x_own1, x_got1]
    sent, kept10, gt_own, gt_got = call(
        both_first_kernel, "fisher_of_other_grads", [pair_shape, kept_shape, gt_shape, gt_shape], [], [*xs, g_other, three]
    )
    swap10 = swap_x(1, sent)
    w0 = bring_weights(0, weights, kept10)
    sent, kept11 = call(
        both_second_kernel, "fisher_of_other_grads", [pair_shape, kept_shape], [], [*xs, gt_own, gt_got, w0[0]]
    )
    swap11 = swap_x(3, sent)
    late_weights = call(load_weights_kernel, "load_weights", (weights.shape, BF16), [weights], [kept11], [dma])

    own0, other0 = join_direct(sum0, got0, kept11)
    words0 = weigh(0, own0, other0, w0, own0)
    part10 = middle(3, swap10, kept10, words0[3])
    first = call(sum_kernel, "sum_over_z", words, [], [*words0, part10[0]])
    part11 = middle(1, swap11, kept11, first)
    own1, other1 = join(settle(part10, part11[0]), part11, first)
    w1 = bring_weights(1, late_weights, own1)
    words1 = weigh(1, own1, other1, w1, w1[0])
    met = call(meet_kernel, "meet_over_y", sums, [], [*results(0, first), own1])
    second = call(sum_kernel, "sum_over_z", words, [], [*words1, own1])
    near, far = results(1, second)
    return pl.pallas_call(
        merge_kernel,
        out_shape=jax.ShapeDtypeStruct((wide // Z, outs), F32),
        in_specs=[VMEM] * 3,
        out_specs=VMEM,
        compiler_params=pltpu.CompilerParams(vmem_limit_bytes=VMEM_LIMIT),
        name="merge_members",
    )(in_vmem(near), in_vmem(far), in_vmem(met))


def solution(mesh):
    in_specs = (P("member", "tok", "col"), P("member", "tok", "col"), P("member", "tok", "col"))
    out_specs = P(("tok", "member"), "col")
    return jax.shard_map(shards, mesh=mesh, in_specs=in_specs, out_specs=out_specs, check_vma=False)
```

```python
import jax
import jax.numpy as jnp
from jax import lax
from jax.experimental import pallas as pl
from jax.experimental.pallas import tpu as pltpu
from jax.sharding import PartitionSpec as P

F32 = jnp.float32
BF16 = jnp.bfloat16
HBM = pl.BlockSpec(memory_space=pltpu.HBM)
VMEM = pl.BlockSpec(memory_space=pltpu.VMEM)
VMEM_LIMIT = 16 << 20

GRID = 1.00297
BIG = 2.0**28
SMALL = 2.0**16
EDGE = 2.0**-40
EDGE_CODE = 2.0**-24

X, CORES, Z = 4, 2, 4

ORDER = ((2, 1), (3, 0))


def code_of(values):
    scaled = values * BIG
    return jnp.where(values >= EDGE, scaled * scaled, values * SMALL)


def value_of(code):
    return jnp.where(code >= EDGE_CODE, jnp.sqrt(code) * (1.0 / BIG), code * (1.0 / SMALL))


def encode(values):
    return code_of(values).astype(BF16)


def decode(sent):
    return value_of(sent.astype(F32))


def encode_fine(values):
    code = code_of(values)
    first = code.astype(BF16).astype(F32)
    second = (code * (1.0 / GRID)).astype(BF16).astype(F32)
    near = jnp.abs(first - code) <= jnp.abs(second * GRID - code)
    return jnp.where(near, first, -second).astype(BF16)


def decode_fine(sent):
    code = sent.astype(F32)
    return value_of(jnp.where(code < 0.0, code * (-GRID), code))


def in_vmem(array):
    return pltpu.with_memory_space_constraint(array, pltpu.VMEM)


def in_hbm(array):
    return pltpu.with_memory_space_constraint(array, pltpu.HBM)


def call(kernel, name, outs, hbm, vmem, scratch=()):
    single = not isinstance(outs, list)
    shapes = [pltpu.VMEM(shape, kind) for shape, kind in ([outs] if single else outs)]
    result = pl.pallas_call(
        kernel,
        out_shape=shapes,
        in_specs=[HBM] * len(hbm) + [VMEM] * len(vmem),
        out_specs=[VMEM] * len(shapes),
        scratch_shapes=list(scratch),
        compiler_params=pltpu.CompilerParams(vmem_limit_bytes=VMEM_LIMIT),
        cost_estimate=pl.CostEstimate(flops=1, bytes_accessed=1, transcendentals=0),
        name=name,
    )(*[in_hbm(a) for a in hbm], *[in_vmem(a) for a in vmem])
    return result[0] if single else result


def squared_transposed(g):
    g = g.astype(F32)
    return (g * g).T.astype(BF16)


def fisher_block(x, gt_ref):
    return jnp.dot(gt_ref[...], x * x, preferred_element_type=F32)


def where_am_i():
    tok, half, member = lax.axis_index("tok"), lax.axis_index("col"), lax.axis_index("member")
    return tok // 2, tok % 2, half, member // Z, member % Z


def load_inputs(member, pair, x_ref, x_out, sem):
    x, _, half, _, _ = where_am_i()
    wide = x_ref.shape[2] // 4
    copies = []
    for s, flip in enumerate(ORDER[pair]):
        owner = x ^ flip
        local = jnp.where(owner // 2 == half, 2 * (owner % 2), 2 * ((3 - owner) % 2) + 1)
        at = pl.multiple_of(local * wide, wide)
        source = x_ref.at[member, :, pl.ds(at, wide)]
        copies.append(pltpu.make_async_copy(source, x_out.at[:, pl.ds(s * wide, wide)], sem.at[s]))
        copies[s].start()
    return copies


def load_first_kernel(x_ref, g_ref, out, sem, g_sem):
    core = where_am_i()[1]
    outs = g_ref.shape[2]
    load = pltpu.make_async_copy(g_ref.at[1 - core], out.at[:, pl.ds(out.shape[1] - outs, outs)], g_sem)
    load.start()
    for copy in load_inputs(1 - core, 0, x_ref, out, sem) + [load]:
        copy.wait()


def load_second_kernel(x_ref, after, x_out, sem):
    for copy in load_inputs(1 - where_am_i()[1], 1, x_ref, x_out, sem):
        copy.wait()


def pair_kernel(own, got, after, out):
    outs = own.shape[1]
    out[0], out[1] = own[...], got[:, got.shape[1] - outs :]


def columns(s, x_ref, wide):
    return x_ref[:, s * wide : (s + 1) * wide]


def own_tokens(copies, x_out, gt_ref, part_out):
    for s in range(2):
        copies[s].wait()
        part_out[s] = fisher_block(columns(s, x_out, part_out.shape[2]), gt_ref)


def own_first_kernel(x_ref, g_ref, after, x_out, g_out, gt_out, part_out, sem, g_sem):
    core = where_am_i()[1]
    load = pltpu.make_async_copy(g_ref.at[core], g_out, g_sem)
    load.start()
    copies = load_inputs(core, 0, x_ref, x_out, sem)
    load.wait()
    gt_out[...] = squared_transposed(g_out[...])
    own_tokens(copies, x_out, gt_out, part_out)


def own_second_kernel(x_ref, gt_ref, after, x_out, part_out, sem):
    copies = load_inputs(where_am_i()[1], 1, x_ref, x_out, sem)
    own_tokens(copies, x_out, gt_ref, part_out)


def add_first_kernel(x_ref, part_ref, after, two_out, one_out, gt_out):
    wide, outs = part_ref.shape[2], part_ref.shape[1]
    gt_out[...] = squared_transposed(x_ref[:, 2 * wide :])
    for s, out in enumerate((two_out, one_out)):
        out[...] = encode(part_ref[s] + fisher_block(columns(s, x_ref, wide), gt_out))


def add_second_kernel(x_ref, gt_ref, part_ref, after, three_out, own_out):
    wide = part_ref.shape[2]
    three_out[...] = encode(part_ref[0] + fisher_block(columns(0, x_ref, wide), gt_ref))
    own_out[...] = part_ref[1] + fisher_block(columns(1, x_ref, wide), gt_ref)


def half_block(flip, part, x_refs, gt_refs, wide):
    pair = 0 if flip in ORDER[0] else 1
    at = (2 * ORDER[pair].index(flip) + part) * wide
    own, got = x_refs[2 * pair : 2 * pair + 2]
    return fisher_block(own[:, at : at + wide], gt_refs[0]) + fisher_block(got[:, at : at + wide], gt_refs[1])


def both_first_kernel(own_a, got_a, own_b, got_b, g_ref, after, sent_out, kept_out, gta_out, gtb_out):
    gta_out[...] = squared_transposed(g_ref[0])
    gtb_out[...] = squared_transposed(g_ref[1])
    for s, flip in enumerate((1, 2, 0, 3)):
        put(s, half_block(flip, 0, (own_a, got_a, own_b, got_b), (gta_out, gtb_out), sent_out.shape[2]), sent_out, kept_out)


def both_second_kernel(own_a, got_a, own_b, got_b, gta_ref, gtb_ref, after, sent_out, kept_out):
    for s, flip in enumerate((3, 2, 0, 1)):
        put(s, half_block(flip, 1, (own_a, got_a, own_b, got_b), (gta_ref, gtb_ref), sent_out.shape[2]), sent_out, kept_out)


def put(s, block, sent_out, kept_out):
    if s < 2:
        sent_out[s] = encode(block)
    else:
        kept_out[s - 2] = block


def middle_kernel(kept_ref, got_ref, after, sent_out, own_out):
    sent_out[...] = encode_fine(kept_ref[1] + decode(got_ref[1]))
    own_out[...] = kept_ref[0] + decode(got_ref[0])


def settle_kernel(own, got, after, out):
    out[...] = own[...] + decode_fine(got[...])


def join_kernel(first_ref, own, got, after, kept_out, sent_out):
    first = first_ref[...]
    second = own[...] + decode_fine(got[...])
    core = where_am_i()[1]
    kept_out[...] = jnp.where(core == 0, first, second)
    sent_out[...] = encode_fine(jnp.where(core == 0, second, first))


def join_direct_kernel(own, one, two, three, after, kept_out, sent_out):
    wide = kept_out.shape[1]
    halves = []
    for s in range(2):
        got = [decode(columns(s, ref, wide)) for ref in (one, two, three)]
        halves.append(columns(s, own, wide) + got[0] + got[1] + got[2])
    core = where_am_i()[1]
    kept_out[...] = jnp.where(core == 0, halves[0], halves[1])
    sent_out[...] = encode_fine(jnp.where(core == 0, halves[1], halves[0]))


def split_kernel(w_ref, after, own_out, send_out):
    rows, core = own_out.shape[1], where_am_i()[1]
    own_out[...] = w_ref[:, pl.ds(pl.multiple_of(core * rows, rows), rows), :]
    send_out[...] = w_ref[:, pl.ds(pl.multiple_of((1 - core) * rows, rows), rows), :]


def to_words(weighted, total, out):
    high = weighted.astype(BF16)
    out[0] = high
    out[1] = (weighted - high.astype(F32)).astype(BF16)
    out[2] = encode_fine(total)


def from_words(words):
    return words[0].astype(F32) + words[1].astype(F32), decode_fine(words[2])


def weigh_kernel(phase, own, other, w_own, w_other, after, one_out, two_out, three_out, sums_out):
    _, core, half, _, z = where_am_i()
    part = own.shape[1] // Z
    mine = (core ^ half ^ phase) == 0
    for d, out in ((2, two_out), (1, one_out), (3, three_out), (0, sums_out)):
        cols = pl.ds(pl.multiple_of((z + d) % Z * part, part), part)
        weighted = total = 0.0
        for values, m in ((own[:, cols], core), (decode_fine(other[:, cols]), 1 - core)):
            fisher = values.T
            weight = jnp.where(mine, w_own[m, cols, :].astype(F32), w_other[m, cols, :].astype(F32))
            weighted += fisher * weight
            total += fisher
        if d == 0 or phase == 0:
            out[0, :part], out[1, :part] = weighted, total
        else:
            to_words(weighted, total, out)


def over_z(sums, words):
    weighted, total = sums[0], sums[1]
    for ref in words:
        more, added = from_words(ref)
        weighted += more
        total += added
    return weighted, total


def sum_wide_kernel(one, two, three, sums, after, out):
    part = sums.shape[1]
    weighted, total = sums[0], sums[1]
    for ref in (one, two, three):
        weighted += ref[0, :part]
        total += ref[1, :part]
    to_words(weighted, total, out)


def sum_kernel(one, two, three, sums, after, out):
    to_words(*over_z(sums, (one, two, three)), out)


def meet_kernel(near, far, after, out):
    (weighted, total), (more, added) = from_words(near), from_words(far)
    out[0], out[1] = weighted + more, total + added


def merge_kernel(near, far, sums, out):
    (weighted, total), (more, added) = from_words(near), from_words(far)
    out[...] = (weighted + more + sums[0]) / (total + added + sums[1])


def keeper(local, half):
    home = 2 * half + local // 2
    return home if local % 2 == 0 else 3 - home


def kept(x, half):
    return 2 * (x % 2) if x // 2 == half else 2 * ((3 - x) % 2) + 1


def weight_pairs():
    pairs = []
    for tok in range(X * CORES):
        half, local = divmod(tok, 4)
        for col in range(2):
            pairs.append((tok * 2 + col, (keeper(local, half) * 2 + col) * 2 + half))
    return pairs


def result_pairs(phase, sender):
    pairs = []
    for z in range(Z):
        for tok in range(X * CORES):
            x, core = divmod(tok, 2)
            for half in range(2):
                to_tok = 4 * half + kept(x, half)
                to = ((core * Z + z) * 8 + to_tok) * 2 + (half ^ phase)
                pairs.append((((sender * Z + z) * 8 + tok) * 2 + half, to))
    return pairs


def x_pairs(flip):
    return [(t, ((t // 2) ^ flip) * 2 + t % 2) for t in range(X * CORES)]


def z_pairs(distance):
    return [(m, m // Z * Z + (m + distance) % Z) for m in range(2 * Z)]


def shards(inputs, grads, weights):
    tokens, outs = grads.shape[1:]
    wide = inputs.shape[2] // 8
    x_shape, g_shape, gt_shape = ((tokens, 4 * wide), BF16), ((tokens, outs), BF16), ((outs, tokens), BF16)
    part_shape, sent_shape, sum_shape = ((2, outs, 2 * wide), F32), ((outs, 2 * wide), BF16), ((outs, 2 * wide), F32)
    code_shape, own_shape = ((outs, wide), BF16), ((outs, wide), F32)
    pair_shape, kept_shape = ((2, outs, wide), BF16), ((2, outs, wide), F32)
    wide_words = ((2, wide // Z, outs), F32)
    words, sums = ((3, wide // Z, outs), BF16), ((2, wide // Z, outs), F32)
    dma = pltpu.SemaphoreType.DMA

    def swap_cores(send):
        return lax.ppermute(send, "tok", [(t, t ^ 1) for t in range(8)])

    def swap_cols(send):
        return lax.ppermute(send, "col", [(0, 1), (1, 0)])

    def swap_x(flip, sent):
        return lax.ppermute(sent, "tok", x_pairs(flip))

    def middle(flip, got, kept_blocks, after):
        sent, own = call(middle_kernel, "fisher_over_first_swap", [code_shape, own_shape], [], [kept_blocks, got, after])
        return own, swap_x(flip, sent)

    def settle(one, after):
        return call(settle_kernel, "fisher_over_tokens", own_shape, [], [*one, after])

    def join_direct(own, got, after):
        kept_block, sent = call(
            join_direct_kernel, "fisher_over_tokens", [own_shape, code_shape], [], [own, got[1], got[2], got[3], after]
        )
        return kept_block, swap_cores(sent)

    def join(first, two, after):
        kept_block, sent = call(join_kernel, "fisher_over_tokens", [own_shape, code_shape], [], [first, *two, after])
        return kept_block, swap_cores(sent)

    def results(phase, sums):
        return [lax.ppermute(sums, ("member", "tok", "col"), result_pairs(phase, y_lo)) for y_lo in range(2)]

    def bring_weights(after):
        arrived = lax.ppermute(weights, ("tok", "col"), weight_pairs())
        half_shape = ((2, weights.shape[1] // 2, outs), BF16)
        own, send = call(split_kernel, "split_weights", [half_shape, half_shape], [], [arrived, after])
        return own, swap_cores(send)

    def weigh(phase, own, other, moved, after):
        one, two, three, own_sums = call(
            lambda *refs: weigh_kernel(phase, *refs), "weigh_members", [words if phase else wide_words] * 3 + [sums], [], [own, other, *moved, after]
        )
        send = ((2, two), (1, one), (3, three))
        return [lax.ppermute(v, "member", z_pairs(d)) for d, v in send] + [own_sums]

    x_send0 = call(
        load_first_kernel, "load_to_swap", ((tokens, 4 * wide + outs), BF16), [inputs, grads], [], [dma((2,)), dma]
    )
    x_got0 = swap_cores(x_send0)
    x_send1 = call(load_second_kernel, "load_to_swap", x_shape, [inputs], [x_send0], [dma((2,))])
    x_got1 = swap_cores(x_send1)
    x_own0, g_own, gt_own, part0 = call(
        own_first_kernel, "fisher_of_own_tokens", [x_shape, g_shape, gt_shape, part_shape], [inputs, grads], [x_send1],
        [dma((2,)), dma],
    )
    g_pair = call(pair_kernel, "pair_grads", ((2, tokens, outs), BF16), [], [g_own, x_got0, gt_own])
    g_other = swap_cols(g_pair)
    two, one, gt_got = call(
        add_first_kernel, "fisher_of_both_cores", [sent_shape, sent_shape, gt_shape], [], [x_got0, part0, g_pair]
    )
    got0 = {2: swap_x(2, two), 1: swap_x(1, one)}
    x_own1, part1 = call(
        own_second_kernel, "fisher_of_own_tokens", [x_shape, part_shape], [inputs], [gt_own, two], [dma((2,))]
    )
    three, sum0 = call(
        add_second_kernel, "fisher_of_both_cores", [sent_shape, sum_shape], [], [x_got1, gt_got, part1, x_own1]
    )
    got0[3] = swap_x(3, three)

    xs = [x_own0, x_got0, x_own1, x_got1]
    sent, kept10, gt_own, gt_got = call(
        both_first_kernel, "fisher_of_other_grads", [pair_shape, kept_shape, gt_shape, gt_shape], [], [*xs, g_other, three]
    )
    swap10 = swap_x(1, sent)
    moved = bring_weights(kept10)
    sent, kept11 = call(
        both_second_kernel, "fisher_of_other_grads", [pair_shape, kept_shape], [], [*xs, gt_own, gt_got, moved[0]]
    )
    swap11 = swap_x(3, sent)

    own0, other0 = join_direct(sum0, got0, kept11)
    words0 = weigh(0, own0, other0, moved, own0)
    part10 = middle(3, swap10, kept10, words0[3])
    part11 = middle(1, swap11, kept11, part10[0])
    first = call(sum_wide_kernel, "sum_over_z", words, [], [*words0, part11[0]])
    own1, other1 = join(settle(part10, first), part11, first)
    words1 = weigh(1, own1, other1, moved, own1)
    met = call(meet_kernel, "meet_over_y", sums, [], [*results(0, first), own1])
    second = call(sum_kernel, "sum_over_z", words, [], [*words1, own1])
    near, far = results(1, second)
    return pl.pallas_call(
        merge_kernel,
        out_shape=jax.ShapeDtypeStruct((wide // Z, outs), F32),
        in_specs=[VMEM] * 3,
        out_specs=VMEM,
        compiler_params=pltpu.CompilerParams(vmem_limit_bytes=VMEM_LIMIT),
        name="merge_members",
    )(in_vmem(near), in_vmem(far), in_vmem(met))


def solution(mesh):
    in_specs = (P("member", "tok", "col"), P("member", "tok", "col"), P("member", "tok", "col"))
    out_specs = P(("tok", "member"), "col")
    return jax.shard_map(shards, mesh=mesh, in_specs=in_specs, out_specs=out_specs, check_vma=False)
```

```python
import jax
import jax.numpy as jnp
from jax import lax
from jax.experimental import pallas as pl
from jax.experimental.pallas import tpu as pltpu
from jax.sharding import PartitionSpec as P

F32 = jnp.float32
BF16 = jnp.bfloat16
HBM = pl.BlockSpec(memory_space=pltpu.HBM)
VMEM = pl.BlockSpec(memory_space=pltpu.VMEM)
VMEM_LIMIT = 16 << 20

GRID = 1.00297
BIG = 2.0**28
SMALL = 2.0**16
EDGE = 2.0**-40
EDGE_CODE = 2.0**-24

X, CORES, Z = 4, 2, 4

ORDER = ((2, 1), (3, 0))


def code_of(values):
    scaled = values * BIG
    return jnp.where(values >= EDGE, scaled * scaled, values * SMALL)


def value_of(code):
    return jnp.where(code >= EDGE_CODE, jnp.sqrt(code) * (1.0 / BIG), code * (1.0 / SMALL))


def encode(values):
    return code_of(values).astype(BF16)


def decode(sent):
    return value_of(sent.astype(F32))


def encode_fine(values):
    code = code_of(values)
    first = code.astype(BF16).astype(F32)
    second = (code * (1.0 / GRID)).astype(BF16).astype(F32)
    near = jnp.abs(first - code) <= jnp.abs(second * GRID - code)
    return jnp.where(near, first, -second).astype(BF16)


def decode_fine(sent):
    code = sent.astype(F32)
    return value_of(jnp.where(code < 0.0, code * (-GRID), code))


def in_vmem(array):
    return pltpu.with_memory_space_constraint(array, pltpu.VMEM)


def in_hbm(array):
    return pltpu.with_memory_space_constraint(array, pltpu.HBM)


def call(kernel, name, outs, hbm, vmem, scratch=()):
    single = not isinstance(outs, list)
    shapes = [pltpu.VMEM(shape, kind) for shape, kind in ([outs] if single else outs)]
    result = pl.pallas_call(
        kernel,
        out_shape=shapes,
        in_specs=[HBM] * len(hbm) + [VMEM] * len(vmem),
        out_specs=[VMEM] * len(shapes),
        scratch_shapes=list(scratch),
        compiler_params=pltpu.CompilerParams(vmem_limit_bytes=VMEM_LIMIT),
        cost_estimate=pl.CostEstimate(flops=1, bytes_accessed=1, transcendentals=0),
        name=name,
    )(*[in_hbm(a) for a in hbm], *[in_vmem(a) for a in vmem])
    return result[0] if single else result


def squared_transposed(g):
    g = g.astype(F32)
    return (g * g).T.astype(BF16)


def fisher_block(x, gt_ref):
    return jnp.dot(gt_ref[...], x * x, preferred_element_type=F32)


def where_am_i():
    tok, half, member = lax.axis_index("tok"), lax.axis_index("col"), lax.axis_index("member")
    return tok // 2, tok % 2, half, member // Z, member % Z


def load_inputs(member, pair, x_ref, x_out, sem):
    x, _, half, _, _ = where_am_i()
    wide = x_ref.shape[2] // 4
    copies = []
    for s, flip in enumerate(ORDER[pair]):
        owner = x ^ flip
        local = jnp.where(owner // 2 == half, 2 * (owner % 2), 2 * ((3 - owner) % 2) + 1)
        at = pl.multiple_of(local * wide, wide)
        source = x_ref.at[member, :, pl.ds(at, wide)]
        copies.append(pltpu.make_async_copy(source, x_out.at[:, pl.ds(s * wide, wide)], sem.at[s]))
        copies[s].start()
    return copies


def load_first_kernel(x_ref, g_ref, out, sem, g_sem):
    core = where_am_i()[1]
    outs = g_ref.shape[2]
    load = pltpu.make_async_copy(g_ref.at[1 - core], out.at[:, pl.ds(out.shape[1] - outs, outs)], g_sem)
    load.start()
    for copy in load_inputs(1 - core, 0, x_ref, out, sem) + [load]:
        copy.wait()


def pair_kernel(own, got, after, out):
    outs = own.shape[1]
    out[0], out[1] = own[...], got[:, got.shape[1] - outs :]


def columns(s, x_ref, wide):
    return x_ref[:, s * wide : (s + 1) * wide]


def load_rest_kernel(
    x_ref, g_ref, after, send_out, own_a_out, own_b_out, g_out, gt_out, part_a_out, part_b_out, sem, g_sem
):
    core = where_am_i()[1]
    load = pltpu.make_async_copy(g_ref.at[core], g_out, g_sem)
    load.start()
    send = load_inputs(1 - core, 1, x_ref, send_out, sem.at[0])
    own_a = load_inputs(core, 0, x_ref, own_a_out, sem.at[1])
    own_b = load_inputs(core, 1, x_ref, own_b_out, sem.at[2])
    load.wait()
    gt_out[...] = squared_transposed(g_out[...])
    for copies, x_out, part_out in ((own_a, own_a_out, part_a_out), (own_b, own_b_out, part_b_out)):
        for s in range(2):
            copies[s].wait()
            part_out[s] = fisher_block(columns(s, x_out, part_out.shape[2]), gt_out)
    for copy in send:
        copy.wait()


def add_first_kernel(x_ref, part_ref, after, two_out, one_out, gt_out):
    wide, outs = part_ref.shape[2], part_ref.shape[1]
    gt_out[...] = squared_transposed(x_ref[:, 2 * wide :])
    for s, out in enumerate((two_out, one_out)):
        out[...] = encode(part_ref[s] + fisher_block(columns(s, x_ref, wide), gt_out))


def add_second_kernel(x_ref, gt_ref, part_ref, after, three_out, own_out):
    wide = part_ref.shape[2]
    three_out[...] = encode(part_ref[0] + fisher_block(columns(0, x_ref, wide), gt_ref))
    own_out[...] = part_ref[1] + fisher_block(columns(1, x_ref, wide), gt_ref)


def half_block(flip, part, x_refs, gt_refs, wide):
    pair = 0 if flip in ORDER[0] else 1
    at = (2 * ORDER[pair].index(flip) + part) * wide
    own, got = x_refs[2 * pair : 2 * pair + 2]
    return fisher_block(own[:, at : at + wide], gt_refs[0]) + fisher_block(got[:, at : at + wide], gt_refs[1])


def both_first_kernel(own_a, got_a, own_b, got_b, g_ref, after, sent_out, kept_out, gta_out, gtb_out):
    gta_out[...] = squared_transposed(g_ref[0])
    gtb_out[...] = squared_transposed(g_ref[1])
    for s, flip in enumerate((1, 2, 0, 3)):
        put(s, half_block(flip, 0, (own_a, got_a, own_b, got_b), (gta_out, gtb_out), sent_out.shape[2]), sent_out, kept_out)


def both_second_kernel(own_a, got_a, own_b, got_b, gta_ref, gtb_ref, after, sent_out, kept_out):
    for s, flip in enumerate((3, 2, 0, 1)):
        put(s, half_block(flip, 1, (own_a, got_a, own_b, got_b), (gta_ref, gtb_ref), sent_out.shape[2]), sent_out, kept_out)


def put(s, block, sent_out, kept_out):
    if s < 2:
        sent_out[s] = encode(block)
    else:
        kept_out[s - 2] = block


def middle_kernel(kept_ref, got_ref, after, sent_out, own_out):
    sent_out[...] = encode_fine(kept_ref[1] + decode(got_ref[1]))
    own_out[...] = kept_ref[0] + decode(got_ref[0])


def settle_kernel(own, got, after, out):
    out[...] = own[...] + decode_fine(got[...])


def join_kernel(first_ref, own, got, after, kept_out, sent_out):
    first = first_ref[...]
    second = own[...] + decode_fine(got[...])
    core = where_am_i()[1]
    kept_out[...] = jnp.where(core == 0, first, second)
    sent_out[...] = encode_fine(jnp.where(core == 0, second, first))


def join_direct_kernel(own, one, two, three, after, kept_out, sent_out):
    wide = kept_out.shape[1]
    halves = []
    for s in range(2):
        got = [decode(columns(s, ref, wide)) for ref in (one, two, three)]
        halves.append(columns(s, own, wide) + got[0] + got[1] + got[2])
    core = where_am_i()[1]
    kept_out[...] = jnp.where(core == 0, halves[0], halves[1])
    sent_out[...] = encode_fine(jnp.where(core == 0, halves[1], halves[0]))


def split_kernel(w_ref, after, own_out, send_out):
    rows, core = own_out.shape[1], where_am_i()[1]
    own_out[...] = w_ref[:, pl.ds(pl.multiple_of(core * rows, rows), rows), :]
    send_out[...] = w_ref[:, pl.ds(pl.multiple_of((1 - core) * rows, rows), rows), :]


def to_words(weighted, total, out):
    high = weighted.astype(BF16)
    out[0] = high
    out[1] = (weighted - high.astype(F32)).astype(BF16)
    out[2] = encode_fine(total)


def from_words(words):
    return words[0].astype(F32) + words[1].astype(F32), decode_fine(words[2])


def weigh_kernel(phase, own, other, w_own, w_other, after, one_out, two_out, three_out, sums_out):
    _, core, half, _, z = where_am_i()
    part = own.shape[1] // Z
    mine = (core ^ half ^ phase) == 0
    for d, out in ((2, two_out), (1, one_out), (3, three_out), (0, sums_out)):
        cols = pl.ds(pl.multiple_of((z + d) % Z * part, part), part)
        weighted = total = 0.0
        for values, m in ((own[:, cols], core), (decode_fine(other[:, cols]), 1 - core)):
            fisher = values.T
            weight = jnp.where(mine, w_own[m, cols, :].astype(F32), w_other[m, cols, :].astype(F32))
            weighted += fisher * weight
            total += fisher
        if d == 0 or phase == 0:
            out[0, :part], out[1, :part] = weighted, total
        else:
            to_words(weighted, total, out)


def over_z(sums, words):
    weighted, total = sums[0], sums[1]
    for ref in words:
        more, added = from_words(ref)
        weighted += more
        total += added
    return weighted, total


def sum_wide_kernel(one, two, three, sums, after, out):
    part = sums.shape[1]
    weighted, total = sums[0], sums[1]
    for ref in (one, two, three):
        weighted += ref[0, :part]
        total += ref[1, :part]
    to_words(weighted, total, out)


def sum_kernel(one, two, three, sums, after, out):
    to_words(*over_z(sums, (one, two, three)), out)


def meet_kernel(near, far, after, out):
    (weighted, total), (more, added) = from_words(near), from_words(far)
    out[0], out[1] = weighted + more, total + added


def merge_kernel(near, far, sums, out):
    (weighted, total), (more, added) = from_words(near), from_words(far)
    out[...] = (weighted + more + sums[0]) / (total + added + sums[1])


def keeper(local, half):
    home = 2 * half + local // 2
    return home if local % 2 == 0 else 3 - home


def kept(x, half):
    return 2 * (x % 2) if x // 2 == half else 2 * ((3 - x) % 2) + 1


def weight_pairs():
    pairs = []
    for tok in range(X * CORES):
        half, local = divmod(tok, 4)
        for col in range(2):
            pairs.append((tok * 2 + col, (keeper(local, half) * 2 + col) * 2 + half))
    return pairs


def result_pairs(phase, sender):
    pairs = []
    for z in range(Z):
        for tok in range(X * CORES):
            x, core = divmod(tok, 2)
            for half in range(2):
                to_tok = 4 * half + kept(x, half)
                to = ((core * Z + z) * 8 + to_tok) * 2 + (half ^ phase)
                pairs.append((((sender * Z + z) * 8 + tok) * 2 + half, to))
    return pairs


def x_pairs(flip):
    return [(t, ((t // 2) ^ flip) * 2 + t % 2) for t in range(X * CORES)]


def z_pairs(distance):
    return [(m, m // Z * Z + (m + distance) % Z) for m in range(2 * Z)]


def shards(inputs, grads, weights):
    tokens, outs = grads.shape[1:]
    wide = inputs.shape[2] // 8
    x_shape, g_shape, gt_shape = ((tokens, 4 * wide), BF16), ((tokens, outs), BF16), ((outs, tokens), BF16)
    part_shape, sent_shape, sum_shape = ((2, outs, 2 * wide), F32), ((outs, 2 * wide), BF16), ((outs, 2 * wide), F32)
    code_shape, own_shape = ((outs, wide), BF16), ((outs, wide), F32)
    pair_shape, kept_shape = ((2, outs, wide), BF16), ((2, outs, wide), F32)
    wide_words = ((2, wide // Z, outs), F32)
    words, sums = ((3, wide // Z, outs), BF16), ((2, wide // Z, outs), F32)
    dma = pltpu.SemaphoreType.DMA

    def swap_cores(send):
        return lax.ppermute(send, "tok", [(t, t ^ 1) for t in range(8)])

    def swap_cols(send):
        return lax.ppermute(send, "col", [(0, 1), (1, 0)])

    def swap_x(flip, sent):
        return lax.ppermute(sent, "tok", x_pairs(flip))

    def middle(flip, got, kept_blocks, after):
        sent, own = call(middle_kernel, "fisher_over_first_swap", [code_shape, own_shape], [], [kept_blocks, got, after])
        return own, swap_x(flip, sent)

    def settle(one, after):
        return call(settle_kernel, "fisher_over_tokens", own_shape, [], [*one, after])

    def join_direct(own, got, after):
        kept_block, sent = call(
            join_direct_kernel, "fisher_over_tokens", [own_shape, code_shape], [], [own, got[1], got[2], got[3], after]
        )
        return kept_block, swap_cores(sent)

    def join(first, two, after):
        kept_block, sent = call(join_kernel, "fisher_over_tokens", [own_shape, code_shape], [], [first, *two, after])
        return kept_block, swap_cores(sent)

    def results(phase, sums):
        return [lax.ppermute(sums, ("member", "tok", "col"), result_pairs(phase, y_lo)) for y_lo in range(2)]

    def bring_weights(after):
        arrived = lax.ppermute(weights, ("tok", "col"), weight_pairs())
        half_shape = ((2, weights.shape[1] // 2, outs), BF16)
        own, send = call(split_kernel, "split_weights", [half_shape, half_shape], [], [arrived, after])
        return own, swap_cores(send)

    def weigh(phase, own, other, moved, after):
        one, two, three, own_sums = call(
            lambda *refs: weigh_kernel(phase, *refs), "weigh_members", [words if phase else wide_words] * 3 + [sums], [], [own, other, *moved, after]
        )
        send = ((2, two), (1, one), (3, three))
        return [lax.ppermute(v, "member", z_pairs(d)) for d, v in send] + [own_sums]

    x_send0 = call(
        load_first_kernel, "load_to_swap", ((tokens, 4 * wide + outs), BF16), [inputs, grads], [], [dma((2,)), dma]
    )
    x_got0 = swap_cores(x_send0)
    x_send1, x_own0, x_own1, g_own, gt_own, part0, part1 = call(
        load_rest_kernel, "load_and_fisher_of_own_tokens",
        [x_shape, x_shape, x_shape, g_shape, gt_shape, part_shape, part_shape], [inputs, grads], [x_send0],
        [dma((3, 2)), dma],
    )
    x_got1 = swap_cores(x_send1)
    g_pair = call(pair_kernel, "pair_grads", ((2, tokens, outs), BF16), [], [g_own, x_got0, gt_own])
    g_other = swap_cols(g_pair)
    two, one, gt_got = call(
        add_first_kernel, "fisher_of_both_cores", [sent_shape, sent_shape, gt_shape], [], [x_got0, part0, g_pair]
    )
    got0 = {2: swap_x(2, two), 1: swap_x(1, one)}
    three, sum0 = call(
        add_second_kernel, "fisher_of_both_cores", [sent_shape, sum_shape], [], [x_got1, gt_got, part1, two]
    )
    got0[3] = swap_x(3, three)

    xs = [x_own0, x_got0, x_own1, x_got1]
    sent, kept10, gt_own, gt_got = call(
        both_first_kernel, "fisher_of_other_grads", [pair_shape, kept_shape, gt_shape, gt_shape], [], [*xs, g_other, three]
    )
    swap10 = swap_x(1, sent)
    moved = bring_weights(kept10)
    sent, kept11 = call(
        both_second_kernel, "fisher_of_other_grads", [pair_shape, kept_shape], [], [*xs, gt_own, gt_got, moved[0]]
    )
    swap11 = swap_x(3, sent)

    own0, other0 = join_direct(sum0, got0, kept11)
    words0 = weigh(0, own0, other0, moved, own0)
    part10 = middle(3, swap10, kept10, words0[3])
    part11 = middle(1, swap11, kept11, part10[0])
    first = call(sum_wide_kernel, "sum_over_z", words, [], [*words0, part11[0]])
    own1, other1 = join(settle(part10, first), part11, first)
    words1 = weigh(1, own1, other1, moved, own1)
    met = call(meet_kernel, "meet_over_y", sums, [], [*results(0, first), own1])
    second = call(sum_kernel, "sum_over_z", words, [], [*words1, own1])
    near, far = results(1, second)
    return pl.pallas_call(
        merge_kernel,
        out_shape=jax.ShapeDtypeStruct((wide // Z, outs), F32),
        in_specs=[VMEM] * 3,
        out_specs=VMEM,
        compiler_params=pltpu.CompilerParams(vmem_limit_bytes=VMEM_LIMIT),
        name="merge_members",
    )(in_vmem(near), in_vmem(far), in_vmem(met))


def solution(mesh):
    in_specs = (P("member", "tok", "col"), P("member", "tok", "col"), P("member", "tok", "col"))
    out_specs = P(("tok", "member"), "col")
    return jax.shard_map(shards, mesh=mesh, in_specs=in_specs, out_specs=out_specs, check_vma=False)
```

```python
import jax
import jax.numpy as jnp
from jax import lax
from jax.experimental import pallas as pl
from jax.experimental.pallas import tpu as pltpu
from jax.sharding import PartitionSpec as P

F32 = jnp.float32
BF16 = jnp.bfloat16
HBM = pl.BlockSpec(memory_space=pltpu.HBM)
VMEM = pl.BlockSpec(memory_space=pltpu.VMEM)
VMEM_LIMIT = 16 << 20

GRID = 1.00297
BIG = 2.0**28
SMALL = 2.0**16
EDGE = 2.0**-40
EDGE_CODE = 2.0**-24

X, CORES, Z = 4, 2, 4

ORDER = ((2, 1), (3, 0))


def code_of(values):
    scaled = values * BIG
    return jnp.where(values >= EDGE, scaled * scaled, values * SMALL)


def value_of(code):
    return jnp.where(code >= EDGE_CODE, jnp.sqrt(code) * (1.0 / BIG), code * (1.0 / SMALL))


def encode(values):
    return code_of(values).astype(BF16)


def decode(sent):
    return value_of(sent.astype(F32))


def encode_fine(values):
    code = code_of(values)
    first = code.astype(BF16).astype(F32)
    second = (code * (1.0 / GRID)).astype(BF16).astype(F32)
    near = jnp.abs(first - code) <= jnp.abs(second * GRID - code)
    return jnp.where(near, first, -second).astype(BF16)


def decode_fine(sent):
    code = sent.astype(F32)
    return value_of(jnp.where(code < 0.0, code * (-GRID), code))


def in_vmem(array):
    return pltpu.with_memory_space_constraint(array, pltpu.VMEM)


def in_hbm(array):
    return pltpu.with_memory_space_constraint(array, pltpu.HBM)


def call(kernel, name, outs, hbm, vmem, scratch=()):
    single = not isinstance(outs, list)
    shapes = [pltpu.VMEM(shape, kind) for shape, kind in ([outs] if single else outs)]
    result = pl.pallas_call(
        kernel,
        out_shape=shapes,
        in_specs=[HBM] * len(hbm) + [VMEM] * len(vmem),
        out_specs=[VMEM] * len(shapes),
        scratch_shapes=list(scratch),
        compiler_params=pltpu.CompilerParams(vmem_limit_bytes=VMEM_LIMIT),
        cost_estimate=pl.CostEstimate(flops=1, bytes_accessed=1, transcendentals=0),
        name=name,
    )(*[in_hbm(a) for a in hbm], *[in_vmem(a) for a in vmem])
    return result[0] if single else result


def squared_transposed(g):
    g = g.astype(F32)
    return (g * g).T.astype(BF16)


def fisher_block(x, gt_ref):
    return jnp.dot(gt_ref[...], x * x, preferred_element_type=F32)


def where_am_i():
    tok, half, member = lax.axis_index("tok"), lax.axis_index("col"), lax.axis_index("member")
    return tok // 2, tok % 2, half, member // Z, member % Z


def load_inputs(member, pair, x_ref, x_out, sem):
    x, _, half, _, _ = where_am_i()
    wide = x_ref.shape[2] // 4
    copies = []
    for s, flip in enumerate(ORDER[pair]):
        owner = x ^ flip
        local = jnp.where(owner // 2 == half, 2 * (owner % 2), 2 * ((3 - owner) % 2) + 1)
        at = pl.multiple_of(local * wide, wide)
        source = x_ref.at[member, :, pl.ds(at, wide)]
        copies.append(pltpu.make_async_copy(source, x_out.at[:, pl.ds(s * wide, wide)], sem.at[s]))
        copies[s].start()
    return copies


def load_first_kernel(x_ref, g_ref, out, sem, g_sem):
    core = where_am_i()[1]
    outs = g_ref.shape[2]
    load = pltpu.make_async_copy(g_ref.at[1 - core], out.at[:, pl.ds(out.shape[1] - outs, outs)], g_sem)
    load.start()
    for copy in load_inputs(1 - core, 0, x_ref, out, sem) + [load]:
        copy.wait()


def load_second_kernel(x_ref, after, x_out, sem):
    for copy in load_inputs(1 - where_am_i()[1], 1, x_ref, x_out, sem):
        copy.wait()


def pair_kernel(own, got, after, out):
    outs = own.shape[1]
    out[0], out[1] = own[...], got[:, got.shape[1] - outs :]


def columns(s, x_ref, wide):
    return x_ref[:, s * wide : (s + 1) * wide]


def own_tokens(copies, x_out, gt_ref, part_out):
    for s in range(2):
        copies[s].wait()
        part_out[s] = fisher_block(columns(s, x_out, part_out.shape[2]), gt_ref)


def own_first_kernel(x_ref, g_ref, after, x_out, g_out, gt_out, part_out, sem, g_sem):
    core = where_am_i()[1]
    load = pltpu.make_async_copy(g_ref.at[core], g_out, g_sem)
    load.start()
    copies = load_inputs(core, 0, x_ref, x_out, sem)
    load.wait()
    gt_out[...] = squared_transposed(g_out[...])
    own_tokens(copies, x_out, gt_out, part_out)


def own_second_kernel(x_ref, gt_ref, after, x_out, part_out, sem):
    copies = load_inputs(where_am_i()[1], 1, x_ref, x_out, sem)
    own_tokens(copies, x_out, gt_ref, part_out)


def add_first_kernel(x_ref, part_ref, after, two_out, one_out, gt_out):
    wide, outs = part_ref.shape[2], part_ref.shape[1]
    gt_out[...] = squared_transposed(x_ref[:, 2 * wide :])
    for s, out in enumerate((two_out, one_out)):
        out[...] = encode(part_ref[s] + fisher_block(columns(s, x_ref, wide), gt_out))


def add_second_kernel(x_ref, gt_ref, part_ref, after, three_out, own_out):
    wide = part_ref.shape[2]
    three_out[...] = encode(part_ref[0] + fisher_block(columns(0, x_ref, wide), gt_ref))
    own_out[...] = part_ref[1] + fisher_block(columns(1, x_ref, wide), gt_ref)


def half_block(flip, part, x_refs, gt_refs, wide):
    pair = 0 if flip in ORDER[0] else 1
    at = (2 * ORDER[pair].index(flip) + part) * wide
    own, got = x_refs[2 * pair : 2 * pair + 2]
    return fisher_block(own[:, at : at + wide], gt_refs[0]) + fisher_block(got[:, at : at + wide], gt_refs[1])


def both_first_kernel(own_a, got_a, own_b, got_b, g_ref, after, sent_out, kept_out, gta_out, gtb_out):
    gta_out[...] = squared_transposed(g_ref[0])
    gtb_out[...] = squared_transposed(g_ref[1])
    for s, flip in enumerate((1, 2, 0, 3)):
        put(s, half_block(flip, 0, (own_a, got_a, own_b, got_b), (gta_out, gtb_out), sent_out.shape[2]), sent_out, kept_out)


def both_second_kernel(own_a, got_a, own_b, got_b, gta_ref, gtb_ref, after, sent_out, kept_out):
    for s, flip in enumerate((3, 2, 0, 1)):
        put(s, half_block(flip, 1, (own_a, got_a, own_b, got_b), (gta_ref, gtb_ref), sent_out.shape[2]), sent_out, kept_out)


def put(s, block, sent_out, kept_out):
    if s < 2:
        sent_out[s] = encode(block)
    else:
        kept_out[s - 2] = block


def middle_kernel(kept_ref, got_ref, after, sent_out, own_out):
    sent_out[...] = encode_fine(kept_ref[1] + decode(got_ref[1]))
    own_out[...] = kept_ref[0] + decode(got_ref[0])


def settle_kernel(own, got, after, out):
    out[...] = own[...] + decode_fine(got[...])


def join_kernel(first_ref, own, got, after, kept_out, sent_out):
    first = first_ref[...]
    second = own[...] + decode_fine(got[...])
    core = where_am_i()[1]
    kept_out[...] = jnp.where(core == 0, first, second)
    sent_out[...] = encode_fine(jnp.where(core == 0, second, first))


def join_direct_kernel(own, one, two, three, after, kept_out, sent_out):
    wide = kept_out.shape[1]
    halves = []
    for s in range(2):
        got = [decode(columns(s, ref, wide)) for ref in (one, two, three)]
        halves.append(columns(s, own, wide) + got[0] + got[1] + got[2])
    core = where_am_i()[1]
    kept_out[...] = jnp.where(core == 0, halves[0], halves[1])
    sent_out[...] = encode_fine(jnp.where(core == 0, halves[1], halves[0]))


def split_kernel(w_ref, after, own_out, send_out):
    rows, core = own_out.shape[1], where_am_i()[1]
    own_out[...] = w_ref[:, pl.ds(pl.multiple_of(core * rows, rows), rows), :]
    send_out[...] = w_ref[:, pl.ds(pl.multiple_of((1 - core) * rows, rows), rows), :]


def to_words(weighted, total, out):
    high = weighted.astype(BF16)
    out[0] = high
    out[1] = (weighted - high.astype(F32)).astype(BF16)
    out[2] = encode_fine(total)


def from_words(words):
    return words[0].astype(F32) + words[1].astype(F32), decode_fine(words[2])


def weigh_kernel(phase, own, other, w_own, w_other, after, one_out, two_out, three_out, sums_out):
    _, core, half, _, z = where_am_i()
    part = own.shape[1] // Z
    mine = (core ^ half ^ phase) == 0
    for d, out in ((2, two_out), (1, one_out), (3, three_out), (0, sums_out)):
        cols = pl.ds(pl.multiple_of((z + d) % Z * part, part), part)
        weighted = total = 0.0
        for values, m in ((own[:, cols], core), (decode_fine(other[:, cols]), 1 - core)):
            fisher = values.T
            weight = jnp.where(mine, w_own[m, cols, :].astype(F32), w_other[m, cols, :].astype(F32))
            weighted += fisher * weight
            total += fisher
        if d == 0 or phase == 0:
            out[0, :part], out[1, :part] = weighted, total
        else:
            to_words(weighted, total, out)


def over_z(sums, words):
    weighted, total = sums[0], sums[1]
    for ref in words:
        more, added = from_words(ref)
        weighted += more
        total += added
    return weighted, total


def sum_wide_kernel(one, two, three, sums, after, out):
    part = sums.shape[1]
    weighted, total = sums[0], sums[1]
    for ref in (one, two, three):
        weighted += ref[0, :part]
        total += ref[1, :part]
    to_words(weighted, total, out)


def sum_kernel(one, two, three, sums, after, out):
    to_words(*over_z(sums, (one, two, three)), out)


def meet_kernel(near, far, after, out):
    (weighted, total), (more, added) = from_words(near), from_words(far)
    out[0], out[1] = weighted + more, total + added


def merge_kernel(near, far, sums, out):
    (weighted, total), (more, added) = from_words(near), from_words(far)
    out[...] = (weighted + more + sums[0]) / (total + added + sums[1])


def keeper(local, half):
    home = 2 * half + local // 2
    return home if local % 2 == 0 else 3 - home


def kept(x, half):
    return 2 * (x % 2) if x // 2 == half else 2 * ((3 - x) % 2) + 1


def weight_pairs(phase):
    pairs = []
    for tok in range(X * CORES):
        half, local = divmod(tok, 4)
        col = half ^ phase
        pairs.append((tok * 2 + col, (keeper(local, half) * 2 + col) * 2 + half))
    return pairs


def result_pairs(phase, sender):
    pairs = []
    for z in range(Z):
        for tok in range(X * CORES):
            x, core = divmod(tok, 2)
            for half in range(2):
                to_tok = 4 * half + kept(x, half)
                to = ((core * Z + z) * 8 + to_tok) * 2 + (half ^ phase)
                pairs.append((((sender * Z + z) * 8 + tok) * 2 + half, to))
    return pairs


def x_pairs(flip):
    return [(t, ((t // 2) ^ flip) * 2 + t % 2) for t in range(X * CORES)]


def z_pairs(distance):
    return [(m, m // Z * Z + (m + distance) % Z) for m in range(2 * Z)]


def shards(inputs, grads, weights):
    tokens, outs = grads.shape[1:]
    wide = inputs.shape[2] // 8
    x_shape, g_shape, gt_shape = ((tokens, 4 * wide), BF16), ((tokens, outs), BF16), ((outs, tokens), BF16)
    part_shape, sent_shape, sum_shape = ((2, outs, 2 * wide), F32), ((outs, 2 * wide), BF16), ((outs, 2 * wide), F32)
    code_shape, own_shape = ((outs, wide), BF16), ((outs, wide), F32)
    pair_shape, kept_shape = ((2, outs, wide), BF16), ((2, outs, wide), F32)
    wide_words = ((2, wide // Z, outs), F32)
    words, sums = ((3, wide // Z, outs), BF16), ((2, wide // Z, outs), F32)
    dma = pltpu.SemaphoreType.DMA

    def swap_cores(send):
        return lax.ppermute(send, "tok", [(t, t ^ 1) for t in range(8)])

    def swap_cols(send):
        return lax.ppermute(send, "col", [(0, 1), (1, 0)])

    def swap_x(flip, sent):
        return lax.ppermute(sent, "tok", x_pairs(flip))

    def middle(flip, got, kept_blocks, after):
        sent, own = call(middle_kernel, "fisher_over_first_swap", [code_shape, own_shape], [], [kept_blocks, got, after])
        return own, swap_x(flip, sent)

    def settle(one, after):
        return call(settle_kernel, "fisher_over_tokens", own_shape, [], [*one, after])

    def join_direct(own, got, after):
        kept_block, sent = call(
            join_direct_kernel, "fisher_over_tokens", [own_shape, code_shape], [], [own, got[1], got[2], got[3], after]
        )
        return kept_block, swap_cores(sent)

    def join(first, two, after):
        kept_block, sent = call(join_kernel, "fisher_over_tokens", [own_shape, code_shape], [], [first, *two, after])
        return kept_block, swap_cores(sent)

    def results(phase, sums):
        return [lax.ppermute(sums, ("member", "tok", "col"), result_pairs(phase, y_lo)) for y_lo in range(2)]

    def bring_weights(phase, after):
        arrived = lax.ppermute(weights, ("tok", "col"), weight_pairs(phase))
        half_shape = ((2, weights.shape[1] // 2, outs), BF16)
        own, send = call(split_kernel, "split_weights", [half_shape, half_shape], [], [arrived, after])
        return own, swap_cores(send)

    def weigh(phase, own, other, moved, after):
        one, two, three, own_sums = call(
            lambda *refs: weigh_kernel(phase, *refs), "weigh_members", [words if phase else wide_words] * 3 + [sums], [], [own, other, *moved, after]
        )
        send = ((2, two), (1, one), (3, three))
        return [lax.ppermute(v, "member", z_pairs(d)) for d, v in send] + [own_sums]

    x_send0 = call(
        load_first_kernel, "load_to_swap", ((tokens, 4 * wide + outs), BF16), [inputs, grads], [], [dma((2,)), dma]
    )
    x_got0 = swap_cores(x_send0)
    x_send1 = call(load_second_kernel, "load_to_swap", x_shape, [inputs], [x_send0], [dma((2,))])
    x_got1 = swap_cores(x_send1)
    x_own0, g_own, gt_own, part0 = call(
        own_first_kernel, "fisher_of_own_tokens", [x_shape, g_shape, gt_shape, part_shape], [inputs, grads], [x_send1],
        [dma((2,)), dma],
    )
    g_pair = call(pair_kernel, "pair_grads", ((2, tokens, outs), BF16), [], [g_own, x_got0, gt_own])
    g_other = swap_cols(g_pair)
    two, one, gt_got = call(
        add_first_kernel, "fisher_of_both_cores", [sent_shape, sent_shape, gt_shape], [], [x_got0, part0, g_pair]
    )
    got0 = {2: swap_x(2, two), 1: swap_x(1, one)}
    x_own1, part1 = call(
        own_second_kernel, "fisher_of_own_tokens", [x_shape, part_shape], [inputs], [gt_own, two], [dma((2,))]
    )
    three, sum0 = call(
        add_second_kernel, "fisher_of_both_cores", [sent_shape, sum_shape], [], [x_got1, gt_got, part1, x_own1]
    )
    got0[3] = swap_x(3, three)

    xs = [x_own0, x_got0, x_own1, x_got1]
    sent, kept10, gt_own, gt_got = call(
        both_first_kernel, "fisher_of_other_grads", [pair_shape, kept_shape, gt_shape, gt_shape], [], [*xs, g_other, three]
    )
    swap10 = swap_x(1, sent)
    w0 = bring_weights(0, kept10)
    sent, kept11 = call(
        both_second_kernel, "fisher_of_other_grads", [pair_shape, kept_shape], [], [*xs, gt_own, gt_got, w0[0]]
    )
    swap11 = swap_x(3, sent)

    own0, other0 = join_direct(sum0, got0, kept11)
    words0 = weigh(0, own0, other0, w0, own0)
    part10 = middle(3, swap10, kept10, words0[3])
    part11 = middle(1, swap11, kept11, part10[0])
    w1 = bring_weights(1, part11[0])
    first = call(sum_wide_kernel, "sum_over_z", words, [], [*words0, w1[0]])
    own1, other1 = join(settle(part10, first), part11, first)
    words1 = weigh(1, own1, other1, w1, own1)
    met = call(meet_kernel, "meet_over_y", sums, [], [*results(0, first), own1])
    second = call(sum_kernel, "sum_over_z", words, [], [*words1, own1])
    near, far = results(1, second)
    return pl.pallas_call(
        merge_kernel,
        out_shape=jax.ShapeDtypeStruct((wide // Z, outs), F32),
        in_specs=[VMEM] * 3,
        out_specs=VMEM,
        compiler_params=pltpu.CompilerParams(vmem_limit_bytes=VMEM_LIMIT),
        name="merge_members",
    )(in_vmem(near), in_vmem(far), in_vmem(met))


def solution(mesh):
    in_specs = (P("member", "tok", "col"), P("member", "tok", "col"), P("member", "tok", "col"))
    out_specs = P(("tok", "member"), "col")
    return jax.shard_map(shards, mesh=mesh, in_specs=in_specs, out_specs=out_specs, check_vma=False)
```

```python
import jax
import jax.numpy as jnp
from jax import lax
from jax.experimental import pallas as pl
from jax.experimental.pallas import tpu as pltpu
from jax.sharding import PartitionSpec as P

F32 = jnp.float32
BF16 = jnp.bfloat16
HBM = pl.BlockSpec(memory_space=pltpu.HBM)
VMEM = pl.BlockSpec(memory_space=pltpu.VMEM)
VMEM_LIMIT = 16 << 20

GRID = 1.00297
BIG = 2.0**28
SMALL = 2.0**16
EDGE = 2.0**-40
EDGE_CODE = 2.0**-24

X, CORES, Z = 4, 2, 4

ORDER = ((2, 1), (3, 0))


def code_of(values):
    scaled = values * BIG
    return jnp.where(values >= EDGE, scaled * scaled, values * SMALL)


def value_of(code):
    return jnp.where(code >= EDGE_CODE, jnp.sqrt(code) * (1.0 / BIG), code * (1.0 / SMALL))


def encode(values):
    return code_of(values).astype(BF16)


def decode(sent):
    return value_of(sent.astype(F32))


def encode_fine(values):
    code = code_of(values)
    first = code.astype(BF16).astype(F32)
    second = (code * (1.0 / GRID)).astype(BF16).astype(F32)
    near = jnp.abs(first - code) <= jnp.abs(second * GRID - code)
    return jnp.where(near, first, -second).astype(BF16)


def decode_fine(sent):
    code = sent.astype(F32)
    return value_of(jnp.where(code < 0.0, code * (-GRID), code))


def in_vmem(array):
    return pltpu.with_memory_space_constraint(array, pltpu.VMEM)


def in_hbm(array):
    return pltpu.with_memory_space_constraint(array, pltpu.HBM)


def call(kernel, name, outs, hbm, vmem, scratch=()):
    single = not isinstance(outs, list)
    shapes = [pltpu.VMEM(shape, kind) for shape, kind in ([outs] if single else outs)]
    result = pl.pallas_call(
        kernel,
        out_shape=shapes,
        in_specs=[HBM] * len(hbm) + [VMEM] * len(vmem),
        out_specs=[VMEM] * len(shapes),
        scratch_shapes=list(scratch),
        compiler_params=pltpu.CompilerParams(vmem_limit_bytes=VMEM_LIMIT),
        cost_estimate=pl.CostEstimate(flops=1, bytes_accessed=1, transcendentals=0),
        name=name,
    )(*[in_hbm(a) for a in hbm], *[in_vmem(a) for a in vmem])
    return result[0] if single else result


def squared_transposed(g):
    g = g.astype(F32)
    return (g * g).T.astype(BF16)


def fisher_block(x, gt_ref):
    return jnp.dot(gt_ref[...], x * x, preferred_element_type=F32)


def where_am_i():
    tok, half, member = lax.axis_index("tok"), lax.axis_index("col"), lax.axis_index("member")
    return tok // 2, tok % 2, half, member // Z, member % Z


def load_inputs(member, pair, x_ref, x_out, sem):
    x, _, half, _, _ = where_am_i()
    wide = x_ref.shape[2] // 4
    copies = []
    for s, flip in enumerate(ORDER[pair]):
        owner = x ^ flip
        local = jnp.where(owner // 2 == half, 2 * (owner % 2), 2 * ((3 - owner) % 2) + 1)
        at = pl.multiple_of(local * wide, wide)
        source = x_ref.at[member, :, pl.ds(at, wide)]
        copies.append(pltpu.make_async_copy(source, x_out.at[:, pl.ds(s * wide, wide)], sem.at[s]))
        copies[s].start()
    return copies


def load_first_kernel(x_ref, g_ref, out, sem, g_sem):
    core = where_am_i()[1]
    outs = g_ref.shape[2]
    load = pltpu.make_async_copy(g_ref.at[1 - core], out.at[:, pl.ds(out.shape[1] - outs, outs)], g_sem)
    load.start()
    for copy in load_inputs(1 - core, 0, x_ref, out, sem) + [load]:
        copy.wait()


def load_second_kernel(x_ref, after, x_out, sem):
    for copy in load_inputs(1 - where_am_i()[1], 1, x_ref, x_out, sem):
        copy.wait()


def pair_kernel(own, got, after, out):
    outs = own.shape[1]
    out[0], out[1] = own[...], got[:, got.shape[1] - outs :]


def columns(s, x_ref, wide):
    return x_ref[:, s * wide : (s + 1) * wide]


def own_tokens(copies, x_out, gt_ref, part_out):
    for s in range(2):
        copies[s].wait()
        part_out[s] = fisher_block(columns(s, x_out, part_out.shape[2]), gt_ref)


def own_first_kernel(x_ref, g_ref, after, x_out, g_out, gt_out, part_out, sem, g_sem):
    core = where_am_i()[1]
    load = pltpu.make_async_copy(g_ref.at[core], g_out, g_sem)
    load.start()
    copies = load_inputs(core, 0, x_ref, x_out, sem)
    load.wait()
    gt_out[...] = squared_transposed(g_out[...])
    own_tokens(copies, x_out, gt_out, part_out)


def own_second_kernel(x_ref, gt_ref, after, x_out, part_out, sem):
    copies = load_inputs(where_am_i()[1], 1, x_ref, x_out, sem)
    own_tokens(copies, x_out, gt_ref, part_out)


def add_first_kernel(x_ref, part_ref, after, two_out, one_out, gt_out):
    wide, outs = part_ref.shape[2], part_ref.shape[1]
    gt_out[...] = squared_transposed(x_ref[:, 2 * wide :])
    for s, out in enumerate((two_out, one_out)):
        out[...] = encode(part_ref[s] + fisher_block(columns(s, x_ref, wide), gt_out))


def add_second_kernel(x_ref, gt_ref, part_ref, after, three_out, own_out):
    wide = part_ref.shape[2]
    three_out[...] = encode(part_ref[0] + fisher_block(columns(0, x_ref, wide), gt_ref))
    own_out[...] = part_ref[1] + fisher_block(columns(1, x_ref, wide), gt_ref)


def half_block(flip, part, x_refs, gt_refs, wide):
    pair = 0 if flip in ORDER[0] else 1
    at = (2 * ORDER[pair].index(flip) + part) * wide
    own, got = x_refs[2 * pair : 2 * pair + 2]
    return fisher_block(own[:, at : at + wide], gt_refs[0]) + fisher_block(got[:, at : at + wide], gt_refs[1])


def both_first_kernel(own_a, got_a, own_b, got_b, g_ref, after, sent_out, kept_out, gta_out, gtb_out):
    gta_out[...] = squared_transposed(g_ref[0])
    gtb_out[...] = squared_transposed(g_ref[1])
    for s, flip in enumerate((1, 2, 0, 3)):
        put(s, half_block(flip, 0, (own_a, got_a, own_b, got_b), (gta_out, gtb_out), sent_out.shape[2]), sent_out, kept_out)


def both_second_kernel(own_a, got_a, own_b, got_b, gta_ref, gtb_ref, after, sent_out, kept_out):
    for s, flip in enumerate((3, 2, 0, 1)):
        put(s, half_block(flip, 1, (own_a, got_a, own_b, got_b), (gta_ref, gtb_ref), sent_out.shape[2]), sent_out, kept_out)


def put(s, block, sent_out, kept_out):
    if s < 2:
        sent_out[s] = encode(block)
    else:
        kept_out[s - 2] = block


def middle_kernel(kept_ref, got_ref, after, sent_out, own_out):
    sent_out[...] = encode_fine(kept_ref[1] + decode(got_ref[1]))
    own_out[...] = kept_ref[0] + decode(got_ref[0])


def settle_kernel(own, got, after, out):
    out[...] = own[...] + decode_fine(got[...])


def join_kernel(first_ref, own, got, after, kept_out, sent_out):
    first = first_ref[...]
    second = own[...] + decode_fine(got[...])
    core = where_am_i()[1]
    kept_out[...] = jnp.where(core == 0, first, second)
    sent_out[...] = encode_fine(jnp.where(core == 0, second, first))


def join_direct_kernel(own, one, two, three, after, kept_out, sent_out):
    wide = kept_out.shape[1]
    halves = []
    for s in range(2):
        got = [decode(columns(s, ref, wide)) for ref in (one, two, three)]
        halves.append(columns(s, own, wide) + got[0] + got[1] + got[2])
    core = where_am_i()[1]
    kept_out[...] = jnp.where(core == 0, halves[0], halves[1])
    sent_out[...] = encode_fine(jnp.where(core == 0, halves[1], halves[0]))


def split_kernel(w_ref, after, own_out, send_out):
    rows, core = own_out.shape[1], where_am_i()[1]
    own_out[...] = w_ref[:, pl.ds(pl.multiple_of(core * rows, rows), rows), :]
    send_out[...] = w_ref[:, pl.ds(pl.multiple_of((1 - core) * rows, rows), rows), :]


def to_words(weighted, total, out):
    high = weighted.astype(BF16)
    out[0] = high
    out[1] = (weighted - high.astype(F32)).astype(BF16)
    out[2] = encode_fine(total)


def from_words(words):
    return words[0].astype(F32) + words[1].astype(F32), decode_fine(words[2])


def weigh_kernel(phase, own, other, w_own, w_other, after, one_out, two_out, three_out, sums_out):
    _, core, half, _, z = where_am_i()
    part = own.shape[1] // Z
    mine = (core ^ half ^ phase) == 0
    for d, out in ((2, two_out), (1, one_out), (3, three_out), (0, sums_out)):
        cols = pl.ds(pl.multiple_of((z + d) % Z * part, part), part)
        weighted = total = 0.0
        for values, m in ((own[:, cols], core), (decode_fine(other[:, cols]), 1 - core)):
            fisher = values.T
            weight = jnp.where(mine, w_own[m, cols, :].astype(F32), w_other[m, cols, :].astype(F32))
            weighted += fisher * weight
            total += fisher
        if d == 0 or phase == 0:
            out[0, :part], out[1, :part] = weighted, total
        else:
            to_words(weighted, total, out)


def over_z(sums, words):
    weighted, total = sums[0], sums[1]
    for ref in words:
        more, added = from_words(ref)
        weighted += more
        total += added
    return weighted, total


def sum_wide_kernel(one, two, three, sums, after, out):
    part = sums.shape[1]
    weighted, total = sums[0], sums[1]
    for ref in (one, two, three):
        weighted += ref[0, :part]
        total += ref[1, :part]
    to_words(weighted, total, out)


def sum_kernel(one, two, three, sums, after, out):
    to_words(*over_z(sums, (one, two, three)), out)


def meet_kernel(near, far, after, out):
    (weighted, total), (more, added) = from_words(near), from_words(far)
    out[0], out[1] = weighted + more, total + added


def merge_kernel(near, far, sums, out):
    (weighted, total), (more, added) = from_words(near), from_words(far)
    out[...] = (weighted + more + sums[0]) / (total + added + sums[1])


def keeper(local, half):
    home = 2 * half + local // 2
    return home if local % 2 == 0 else 3 - home


def kept(x, half):
    return 2 * (x % 2) if x // 2 == half else 2 * ((3 - x) % 2) + 1


def weight_pairs():
    pairs = []
    for tok in range(X * CORES):
        half, local = divmod(tok, 4)
        for col in range(2):
            pairs.append((tok * 2 + col, (keeper(local, half) * 2 + col) * 2 + half))
    return pairs


def result_pairs(phase, sender):
    pairs = []
    for z in range(Z):
        for tok in range(X * CORES):
            x, core = divmod(tok, 2)
            for half in range(2):
                to_tok = 4 * half + kept(x, half)
                to = ((core * Z + z) * 8 + to_tok) * 2 + (half ^ phase)
                pairs.append((((sender * Z + z) * 8 + tok) * 2 + half, to))
    return pairs


def x_pairs(flip):
    return [(t, ((t // 2) ^ flip) * 2 + t % 2) for t in range(X * CORES)]


def z_pairs(distance):
    return [(m, m // Z * Z + (m + distance) % Z) for m in range(2 * Z)]


def shards(inputs, grads, weights):
    tokens, outs = grads.shape[1:]
    wide = inputs.shape[2] // 8
    x_shape, g_shape, gt_shape = ((tokens, 4 * wide), BF16), ((tokens, outs), BF16), ((outs, tokens), BF16)
    part_shape, sent_shape, sum_shape = ((2, outs, 2 * wide), F32), ((outs, 2 * wide), BF16), ((outs, 2 * wide), F32)
    code_shape, own_shape = ((outs, wide), BF16), ((outs, wide), F32)
    pair_shape, kept_shape = ((2, outs, wide), BF16), ((2, outs, wide), F32)
    wide_words = ((2, wide // Z, outs), F32)
    words, sums = ((3, wide // Z, outs), BF16), ((2, wide // Z, outs), F32)
    dma = pltpu.SemaphoreType.DMA

    def swap_cores(send):
        return lax.ppermute(send, "tok", [(t, t ^ 1) for t in range(8)])

    def swap_cols(send):
        return lax.ppermute(send, "col", [(0, 1), (1, 0)])

    def swap_x(flip, sent):
        return lax.ppermute(sent, "tok", x_pairs(flip))

    def middle(flip, got, kept_blocks, after):
        sent, own = call(middle_kernel, "fisher_over_first_swap", [code_shape, own_shape], [], [kept_blocks, got, after])
        return own, swap_x(flip, sent)

    def settle(one, after):
        return call(settle_kernel, "fisher_over_tokens", own_shape, [], [*one, after])

    def join_direct(own, got, after):
        kept_block, sent = call(
            join_direct_kernel, "fisher_over_tokens", [own_shape, code_shape], [], [own, got[1], got[2], got[3], after]
        )
        return kept_block, swap_cores(sent)

    def join(first, two, after):
        kept_block, sent = call(join_kernel, "fisher_over_tokens", [own_shape, code_shape], [], [first, *two, after])
        return kept_block, swap_cores(sent)

    def results(phase, sums):
        return [lax.ppermute(sums, ("member", "tok", "col"), result_pairs(phase, y_lo)) for y_lo in range(2)]

    def bring_weights(after):
        arrived = lax.ppermute(weights, ("tok", "col"), weight_pairs())
        half_shape = ((2, weights.shape[1] // 2, outs), BF16)
        own, send = call(split_kernel, "split_weights", [half_shape, half_shape], [], [arrived, after])
        return own, swap_cores(send)

    def weigh(phase, own, other, moved, after):
        one, two, three, own_sums = call(
            lambda *refs: weigh_kernel(phase, *refs), "weigh_members", [words if phase else wide_words] * 3 + [sums], [], [own, other, *moved, after]
        )
        send = ((1, one), (2, two), (3, three))
        return [lax.ppermute(v, "member", z_pairs(d)) for d, v in send] + [own_sums]

    x_send0 = call(
        load_first_kernel, "load_to_swap", ((tokens, 4 * wide + outs), BF16), [inputs, grads], [], [dma((2,)), dma]
    )
    x_got0 = swap_cores(x_send0)
    x_send1 = call(load_second_kernel, "load_to_swap", x_shape, [inputs], [x_send0], [dma((2,))])
    x_got1 = swap_cores(x_send1)
    x_own0, g_own, gt_own, part0 = call(
        own_first_kernel, "fisher_of_own_tokens", [x_shape, g_shape, gt_shape, part_shape], [inputs, grads], [x_send1],
        [dma((2,)), dma],
    )
    g_pair = call(pair_kernel, "pair_grads", ((2, tokens, outs), BF16), [], [g_own, x_got0, gt_own])
    g_other = swap_cols(g_pair)
    two, one, gt_got = call(
        add_first_kernel, "fisher_of_both_cores", [sent_shape, sent_shape, gt_shape], [], [x_got0, part0, g_pair]
    )
    got0 = {2: swap_x(2, two), 1: swap_x(1, one)}
    x_own1, part1 = call(
        own_second_kernel, "fisher_of_own_tokens", [x_shape, part_shape], [inputs], [gt_own, two], [dma((2,))]
    )
    three, sum0 = call(
        add_second_kernel, "fisher_of_both_cores", [sent_shape, sum_shape], [], [x_got1, gt_got, part1, x_own1]
    )
    got0[3] = swap_x(3, three)

    xs = [x_own0, x_got0, x_own1, x_got1]
    sent, kept10, gt_own, gt_got = call(
        both_first_kernel, "fisher_of_other_grads", [pair_shape, kept_shape, gt_shape, gt_shape], [], [*xs, g_other, three]
    )
    swap10 = swap_x(1, sent)
    moved = bring_weights(kept10)
    sent, kept11 = call(
        both_second_kernel, "fisher_of_other_grads", [pair_shape, kept_shape], [], [*xs, gt_own, gt_got, moved[0]]
    )
    swap11 = swap_x(3, sent)

    own0, other0 = join_direct(sum0, got0, kept11)
    words0 = weigh(0, own0, other0, moved, own0)
    part10 = middle(3, swap10, kept10, words0[3])
    part11 = middle(1, swap11, kept11, part10[0])
    first = call(sum_wide_kernel, "sum_over_z", words, [], [*words0, part11[0]])
    own1, other1 = join(settle(part10, first), part11, first)
    words1 = weigh(1, own1, other1, moved, own1)
    met = call(meet_kernel, "meet_over_y", sums, [], [*results(0, first), own1])
    second = call(sum_kernel, "sum_over_z", words, [], [*words1, own1])
    near, far = results(1, second)
    return pl.pallas_call(
        merge_kernel,
        out_shape=jax.ShapeDtypeStruct((wide // Z, outs), F32),
        in_specs=[VMEM] * 3,
        out_specs=VMEM,
        compiler_params=pltpu.CompilerParams(vmem_limit_bytes=VMEM_LIMIT),
        name="merge_members",
    )(in_vmem(near), in_vmem(far), in_vmem(met))


def solution(mesh):
    in_specs = (P("member", "tok", "col"), P("member", "tok", "col"), P("member", "tok", "col"))
    out_specs = P(("tok", "member"), "col")
    return jax.shard_map(shards, mesh=mesh, in_specs=in_specs, out_specs=out_specs, check_vma=False)
```

```python
import jax
import jax.numpy as jnp
from jax import lax
from jax.experimental import pallas as pl
from jax.experimental.pallas import tpu as pltpu
from jax.sharding import PartitionSpec as P

F32 = jnp.float32
BF16 = jnp.bfloat16
HBM = pl.BlockSpec(memory_space=pltpu.HBM)
VMEM = pl.BlockSpec(memory_space=pltpu.VMEM)
VMEM_LIMIT = 16 << 20

GRID = 1.00297
BIG = 2.0**28
SMALL = 2.0**16
EDGE = 2.0**-40
EDGE_CODE = 2.0**-24

X, CORES, Z = 4, 2, 4

ORDER = ((2, 1), (3, 0))


def code_of(values):
    scaled = values * BIG
    return jnp.where(values >= EDGE, scaled * scaled, values * SMALL)


def value_of(code):
    return jnp.where(code >= EDGE_CODE, jnp.sqrt(code) * (1.0 / BIG), code * (1.0 / SMALL))


def encode(values):
    return code_of(values).astype(BF16)


def decode(sent):
    return value_of(sent.astype(F32))


def encode_fine(values):
    code = code_of(values)
    first = code.astype(BF16).astype(F32)
    second = (code * (1.0 / GRID)).astype(BF16).astype(F32)
    near = jnp.abs(first - code) <= jnp.abs(second * GRID - code)
    return jnp.where(near, first, -second).astype(BF16)


def decode_fine(sent):
    code = sent.astype(F32)
    return value_of(jnp.where(code < 0.0, code * (-GRID), code))


def in_vmem(array):
    return pltpu.with_memory_space_constraint(array, pltpu.VMEM)


def in_hbm(array):
    return pltpu.with_memory_space_constraint(array, pltpu.HBM)


def call(kernel, name, outs, hbm, vmem, scratch=()):
    single = not isinstance(outs, list)
    shapes = [pltpu.VMEM(shape, kind) for shape, kind in ([outs] if single else outs)]
    result = pl.pallas_call(
        kernel,
        out_shape=shapes,
        in_specs=[HBM] * len(hbm) + [VMEM] * len(vmem),
        out_specs=[VMEM] * len(shapes),
        scratch_shapes=list(scratch),
        compiler_params=pltpu.CompilerParams(vmem_limit_bytes=VMEM_LIMIT),
        cost_estimate=pl.CostEstimate(flops=1, bytes_accessed=1, transcendentals=0),
        name=name,
    )(*[in_hbm(a) for a in hbm], *[in_vmem(a) for a in vmem])
    return result[0] if single else result


def squared_transposed(g):
    g = g.astype(F32)
    return (g * g).T.astype(BF16)


def fisher_block(x, gt_ref):
    return jnp.dot(gt_ref[...], x * x, preferred_element_type=F32)


def where_am_i():
    tok, half, member = lax.axis_index("tok"), lax.axis_index("col"), lax.axis_index("member")
    return tok // 2, tok % 2, half, member // Z, member % Z


def load_inputs(member, pair, x_ref, x_out, sem):
    x, _, half, _, _ = where_am_i()
    wide = x_ref.shape[2] // 4
    copies = []
    for s, flip in enumerate(ORDER[pair]):
        owner = x ^ flip
        local = jnp.where(owner // 2 == half, 2 * (owner % 2), 2 * ((3 - owner) % 2) + 1)
        at = pl.multiple_of(local * wide, wide)
        source = x_ref.at[member, :, pl.ds(at, wide)]
        copies.append(pltpu.make_async_copy(source, x_out.at[:, pl.ds(s * wide, wide)], sem.at[s]))
        copies[s].start()
    return copies


def load_first_kernel(x_ref, g_ref, out, sem, g_sem):
    core = where_am_i()[1]
    outs = g_ref.shape[2]
    load = pltpu.make_async_copy(g_ref.at[1 - core], out.at[:, pl.ds(out.shape[1] - outs, outs)], g_sem)
    load.start()
    for copy in load_inputs(1 - core, 0, x_ref, out, sem) + [load]:
        copy.wait()


def load_second_kernel(x_ref, after, x_out, sem):
    for copy in load_inputs(1 - where_am_i()[1], 1, x_ref, x_out, sem):
        copy.wait()


def pair_kernel(own, got, after, out):
    outs = own.shape[1]
    out[0], out[1] = own[...], got[:, got.shape[1] - outs :]


def columns(s, x_ref, wide):
    return x_ref[:, s * wide : (s + 1) * wide]


def own_tokens(copies, x_out, gt_ref, part_out):
    for s in range(2):
        copies[s].wait()
        part_out[s] = fisher_block(columns(s, x_out, part_out.shape[2]), gt_ref)


def own_first_kernel(x_ref, g_ref, after, x_out, g_out, gt_out, part_out, sem, g_sem):
    core = where_am_i()[1]
    load = pltpu.make_async_copy(g_ref.at[core], g_out, g_sem)
    load.start()
    copies = load_inputs(core, 0, x_ref, x_out, sem)
    load.wait()
    gt_out[...] = squared_transposed(g_out[...])
    own_tokens(copies, x_out, gt_out, part_out)


def own_second_kernel(x_ref, gt_ref, after, x_out, part_out, sem):
    copies = load_inputs(where_am_i()[1], 1, x_ref, x_out, sem)
    own_tokens(copies, x_out, gt_ref, part_out)


def add_first_kernel(x_ref, part_ref, after, two_out, one_out, gt_out):
    wide, outs = part_ref.shape[2], part_ref.shape[1]
    gt_out[...] = squared_transposed(x_ref[:, 2 * wide :])
    for s, out in enumerate((two_out, one_out)):
        out[...] = encode(part_ref[s] + fisher_block(columns(s, x_ref, wide), gt_out))


def add_second_kernel(x_ref, gt_ref, part_ref, after, three_out, own_out):
    wide = part_ref.shape[2]
    three_out[...] = encode(part_ref[0] + fisher_block(columns(0, x_ref, wide), gt_ref))
    own_out[...] = part_ref[1] + fisher_block(columns(1, x_ref, wide), gt_ref)


def half_block(flip, part, x_refs, gt_refs, wide):
    pair = 0 if flip in ORDER[0] else 1
    at = (2 * ORDER[pair].index(flip) + part) * wide
    own, got = x_refs[2 * pair : 2 * pair + 2]
    return fisher_block(own[:, at : at + wide], gt_refs[0]) + fisher_block(got[:, at : at + wide], gt_refs[1])


def both_first_kernel(own_a, got_a, own_b, got_b, g_ref, after, sent_out, kept_out, gta_out, gtb_out):
    gta_out[...] = squared_transposed(g_ref[0])
    gtb_out[...] = squared_transposed(g_ref[1])
    for s, flip in enumerate((1, 2, 0, 3)):
        put(s, half_block(flip, 0, (own_a, got_a, own_b, got_b), (gta_out, gtb_out), sent_out.shape[2]), sent_out, kept_out)


def both_second_kernel(own_a, got_a, own_b, got_b, gta_ref, gtb_ref, after, sent_out, kept_out):
    for s, flip in enumerate((3, 2, 0, 1)):
        put(s, half_block(flip, 1, (own_a, got_a, own_b, got_b), (gta_ref, gtb_ref), sent_out.shape[2]), sent_out, kept_out)


def put(s, block, sent_out, kept_out):
    if s < 2:
        sent_out[s] = encode(block)
    else:
        kept_out[s - 2] = block


def middle_kernel(kept_ref, got_ref, after, sent_out, own_out):
    sent_out[...] = encode_fine(kept_ref[1] + decode(got_ref[1]))
    own_out[...] = kept_ref[0] + decode(got_ref[0])


def settle_kernel(own, got, after, out):
    out[...] = own[...] + decode_fine(got[...])


def join_kernel(first_ref, own, got, after, kept_out, sent_out):
    first = first_ref[...]
    second = own[...] + decode_fine(got[...])
    core = where_am_i()[1]
    kept_out[...] = jnp.where(core == 0, first, second)
    sent_out[...] = encode_fine(jnp.where(core == 0, second, first))


def join_direct_kernel(own, one, two, three, after, kept_out, sent_out):
    wide = kept_out.shape[1]
    halves = []
    for s in range(2):
        got = [decode(columns(s, ref, wide)) for ref in (one, two, three)]
        halves.append(columns(s, own, wide) + got[0] + got[1] + got[2])
    core = where_am_i()[1]
    kept_out[...] = jnp.where(core == 0, halves[0], halves[1])
    sent_out[...] = encode_fine(jnp.where(core == 0, halves[1], halves[0]))


def split_kernel(w_ref, after, own_out, send_out):
    rows, core = own_out.shape[1], where_am_i()[1]
    own_out[...] = w_ref[:, pl.ds(pl.multiple_of(core * rows, rows), rows), :]
    send_out[...] = w_ref[:, pl.ds(pl.multiple_of((1 - core) * rows, rows), rows), :]


def to_words(weighted, total, out):
    high = weighted.astype(BF16)
    out[0] = high
    out[1] = (weighted - high.astype(F32)).astype(BF16)
    out[2] = encode_fine(total)


def from_words(words):
    return words[0].astype(F32) + words[1].astype(F32), decode_fine(words[2])


def weigh_kernel(phase, own, other, w_own, w_other, after, one_out, two_out, three_out, sums_out):
    _, core, half, _, z = where_am_i()
    part = own.shape[1] // Z
    mine = (core ^ half ^ phase) == 0
    for d, out in ((2, two_out), (1, one_out), (3, three_out), (0, sums_out)):
        cols = pl.ds(pl.multiple_of((z + d) % Z * part, part), part)
        weighted = total = 0.0
        for values, m in ((own[:, cols], core), (decode_fine(other[:, cols]), 1 - core)):
            fisher = values.T
            weight = jnp.where(mine, w_own[m, cols, :].astype(F32), w_other[m, cols, :].astype(F32))
            weighted += fisher * weight
            total += fisher
        if d == 0 or phase == 0:
            out[0, :part], out[1, :part] = weighted, total
        else:
            to_words(weighted, total, out)


def over_z(sums, words):
    weighted, total = sums[0], sums[1]
    for ref in words:
        more, added = from_words(ref)
        weighted += more
        total += added
    return weighted, total


def sum_wide_kernel(one, two, three, sums, after, out):
    part = sums.shape[1]
    weighted, total = sums[0], sums[1]
    for ref in (one, two, three):
        weighted += ref[0, :part]
        total += ref[1, :part]
    to_words(weighted, total, out)


def sum_kernel(one, two, three, sums, after, out):
    to_words(*over_z(sums, (one, two, three)), out)


def meet_kernel(near, far, after, out):
    (weighted, total), (more, added) = from_words(near), from_words(far)
    out[0], out[1] = weighted + more, total + added


def merge_kernel(near, far, sums, out):
    (weighted, total), (more, added) = from_words(near), from_words(far)
    out[...] = (weighted + more + sums[0]) / (total + added + sums[1])


def keeper(local, half):
    home = 2 * half + local // 2
    return home if local % 2 == 0 else 3 - home


def kept(x, half):
    return 2 * (x % 2) if x // 2 == half else 2 * ((3 - x) % 2) + 1


def weight_pairs():
    pairs = []
    for tok in range(X * CORES):
        half, local = divmod(tok, 4)
        for col in range(2):
            pairs.append((tok * 2 + col, (keeper(local, half) * 2 + col) * 2 + half))
    return pairs


def result_pairs(phase, sender):
    pairs = []
    for z in range(Z):
        for tok in range(X * CORES):
            x, core = divmod(tok, 2)
            for half in range(2):
                to_tok = 4 * half + kept(x, half)
                to = ((core * Z + z) * 8 + to_tok) * 2 + (half ^ phase)
                pairs.append((((sender * Z + z) * 8 + tok) * 2 + half, to))
    return pairs


def x_pairs(flip):
    return [(t, ((t // 2) ^ flip) * 2 + t % 2) for t in range(X * CORES)]


def z_pairs(distance):
    return [(m, m // Z * Z + (m + distance) % Z) for m in range(2 * Z)]


def shards(inputs, grads, weights):
    tokens, outs = grads.shape[1:]
    wide = inputs.shape[2] // 8
    x_shape, g_shape, gt_shape = ((tokens, 4 * wide), BF16), ((tokens, outs), BF16), ((outs, tokens), BF16)
    part_shape, sent_shape, sum_shape = ((2, outs, 2 * wide), F32), ((outs, 2 * wide), BF16), ((outs, 2 * wide), F32)
    code_shape, own_shape = ((outs, wide), BF16), ((outs, wide), F32)
    pair_shape, kept_shape = ((2, outs, wide), BF16), ((2, outs, wide), F32)
    wide_words = ((2, wide // Z, outs), F32)
    words, sums = ((3, wide // Z, outs), BF16), ((2, wide // Z, outs), F32)
    dma = pltpu.SemaphoreType.DMA

    def swap_cores(send):
        return lax.ppermute(send, "tok", [(t, t ^ 1) for t in range(8)])

    def swap_cols(send):
        return lax.ppermute(send, "col", [(0, 1), (1, 0)])

    def swap_x(flip, sent):
        return lax.ppermute(sent, "tok", x_pairs(flip))

    def middle(flip, got, kept_blocks, after):
        sent, own = call(middle_kernel, "fisher_over_first_swap", [code_shape, own_shape], [], [kept_blocks, got, after])
        return own, swap_x(flip, sent)

    def settle(one, after):
        return call(settle_kernel, "fisher_over_tokens", own_shape, [], [*one, after])

    def join_direct(own, got, after):
        kept_block, sent = call(
            join_direct_kernel, "fisher_over_tokens", [own_shape, code_shape], [], [own, got[1], got[2], got[3], after]
        )
        return kept_block, swap_cores(sent)

    def join(first, two, after):
        kept_block, sent = call(join_kernel, "fisher_over_tokens", [own_shape, code_shape], [], [first, *two, after])
        return kept_block, swap_cores(sent)

    def results(phase, sums):
        return [lax.ppermute(sums, ("member", "tok", "col"), result_pairs(phase, y_lo)) for y_lo in (1, 0)]

    def bring_weights(after):
        arrived = lax.ppermute(weights, ("tok", "col"), weight_pairs())
        half_shape = ((2, weights.shape[1] // 2, outs), BF16)
        own, send = call(split_kernel, "split_weights", [half_shape, half_shape], [], [arrived, after])
        return own, swap_cores(send)

    def weigh(phase, own, other, moved, after):
        one, two, three, own_sums = call(
            lambda *refs: weigh_kernel(phase, *refs), "weigh_members", [words if phase else wide_words] * 3 + [sums], [], [own, other, *moved, after]
        )
        send = ((1, one), (2, two), (3, three))
        return [lax.ppermute(v, "member", z_pairs(d)) for d, v in send] + [own_sums]

    x_send0 = call(
        load_first_kernel, "load_to_swap", ((tokens, 4 * wide + outs), BF16), [inputs, grads], [], [dma((2,)), dma]
    )
    x_got0 = swap_cores(x_send0)
    x_send1 = call(load_second_kernel, "load_to_swap", x_shape, [inputs], [x_send0], [dma((2,))])
    x_got1 = swap_cores(x_send1)
    x_own0, g_own, gt_own, part0 = call(
        own_first_kernel, "fisher_of_own_tokens", [x_shape, g_shape, gt_shape, part_shape], [inputs, grads], [x_send1],
        [dma((2,)), dma],
    )
    g_pair = call(pair_kernel, "pair_grads", ((2, tokens, outs), BF16), [], [g_own, x_got0, gt_own])
    g_other = swap_cols(g_pair)
    two, one, gt_got = call(
        add_first_kernel, "fisher_of_both_cores", [sent_shape, sent_shape, gt_shape], [], [x_got0, part0, g_pair]
    )
    got0 = {2: swap_x(2, two), 1: swap_x(1, one)}
    x_own1, part1 = call(
        own_second_kernel, "fisher_of_own_tokens", [x_shape, part_shape], [inputs], [gt_own, two], [dma((2,))]
    )
    three, sum0 = call(
        add_second_kernel, "fisher_of_both_cores", [sent_shape, sum_shape], [], [x_got1, gt_got, part1, x_own1]
    )
    got0[3] = swap_x(3, three)

    xs = [x_own0, x_got0, x_own1, x_got1]
    sent, kept10, gt_own, gt_got = call(
        both_first_kernel, "fisher_of_other_grads", [pair_shape, kept_shape, gt_shape, gt_shape], [], [*xs, g_other, three]
    )
    swap10 = swap_x(1, sent)
    moved = bring_weights(kept10)
    sent, kept11 = call(
        both_second_kernel, "fisher_of_other_grads", [pair_shape, kept_shape], [], [*xs, gt_own, gt_got, moved[0]]
    )
    swap11 = swap_x(3, sent)

    own0, other0 = join_direct(sum0, got0, kept11)
    words0 = weigh(0, own0, other0, moved, own0)
    part10 = middle(3, swap10, kept10, words0[3])
    part11 = middle(1, swap11, kept11, part10[0])
    first = call(sum_wide_kernel, "sum_over_z", words, [], [*words0, part11[0]])
    own1, other1 = join(settle(part10, first), part11, first)
    words1 = weigh(1, own1, other1, moved, own1)
    met = call(meet_kernel, "meet_over_y", sums, [], [*results(0, first), own1])
    second = call(sum_kernel, "sum_over_z", words, [], [*words1, own1])
    near, far = results(1, second)
    return pl.pallas_call(
        merge_kernel,
        out_shape=jax.ShapeDtypeStruct((wide // Z, outs), F32),
        in_specs=[VMEM] * 3,
        out_specs=VMEM,
        compiler_params=pltpu.CompilerParams(vmem_limit_bytes=VMEM_LIMIT),
        name="merge_members",
    )(in_vmem(near), in_vmem(far), in_vmem(met))


def solution(mesh):
    in_specs = (P("member", "tok", "col"), P("member", "tok", "col"), P("member", "tok", "col"))
    out_specs = P(("tok", "member"), "col")
    return jax.shard_map(shards, mesh=mesh, in_specs=in_specs, out_specs=out_specs, check_vma=False)
```
